32 devices in a mesh: dp: 4 (over x, core), head: 4 (over z), tensor: 2 (over y).
Axes of the slice: x: 2, y: 2, z: 4, core: 2. Of those that a mesh axis runs over, the one named last changes fastest.
Arguments:
- residual: bfloat16 [16384, 1536], P(('dp', 'head', 'tensor')), may hold values from -6 to 6
- segment_ids: int32 [4, 4096], P('dp'), may hold values from 0 to 5, never falling along the last dimension, each value on 1 to 2000 neighbouring positions
- norm_in_gain: float32 [1536], replicated, may hold values from 0.5 to 1.5
- w_zx: bfloat16 [1536, 2, 3072], P('dp', None, ('head', 'tensor')), may hold values from -0.15625 to 0.15625
- w_bc: bfloat16 [1536, 256], P('dp'), may hold values from -0.15625 to 0.15625
- w_dt: bfloat16 [1536, 48], P('dp', ('head', 'tensor')), may hold values from -0.15625 to 0.15625
- conv_x_weight: float32 [4, 3072], P(None, ('head', 'tensor')), may hold values from -3 to 3
- conv_x_bias: float32 [3072], P(('head', 'tensor')), may hold values from -3 to 3
- conv_bc_weight: float32 [4, 256], replicated, may hold values from -3 to 3
- conv_bc_bias: float32 [256], replicated, may hold values from -3 to 3
- dt_bias: float32 [48], P(('head', 'tensor')), may hold values from -6 to -2
- a_log: float32 [48], P(('head', 'tensor')), may hold values from 0 to 2.7
- d_skip: float32 [48], P(('head', 'tensor')), may hold values from 0.5 to 1.5
- norm_gain: float32 [3072], P(('head', 'tensor')), may hold values from 0.5 to 1.5
- w_out: bfloat16 [1536, 3072], P('dp', ('head', 'tensor')), may hold values from -0.109375 to 0.109375
- cotangent: bfloat16 [16384, 1536], P(('dp', 'head', 'tensor')), may hold values from -6 to 6
Outputs:
- block_out: bfloat16 [16384, 1536], P(('dp', 'head', 'tensor'))
- residual_grad: float32 [16384, 1536], P(('dp', 'head', 'tensor'))
- norm_in_gain_grad: float32 [1536], replicated
- w_zx_grad: float32 [1536, 2, 3072], P('dp', None, ('head', 'tensor'))
- w_bc_grad: float32 [1536, 256], P('dp')
- w_dt_grad: float32 [1536, 48], P('dp', ('head', 'tensor'))
- conv_x_weight_grad: float32 [4, 3072], P(None, ('head', 'tensor'))
- conv_x_bias_grad: float32 [3072], P(('head', 'tensor'))
- conv_bc_weight_grad: float32 [4, 256], replicated
- conv_bc_bias_grad: float32 [256], replicated
- dt_bias_grad: float32 [48], P(('head', 'tensor'))
- a_log_grad: float32 [48], P(('head', 'tensor'))
- d_skip_grad: float32 [48], P(('head', 'tensor'))
- norm_gain_grad: float32 [3072], P(('head', 'tensor'))
- w_out_grad: float32 [1536, 3072], P('dp', ('head', 'tensor'))
The draws below stay inside these ranges and needn't reach their ends.
Inputs may be any that keep to these rules, and one draw needn't show every extreme that they name: `segment_ids`: along each sequence the numbers never fall; a document holds at most 2000 tokens.
All inputs are finite; a program needn't handle non-finite values.
Results may differ from the reference program's by a relative error of at most 0.0078.
Values may be sent and summed in bfloat16 or wider, within the bound.
A program may use at most 256 MiB of HBM per device.

```python
import math
import jax
import jax.numpy as jnp
import numpy as np
from jax import lax

D = 1536
HEADS = 48
STATE = 128
CONV = 4
BLOCK = 256
LEN = 4096
DOC_MOST = 2000
DOCS = 6
INNER = 3072
NSEQ = 4
TOKENS = 16384


def shard_levels(own_key, dims, pieces, least, largest):
    gain = 1.0
    for dim, parts in pieces:
        heights = jax.random.uniform(jax.random.fold_in(jax.random.fold_in(own_key, 6), dim), (parts,), jnp.float32, least / len(pieces), largest / len(pieces))
        gain = gain * jnp.repeat(jnp.exp(heights), dims[dim] // parts).reshape((-1,) + (1,) * (len(dims) - 1 - dim))
    return gain


def length_profile(amount, total, bound, skew):
    portions = [(1 << 20) // math.isqrt(standing ** skew) + 1 for standing in range(2, amount + 1)]
    rest, counts = total - bound - (amount - 1), [1] * (amount - 1)
    while rest > 0:
        movable = [i for i in range(amount - 1) if counts[i] < bound]
        pool, left = sum([portions[i] for i in movable]), rest
        for i in movable:
            addition = min(bound - counts[i], max(1, left * portions[i] // pool), rest)
            counts[i] = counts[i] + addition
            rest = rest - addition
    return np.array([bound] + counts)


def ragged(key, count, total, bound, skew):
    if count == 2:
        one = jax.random.randint(key, (), max(1, total - bound), min(bound, total - 1) + 1)
        return jnp.stack([one, total - one])
    lengths = jnp.asarray(length_profile(count, total, bound, skew), jnp.int32)
    pairs = (count - 1) // 2
    donor, receiver = lengths[1:1 + 2 * pairs:2], lengths[2:2 + 2 * pairs:2]
    slack = jnp.minimum(donor - 1, bound - receiver)
    moved = jax.random.randint(jax.random.fold_in(key, 1), (pairs,), 0, 1 << 20) % (slack + 1)
    lengths = lengths.at[1:1 + 2 * pairs:2].set(donor - moved).at[2:2 + 2 * pairs:2].set(receiver + moved)
    return lengths[jax.random.permutation(jax.random.fold_in(key, 2), count)]


def bell_draw(stream_key, shape, width, most, cuts=(), kind=jnp.bfloat16):
    loudness = shard_levels(stream_key, shape, cuts, -0.22, 0.18) if cuts else 1.0
    result = jax.random.normal(stream_key, shape, jnp.float32) * width * loudness
    return jnp.minimum(jnp.maximum(result, -most), most).astype(kind)


def setup_inputs(seed: int = 0) -> dict:
    seeds = jax.random.split(jax.random.key(seed), 17)
    residual = bell_draw(seeds[0], (TOKENS, D), 1.0, 6.0, ((0, 32),))
    segment_ids = jax.vmap(lambda own: jnp.searchsorted(jnp.cumsum(ragged(own, DOCS, LEN, DOC_MOST, 2)), jnp.arange(LEN), side="right"))(jax.random.split(seeds[1], NSEQ)).reshape((NSEQ, LEN)).astype(jnp.int32)
    norm_in_gain = jnp.clip(jax.random.uniform(seeds[2], (D,), jnp.float32, 0.5, 1.5), 0.5, 1.5)
    w_zx = bell_draw(seeds[3], (D, 2, INNER), D ** -0.5, 0.15625, ((0, 4), (2, 8)))
    w_bc = bell_draw(seeds[4], (D, 2 * STATE), D ** -0.5, 0.15625, ((0, 4),))
    w_dt = bell_draw(seeds[5], (D, HEADS), D ** -0.5, 0.15625, ((0, 4), (1, 8)))
    conv_x_weight = bell_draw(seeds[6], (CONV, INNER), CONV ** -0.5, 3.0, ((1, 8),), jnp.float32)
    conv_x_bias = bell_draw(seeds[7], (INNER,), 0.5, 3.0, ((0, 8),), jnp.float32)
    conv_bc_weight = bell_draw(seeds[8], (CONV, 2 * STATE), CONV ** -0.5, 3.0, (), jnp.float32)
    conv_bc_bias = bell_draw(seeds[9], (2 * STATE,), 0.5, 3.0, (), jnp.float32)
    dt_bias = jnp.clip(-6.0 + 4.0 * jax.random.uniform(seeds[10], (HEADS,), jnp.float32) ** shard_levels(seeds[10], (HEADS,), ((0, 8),), -0.2, 0.2), -6.0, -2.0)
    a_log = jnp.clip(2.7 * jax.random.uniform(seeds[11], (HEADS,), jnp.float32) ** shard_levels(seeds[11], (HEADS,), ((0, 8),), -0.2, 0.2), 0.0, 2.7)
    d_skip = jnp.clip(0.5 + 1.0 * jax.random.uniform(seeds[12], (HEADS,), jnp.float32) ** shard_levels(seeds[12], (HEADS,), ((0, 8),), -0.2, 0.2), 0.5, 1.5)
    norm_gain = jnp.clip(0.5 + 1.0 * jax.random.uniform(seeds[13], (INNER,), jnp.float32) ** shard_levels(seeds[13], (INNER,), ((0, 8),), -0.2, 0.2), 0.5, 1.5)
    w_out = bell_draw(seeds[14], (D, INNER), INNER ** -0.5, 0.109375, ((0, 4), (1, 8)))
    cotangent = bell_draw(seeds[15], (TOKENS, D), 1.0, 6.0, ((0, 32),))
    return {"residual": residual, "segment_ids": segment_ids, "norm_in_gain": norm_in_gain, "w_zx": w_zx, "w_bc": w_bc, "w_dt": w_dt, "conv_x_weight": conv_x_weight, "conv_x_bias": conv_x_bias, "conv_bc_weight": conv_bc_weight, "conv_bc_bias": conv_bc_bias, "dt_bias": dt_bias, "a_log": a_log, "d_skip": d_skip, "norm_gain": norm_gain, "w_out": w_out, "cotangent": cotangent}


EPSILON = 1e-05
HIGHEST = lax.Precision.HIGHEST

@jax.custom_vjp
def low(v):
    return lax.optimization_barrier(v.astype(jnp.bfloat16)).astype(jnp.float32)

@jax.custom_vjp
def low_back(v):
    return v

def low_keep(v):
    return (low(v), None)

def low_pass(kept, grad):
    return (grad,)

def back_keep(v):
    return (v, None)

def back_low(kept, grad):
    return (low(grad),)
low.defvjp(low_keep, low_pass)
low_back.defvjp(back_keep, back_low)

def causal_conv(values, taps, offset_bias, segments):
    tap_count = taps.shape[0]
    summed = offset_bias + taps[tap_count - 1] * values
    for offset in range(1, tap_count):
        earlier = jnp.pad(values, ((0, 0), (offset, 0), (0, 0)))[:, :-offset]
        earlier_seg = jnp.pad(segments, ((0, 0), (offset, 0)), constant_values=-1)[:, :-offset]
        same_doc = (earlier_seg == segments).astype(jnp.float32)[..., None]
        summed = summed + taps[tap_count - 1 - offset] * earlier * same_doc
    return jax.nn.silu(summed)

def scan_blocks(x_heads, steps_dt, decay_rate, b_proj, c_proj, segments):
    seq_count, length, head_count, head_width = x_heads.shape
    state_size = b_proj.shape[-1]
    block_count = length // BLOCK

    def to_blocks(values):
        return jnp.moveaxis(values.reshape((seq_count, block_count, BLOCK) + values.shape[2:]), 1, 0)
    seg_blocks = to_blocks(segments)
    prev_end = jnp.concatenate([jnp.full((1, seq_count), -1, jnp.int32), seg_blocks[:-1, :, -1]], 0)
    lower_part = jnp.tril(jnp.ones((BLOCK, BLOCK), jnp.bool_))

    @jax.checkpoint
    def block_step(carried, inputs):
        x_block, dt_block, b_block, c_block, seg_block, end_before = inputs
        cumulative = jnp.cumsum(dt_block * decay_rate, axis=1)
        same_doc = ((seg_block[:, :, None] == seg_block[:, None, :]) & lower_part)[..., None]
        coupling = jnp.einsum('nls,nms->nlm', c_block, b_block, precision=HIGHEST)
        spread = cumulative[:, :, None, :] - cumulative[:, None, :, :]
        kernel = jnp.where(same_doc, jnp.exp(jnp.where(same_doc, spread, 0.0)), 0.0) * coupling[..., None] * dt_block[:, None, :, :]
        within = jnp.einsum('nlmh,nmhp->nlhp', kernel, x_block, precision=HIGHEST)
        carry_in = (seg_block == end_before[:, None]).astype(jnp.float32)[..., None] * jnp.exp(cumulative)
        from_state = jnp.einsum('nls,nhps->nlhp', c_block, carried, precision=HIGHEST) * carry_in[..., None]
        end_seg = seg_block[:, -1]
        tail_weight = jnp.exp(cumulative[:, -1:, :] - cumulative) * dt_block * (seg_block == end_seg[:, None]).astype(jnp.float32)[..., None]
        added_state = jnp.einsum('nmh,nmhp,nms->nhps', tail_weight, x_block, b_block, precision=HIGHEST)
        keep_all = (end_before == end_seg).astype(jnp.float32)[:, None] * jnp.exp(cumulative[:, -1, :])
        carried = carried * keep_all[:, :, None, None] + added_state
        return (carried, within + from_state)
    initial = jnp.zeros((seq_count, head_count, head_width, state_size), jnp.float32)
    _, outputs = lax.scan(block_step, initial, (to_blocks(x_heads), to_blocks(steps_dt), to_blocks(b_proj), to_blocks(c_proj), seg_blocks, prev_end))
    return jnp.moveaxis(outputs, 0, 1).reshape(seq_count, length, head_count, head_width)

def mixer(z_and_x, b_and_c, dt_raw, segments, conv_weight, conv_bias, bc_weight, bc_bias, dt_shift, log_decay, skip_gain):
    seq_count, length = segments.shape
    head_count = dt_shift.shape[0]
    inner_width = z_and_x.shape[-1]
    head_width = inner_width // head_count
    state_size = b_and_c.shape[-1] // 2
    x_conv = causal_conv(z_and_x[:, :, 1], conv_weight, conv_bias, segments)
    bc_conv = causal_conv(b_and_c, bc_weight, bc_bias, segments)
    steps_dt = jax.nn.softplus(dt_raw + dt_shift)
    decay_rate = -jnp.exp(log_decay)
    x_heads = x_conv.reshape(seq_count, length, head_count, head_width)
    scanned = scan_blocks(x_heads, steps_dt, decay_rate, bc_conv[..., :state_size], bc_conv[..., state_size:], segments)
    scanned = scanned + skip_gain[:, None] * x_heads
    return scanned.reshape(seq_count, length, inner_width) * jax.nn.silu(z_and_x[:, :, 0])

def block_forward(rows_in, segments, params):
    in_gain, weight_zx, weight_bc, weight_dt, conv_weight, conv_bias, bc_weight, bc_bias, dt_shift, log_decay, skip_gain, gain_out, weight_out = params
    inv_rms = lax.rsqrt(lax.optimization_barrier(jnp.mean(rows_in * rows_in, axis=1, keepdims=True)) + EPSILON)
    normed = low(rows_in * inv_rms * in_gain)
    z_and_x = low_back(jnp.einsum('td,dki->tki', normed, weight_zx, precision=HIGHEST))
    b_and_c = low_back(jnp.dot(normed, weight_bc, precision=HIGHEST))
    dt_raw = low_back(jnp.dot(normed, weight_dt, precision=HIGHEST))
    gated = mixer(z_and_x[None], b_and_c[None], dt_raw[None], segments[None], conv_weight, conv_bias, bc_weight, bc_bias, dt_shift, log_decay, skip_gain)[0]
    inv_gate = lax.rsqrt(lax.optimization_barrier(jnp.mean(gated * gated, axis=1, keepdims=True)) + EPSILON)
    gated_out = low(gated * inv_gate * gain_out)
    return rows_in + jnp.dot(gated_out, weight_out.T, precision=HIGHEST)

def reference(residual, segment_ids, norm_in_gain, w_zx, w_bc, w_dt, conv_x_weight, conv_x_bias, conv_bc_weight, conv_bc_bias, dt_bias, a_log, d_skip, norm_gain, w_out, cotangent):
    params = (norm_in_gain, w_zx.astype(jnp.float32), w_bc.astype(jnp.float32), w_dt.astype(jnp.float32), conv_x_weight, conv_x_bias, conv_bc_weight, conv_bc_bias, dt_bias, a_log, d_skip, norm_gain, w_out.astype(jnp.float32))
    seq_total, length = segment_ids.shape
    model_width = residual.shape[1]
    rows_all = residual.astype(jnp.float32).reshape(seq_total, length, model_width)
    cot_all = cotangent.astype(jnp.float32).reshape(seq_total, length, model_width)

    def per_sequence(grad_sums, inputs):
        rows_seq, seg_seq, cot_seq = inputs

        def forward_only(rows_arg, param_arg):
            return block_forward(rows_arg, seg_seq, param_arg)
        out_seq, back_fn = jax.vjp(forward_only, rows_seq, params)
        rows_grad, param_grads = back_fn(cot_seq)
        grad_sums = jax.tree.map(lambda left, right: left + right, grad_sums, param_grads)
        return (grad_sums, (out_seq, rows_grad))
    zero_grads = jax.tree.map(jnp.zeros_like, params)
    grad_sums, (outs_all, rows_grads) = lax.scan(per_sequence, zero_grads, (rows_all, segment_ids, cot_all))
    block_out = outs_all.reshape(seq_total * length, model_width).astype(jnp.bfloat16)
    residual_grad = rows_grads.reshape(seq_total * length, model_width)
    return (block_out, residual_grad, grad_sums[0], grad_sums[1], grad_sums[2], grad_sums[3], grad_sums[4], grad_sums[5], grad_sums[6], grad_sums[7], grad_sums[8], grad_sums[9], grad_sums[10], grad_sums[11], grad_sums[12])
```

```python
import jax
import jax.numpy as jnp
from jax import lax
from jax.sharding import PartitionSpec as P

EPSILON = 1e-05
DOC_MOST = 2000
CHUNK = 128
HALO = 16
MASKED = -1e30
HIGHEST = lax.Precision.HIGHEST
SEQ = ("head", "tensor")
ALL = ("dp", "head", "tensor")
BF16 = jnp.bfloat16
F32 = jnp.float32


def dot16(pattern, left, right):
    return jnp.einsum(pattern, left.astype(BF16), right.astype(BF16), preferred_element_type=F32)


def rounded(v):
    return lax.optimization_barrier(v.astype(BF16))


def silu_grad(v):
    gate = jax.nn.sigmoid(v)
    return gate * (1.0 + v * (1.0 - gate))


def conv_before(ext, taps, bias, same):
    own = ext.shape[0] - HALO
    total = bias + taps[-1] * ext[HALO:]
    for back in range(1, taps.shape[0]):
        total = total + taps[-1 - back] * ext[HALO - back : HALO - back + own] * same[back - 1]
    return total


def conv_back(grad, ext, taps, same):
    own = grad.shape[0]
    width = taps.shape[0]
    below = jnp.zeros((HALO, grad.shape[1]), F32)
    total = jnp.concatenate([below, taps[-1] * grad], 0)
    rows = [jnp.sum(grad * ext[HALO:], axis=0)]
    for back in range(1, width):
        masked = grad * same[back - 1]
        rows.append(jnp.sum(masked * ext[HALO - back : HALO - back + own], axis=0))
        total = total + jnp.pad(
            taps[-1 - back] * masked, ((HALO - back, back), (0, 0))
        )
    return total, jnp.stack(rows[::-1], 0), jnp.sum(grad, axis=0)


def from_earlier(values, distance, size):
    return lax.ppermute(values, SEQ, [(i, i + distance) for i in range(size - distance)])


def from_later(values, distance, size):
    return lax.ppermute(values, SEQ, [(i + distance, i) for i in range(size - distance)])


def reach_over(shift, local, keep, size, need):
    total = shift(local.astype(BF16), 1, size).astype(F32)
    factor = shift(keep, 1, size)
    covered = 1
    while covered < min(need, size - 1):
        got = shift(total.astype(BF16), covered, size).astype(F32)
        total = total + factor[:, None, None] * got
        if covered * 2 < min(need, size - 1):
            factor = factor * shift(factor, covered, size)
        covered *= 2
    return total


def body(
    residual,
    segment_ids,
    norm_in_gain,
    w_zx,
    w_bc,
    w_dt,
    conv_x_weight,
    conv_x_bias,
    conv_bc_weight,
    conv_bc_bias,
    dt_bias,
    a_log,
    d_skip,
    norm_gain,
    w_out,
    cotangent,
):
    own, width = residual.shape
    dp_size = lax.axis_size("dp")
    size = lax.axis_size(SEQ)
    place = lax.axis_index(SEQ)
    dp_rows, _, cols = w_zx.shape
    heads_own = w_dt.shape[1]
    inner = cols * size
    heads = heads_own * size
    state2 = w_bc.shape[1]
    state = state2 // 2
    bc_cols = state2 // size
    chunks = own // CHUNK
    head_width = inner // heads

    bc_own = lax.dynamic_slice_in_dim(w_bc, place * bc_cols, bc_cols, 1)
    side = heads_own + bc_cols
    pack = jnp.concatenate([w_zx.reshape(dp_rows, 2 * cols), w_out, bc_own, w_dt], 1)
    full = lax.all_gather(pack, ALL, axis=0, tiled=False).reshape(dp_size, size, dp_rows, -1)
    full = jnp.moveaxis(full, 1, 2).reshape(width, size, -1)
    w_z = full[:, :, :cols].reshape(width, inner)
    w_x = full[:, :, cols : 2 * cols].reshape(width, inner)
    w_o = full[:, :, 2 * cols : 3 * cols].reshape(width, inner)
    w_b = full[:, :, 3 * cols : 3 * cols + bc_cols].reshape(width, state2)
    w_d = full[:, :, 3 * cols + bc_cols :].reshape(width, heads)
    per_head = jnp.concatenate(
        [dt_bias[None], a_log[None], d_skip[None]], 0
    )
    per_channel = jnp.concatenate([conv_x_weight, conv_x_bias[None], norm_gain[None]], 0)
    per_head = lax.all_gather(per_head, SEQ, axis=1, tiled=True)
    per_channel = lax.all_gather(per_channel, SEQ, axis=1, tiled=True)
    taps = conv_x_weight.shape[0]
    x_taps, x_bias, out_gain = per_channel[:taps], per_channel[taps], per_channel[taps + 1]
    dt_shift, log_rate, skip = per_head[0], per_head[1], per_head[2]
    rate = -jnp.exp(log_rate)
    skip_wide = jnp.repeat(skip, head_width)

    seg_all = jnp.pad(segment_ids[0], (HALO, 0), constant_values=-1)
    seg_ext = lax.dynamic_slice_in_dim(seg_all, place * own, own + HALO)
    seg = seg_ext[HALO:]
    same = [
        (seg_ext[HALO - back : HALO - back + own] == seg).astype(F32)[:, None]
        for back in range(1, taps)
    ]
    seg_chunk = seg.reshape(chunks, CHUNK)
    end_chunk = seg_chunk[:, -1]
    end_before = jnp.concatenate([seg_ext[HALO - 1 : HALO], end_chunk[:-1]])
    lower = jnp.tril(jnp.ones((CHUNK, CHUNK), F32))
    mask_bias = jnp.where(
        (seg_chunk[:, :, None] == seg_chunk[:, None, :]) & (lower > 0), 0.0, MASKED
    )

    rows_ext = jnp.concatenate([from_earlier(residual[-HALO:], 1, size), residual], 0).astype(F32)
    inv_ext = lax.rsqrt(jnp.mean(rows_ext * rows_ext, axis=1, keepdims=True) + EPSILON)
    normed = (rows_ext * inv_ext * norm_in_gain).astype(BF16)
    rows_in, inv_rms = rows_ext[HALO:], inv_ext[HALO:]
    x_ext = dot16("td,dk->tk", normed, w_x)
    z = dot16("td,dk->tk", normed[HALO:], w_z)
    bc_ext = dot16("td,dk->tk", normed, w_b)
    dt_raw = dot16("td,dk->tk", normed[HALO:], w_d)

    x_pre = conv_before(x_ext, x_taps, x_bias, same)
    bc_pre = conv_before(bc_ext, conv_bc_weight, conv_bc_bias, same)
    x = jax.nn.silu(x_pre)
    bc = jax.nn.silu(bc_pre).astype(BF16)
    dt = jax.nn.softplus(dt_raw + dt_shift)

    cum = jnp.einsum(
        "lm,cmh->clh", lower, (dt * rate).reshape(chunks, CHUNK, heads), precision=HIGHEST
    )
    b_chunk = bc[:, :state].reshape(chunks, CHUNK, state)
    c_chunk = bc[:, state:].reshape(chunks, CHUNK, state)

    def split(v):
        return v.reshape(chunks, CHUNK, heads, head_width)

    x4 = split(x)
    dt_chunk = dt.reshape(chunks, CHUNK, heads)
    xd = x4 * dt_chunk[..., None]
    xd16 = rounded(xd)
    coupling = dot16("cls,cms->clm", c_chunk, b_chunk)
    cum_t = jnp.moveaxis(cum, 2, 1)
    decay = jnp.exp(cum_t[:, :, :, None] - cum_t[:, :, None, :] + mask_bias[:, None])
    kernel = rounded(decay * coupling[:, None])
    y_within = dot16("chlm,cmhp->clhp", kernel, xd16)
    in_end = (seg_chunk == end_chunk[:, None]).astype(F32)[..., None]
    in_start = (seg_chunk == end_before[:, None]).astype(F32)[..., None]
    tail = jnp.exp(cum[:, -1:] - cum) * in_end
    entry = jnp.exp(cum) * in_start
    keep = jnp.exp(cum[:, -1]) * (end_before == end_chunk).astype(F32)[:, None]
    xt16 = rounded(xd * tail[..., None])
    added = dot16("cmhp,cms->chps", xt16, b_chunk)

    local, keep_local = added[0], keep[0]
    for c in range(1, chunks):
        local = added[c] + keep[c][:, None, None] * local
        keep_local = keep_local * keep[c]
    need = -(-(DOC_MOST - 1) // own)
    entering = [reach_over(from_earlier, local, keep_local, size, need)]
    for c in range(chunks - 1):
        entering.append(added[c] + keep[c][:, None, None] * entering[c])
    entering = jnp.stack(entering, 0)
    entering16 = entering.astype(BF16)
    y_entry = dot16("cls,chps->clhp", c_chunk, entering16)
    y = (y_within + y_entry * entry[..., None]).reshape(own, inner) + skip_wide * x

    z_gate = jax.nn.silu(z)
    gated = y * z_gate
    inv_gate = lax.rsqrt(jnp.mean(gated * gated, axis=1, keepdims=True) + EPSILON)
    gated_out = (gated * inv_gate * out_gain).astype(BF16)
    block_out = (rows_in + dot16("ti,di->td", gated_out, w_o)).astype(BF16)
    grad_gate = dot16("td,di->ti", cotangent, w_o)
    grad_wout = dot16("td,ti->di", cotangent, gated_out)
    grad_norm_gain = jnp.sum(grad_gate * gated * inv_gate, axis=0)
    scaled_gate = grad_gate * out_gain
    cross = jnp.sum(scaled_gate * gated, axis=1, keepdims=True)
    grad_gated = inv_gate * scaled_gate - gated * (inv_gate * inv_gate * inv_gate) * (cross / inner)

    dy = grad_gated * z_gate
    dz = grad_gated * y * silu_grad(z)
    grad_skip = jnp.sum((dy * x).reshape(own, heads, head_width), axis=(0, 2))

    dy4 = split(dy)
    dy16 = rounded(dy4)
    dye16 = rounded(dy4 * entry[..., None])
    back_added = dot16("clhp,cls->chps", dye16, c_chunk)
    back_local = back_added[-1]
    for c in range(chunks - 2, -1, -1):
        back_local = back_added[c] + keep[c][:, None, None] * back_local
    leaving = [reach_over(from_later, back_local, keep_local, size, need)]
    for c in range(chunks - 1, 0, -1):
        leaving.append(back_added[c] + keep[c][:, None, None] * leaving[-1])
    leaving = jnp.stack(leaving[::-1], 0)
    leaving16 = leaving.astype(BF16)
    dxd_within = dot16("chlm,clhp->cmhp", kernel, dy16)
    dxt = dot16("cms,chps->cmhp", b_chunk, leaving16)
    dxd = dxd_within + tail[..., None] * dxt
    dx = (dxd * dt_chunk[..., None]).reshape(own, inner) + skip_wide * dy
    dkernel = dot16("clhp,cmhp->chlm", dy16, xd16)
    dcoupling = jnp.sum(dkernel * decay, axis=1)
    dc = dot16("clm,cms->cls", dcoupling, b_chunk) + dot16("clhp,chps->cls", dye16, entering16)
    db = dot16("clm,cls->cms", dcoupling, c_chunk) + dot16("cmhp,chps->cms", xt16, leaving16)
    falls = jnp.sum(
        dy16.astype(F32) * y_within
        + dye16.astype(F32) * y_entry
        - xd16.astype(F32) * dxd_within,
        axis=3,
    )
    rises = jnp.sum(xt16.astype(F32) * dxt, axis=3)
    strict = lower - jnp.eye(CHUNK, dtype=F32)
    da = (
        jnp.einsum("lm,clh->cmh", lower, falls, precision=HIGHEST)
        + jnp.einsum("lm,cmh->clh", strict, rises, precision=HIGHEST)
        + (keep * jnp.sum(leaving * entering, axis=(2, 3)))[:, None]
    )
    ddt = jnp.sum(x4 * dxd, axis=3) + rate * da
    grad_log = rate * jnp.sum(dt_chunk * da, axis=(0, 1))
    ddt_raw = ddt.reshape(own, heads) * jax.nn.sigmoid(dt_raw + dt_shift)
    grad_shift = jnp.sum(ddt_raw, axis=0)

    gx, grad_taps, grad_bias = conv_back(dx * silu_grad(x_pre), x_ext, x_taps, same)
    dbc = jnp.concatenate([db, dc], 2).reshape(own, state2)
    gbc, grad_bc_taps, grad_bc_bias = conv_back(
        dbc * silu_grad(bc_pre), bc_ext, conv_bc_weight, same
    )
    low_x = gx.astype(BF16)
    low_bc = gbc.astype(BF16)
    above = jnp.zeros((HALO, 1), BF16)
    low_z = dz.astype(BF16)
    low_dt = ddt_raw.astype(BF16)
    normed_own = normed[HALO:]

    own_part = dot16("tk,dk->td", low_z, w_z) + dot16("tk,dk->td", low_dt, w_d)
    ext_part = dot16("tk,dk->td", low_x, w_x) + dot16("tk,dk->td", low_bc, w_b)
    last = from_later(ext_part[:HALO], 1, size)
    grad_normed = own_part + ext_part[HALO:]
    grad_normed = grad_normed.at[own - HALO :].add(last)
    scaled_in = grad_normed * norm_in_gain
    input_grad = (
        cotangent.astype(F32)
        + inv_rms * scaled_in
        - rows_in * (inv_rms * inv_rms * inv_rms) * jnp.mean(scaled_in * rows_in, axis=1, keepdims=True)
    )
    grad_in_gain = jnp.sum(grad_normed * rows_in * inv_rms, axis=0)

    grad_z = dot16("td,tk->dk", normed_own, low_z)
    grad_d = dot16("td,tk->dk", normed_own, low_dt)
    grad_x = dot16("td,tk->dk", normed, low_x)
    grad_b = dot16("td,tk->dk", normed, low_bc)

    def columns(v):
        return v.astype(BF16).reshape(width, size, -1)

    parts = jnp.concatenate([columns(v) for v in (grad_z, grad_x, grad_wout, grad_b, grad_d)], 2)
    parts = jnp.moveaxis(parts.reshape(dp_size, dp_rows, size, -1), 2, 1)
    mine = lax.psum_scatter(
        parts.reshape(dp_size * size * dp_rows, -1), ALL, scatter_dimension=0, tiled=True
    ).astype(F32)
    grad_wzx = mine[:, : 2 * cols].reshape(dp_rows, 2, cols)
    grad_wo = mine[:, 2 * cols : 3 * cols]
    grad_wbc = lax.all_gather(mine[:, 3 * cols : 3 * cols + bc_cols], SEQ, axis=1, tiled=True)
    grad_wdt = mine[:, 3 * cols + bc_cols :]

    channel_sum = jnp.concatenate([grad_taps, grad_bias[None], grad_norm_gain[None]], 0)
    head_sum = jnp.stack([grad_shift, grad_log, grad_skip], 0)
    gain_sum, taps_sum, bias_sum, channel_sum, head_sum = lax.psum(
        (grad_in_gain, grad_bc_taps, grad_bc_bias, channel_sum, head_sum), ALL
    )
    channel_own = lax.dynamic_slice_in_dim(channel_sum, place * cols, cols, 1)
    head_own = lax.dynamic_slice_in_dim(head_sum, place * heads_own, heads_own, 1)
    return (
        block_out,
        input_grad,
        gain_sum,
        grad_wzx,
        grad_wbc,
        grad_wdt,
        channel_own[:taps],
        channel_own[taps],
        taps_sum,
        bias_sum,
        head_own[0],
        head_own[1],
        head_own[2],
        channel_own[taps + 1],
        grad_wo,
    )


def solution(mesh):
    rows = P(ALL, None)
    in_specs = (
        rows,
        P("dp", None),
        P(),
        P("dp", None, SEQ),
        P("dp", None),
        P("dp", SEQ),
        P(None, SEQ),
        P(SEQ),
        P(),
        P(),
        P(SEQ),
        P(SEQ),
        P(SEQ),
        P(SEQ),
        P("dp", SEQ),
        rows,
    )
    out_specs = (
        rows,
        rows,
        P(),
        P("dp", None, SEQ),
        P("dp", None),
        P("dp", SEQ),
        P(None, SEQ),
        P(SEQ),
        P(),
        P(),
        P(SEQ),
        P(SEQ),
        P(SEQ),
        P(SEQ),
        P("dp", SEQ),
    )
    return jax.shard_map(
        body, mesh=mesh, in_specs=in_specs, out_specs=out_specs, check_vma=False
    )
```

```python
import functools

import jax
import jax.numpy as jnp
from jax import lax
from jax.experimental import pallas as pl
from jax.experimental.pallas import tpu as pltpu
from jax.sharding import PartitionSpec as P

EPSILON = 1e-05
DOC_MOST = 2000
CHUNK = 128
HALO = 16
MASKED = -1e30
HIGHEST = lax.Precision.HIGHEST
SEQ = ("head", "tensor")
ALL = ("dp", "head", "tensor")
BF16 = jnp.bfloat16
F32 = jnp.float32
MESH = pl.DeviceIdType.MESH
VMEM_BYTES = 56 << 20


def dot16(pattern, left, right):
    return jnp.einsum(pattern, left.astype(BF16), right.astype(BF16), preferred_element_type=F32)


def rounded(v):
    return lax.optimization_barrier(v.astype(BF16))


def silu_grad(v):
    gate = jax.nn.sigmoid(v)
    return gate * (1.0 + v * (1.0 - gate))


def coordinates():
    dp = lax.axis_index("dp")
    return lax.div(dp, 2), lax.rem(dp, 2), lax.axis_index("head"), lax.axis_index("tensor")


def enter_kernel(x, core, head, tensor, xs, hs, ts, sibling):
    barrier = pltpu.get_barrier_semaphore()
    count = 0
    for step in range(1, hs):
        pl.semaphore_signal(barrier, 1, device_id={"head": lax.rem(head + step, hs)}, device_id_type=MESH)
        count += 1
    for step in range(1, ts):
        pl.semaphore_signal(barrier, 1, device_id={"tensor": lax.rem(tensor + step, ts)}, device_id_type=MESH)
        count += 1
    for step in range(1, xs):
        other = 2 * lax.rem(x + step, xs) + core
        pl.semaphore_signal(barrier, 1, device_id={"dp": other}, device_id_type=MESH)
        count += 1
    if sibling:
        pl.semaphore_signal(barrier, 1, device_id={"dp": 2 * x + 1 - core}, device_id_type=MESH)
        count += 1
    pl.semaphore_wait(barrier, count)


def gather_kernel(sizes, chunks, kinds, *refs):
    xs, hs, ts = sizes
    parts, small = refs[:kinds], refs[kinds]
    fulls, small_full = refs[kinds + 1 : 2 * kinds + 1], refs[2 * kinds + 1]
    send, recv, small_send, small_recv, own_sem = refs[2 * kinds + 2 :]
    x, core, head, tensor = coordinates()
    dp = 2 * x + core
    for kind in range(kinds):
        pltpu.make_async_copy(
            parts[kind], fulls[kind].at[dp, head, tensor], own_sem.at[kind]
        ).start()
    pltpu.make_async_copy(small, small_full.at[head, tensor], own_sem.at[kinds]).start()
    enter_kernel(x, core, head, tensor, xs, hs, ts, True)

    def copy(src, dst, index, slot, device):
        return pltpu.make_async_remote_copy(
            src_ref=src,
            dst_ref=dst,
            send_sem=send.at[index, slot],
            recv_sem=recv.at[index, slot],
            device_id=device,
            device_id_type=MESH,
        )

    def along_head(index):
        kind, start, length, _ = chunks[index]
        rows = pl.ds(start, length)
        return [
            copy(
                parts[kind].at[rows],
                fulls[kind].at[dp, head, tensor, rows],
                index,
                step - 1,
                {"head": lax.rem(head + step, hs)},
            )
            for step in range(1, hs)
        ]

    def over(index, axis, second):
        kind, start, length, _ = chunks[index]
        rows = pl.ds(start, length)
        base = hs - 1 if second else hs - 1 + max(xs, ts)
        copies = []
        if axis == "tensor":
            homes = [dp] if second else [2 * home + core for home in range(xs)]
            for step in range(1, ts):
                for home in homes:
                    view = fulls[kind].at[home, :, tensor, rows]
                    device = {"tensor": lax.rem(tensor + step, ts)}
                    copies.append(copy(view, view, index, base + len(copies), device))
        else:
            for step in range(1, xs):
                view = fulls[kind].at[dp, :, tensor, rows] if second else fulls[kind].at[dp, :, :, rows]
                device = {"dp": 2 * lax.rem(x + step, xs) + core}
                copies.append(copy(view, view, index, base + len(copies), device))
        return copies

    def to_sibling(index):
        kind, start, length, _ = chunks[index]
        rows = pl.ds(start, length)
        base = hs - 1 + max(xs, ts) + max(xs, xs * ts)
        return [
            copy(
                fulls[kind].at[2 * home + core, :, :, rows],
                fulls[kind].at[2 * home + core, :, :, rows],
                index,
                base + home,
                {"dp": 2 * x + 1 - core},
            )
            for home in range(xs)
        ]

    def stage(index, number):
        tensor_first = chunks[index][3]
        if number == 0:
            return along_head(index)
        if number == 1:
            return over(index, "tensor" if tensor_first else "x", True)
        if number == 2:
            return over(index, "x" if tensor_first else "tensor", False)
        return to_sibling(index)

    small_tensor = [
        pltpu.make_async_remote_copy(
            src_ref=small,
            dst_ref=small_full.at[head, tensor],
            send_sem=small_send.at[step - 1],
            recv_sem=small_recv.at[step - 1],
            device_id={"tensor": lax.rem(tensor + step, ts)},
            device_id_type=MESH,
        )
        for step in range(1, ts)
    ]
    small_head = [
        pltpu.make_async_remote_copy(
            src_ref=small_full.at[head],
            dst_ref=small_full.at[head],
            send_sem=small_send.at[ts + step - 2],
            recv_sem=small_recv.at[ts + step - 2],
            device_id={"head": lax.rem(head + step, hs)},
            device_id_type=MESH,
        )
        for step in range(1, hs)
    ]
    total = len(chunks)
    ahead = 4
    for one in small_tensor:
        one.start()
    for index in range(min(ahead, total)):
        for one in stage(index, 0):
            one.start()
    for kind in range(kinds):
        pltpu.make_async_copy(
            parts[kind], fulls[kind].at[dp, head, tensor], own_sem.at[kind]
        ).wait()
    pltpu.make_async_copy(small, small_full.at[head, tensor], own_sem.at[kinds]).wait()
    for one in small_tensor:
        one.wait_recv()
    for one in small_head:
        one.start()
    for tick in range(total + 6):
        for number in range(4):
            index = tick - 2 * number
            if 0 <= index < total:
                for one in stage(index, number):
                    one.wait_recv()
                if number < 3:
                    for one in stage(index, number + 1):
                        one.start()
                if number == 0 and index + ahead < total:
                    for one in stage(index + ahead, 0):
                        one.start()
    for one in small_head:
        one.wait_recv()
    for one in small_tensor + small_head:
        one.wait_send()
    for index in range(total):
        for number in range(4):
            for one in stage(index, number):
                one.wait_send()


def row_chunks(rows, kinds, pieces):
    step = rows // pieces
    return [
        (kind, piece * step, step, piece % 2 == 0) for kind in range(kinds) for piece in range(pieces)
    ]


def gather_weights(parts, small, sizes):
    xs, hs, ts = sizes
    kinds = len(parts)
    chunks = row_chunks(parts[0].shape[0], kinds, 4)
    slots = hs - 1 + max(xs, ts) + max(xs, xs * ts) + xs
    full = [jax.ShapeDtypeStruct((2 * xs, hs, ts) + part.shape, part.dtype) for part in parts]
    full.append(jax.ShapeDtypeStruct((hs, ts) + small.shape, small.dtype))
    anywhere = pl.BlockSpec(memory_space=pl.ANY)
    return pl.pallas_call(
        functools.partial(gather_kernel, sizes, chunks, kinds),
        out_shape=full,
        in_specs=[anywhere] * (kinds + 1),
        out_specs=[anywhere] * (kinds + 1),
        scratch_shapes=[
            pltpu.SemaphoreType.DMA((len(chunks), slots)),
            pltpu.SemaphoreType.DMA((len(chunks), slots)),
            pltpu.SemaphoreType.DMA((hs + ts,)),
            pltpu.SemaphoreType.DMA((hs + ts,)),
            pltpu.SemaphoreType.DMA((kinds + 1,)),
        ],
        compiler_params=pltpu.CompilerParams(
            collective_id=0, has_side_effects=True, vmem_limit_bytes=VMEM_BYTES
        ),
    )(*parts, small)


def scatter_kernel(sizes, chunks, kinds, *refs):
    xs, hs, ts = sizes
    parts, small = refs[:kinds], refs[kinds]
    outs, small_out = refs[kinds + 1 : 2 * kinds + 1], refs[2 * kinds + 1]
    rest = refs[2 * kinds + 2 :]
    bufs, rest = rest[: 4 * len(chunks)], rest[4 * len(chunks) :]
    small_acc, small_in, send, recv, small_send, small_recv, own_sem = rest
    x, core, head, tensor = coordinates()
    dp = 2 * x + core
    total = len(chunks)

    def loads(index):
        kind, start, length, x_first = chunks[index]
        rows = pl.ds(start, length)
        held = bufs[4 * index]
        view = parts[kind].at[x, :, :, rows] if x_first else parts[kind].at[:, :, tensor, rows]
        return pltpu.make_async_copy(view, held, own_sem.at[index])

    def copy(src, dst, index, slot, device):
        return pltpu.make_async_remote_copy(
            src_ref=src,
            dst_ref=dst,
            send_sem=send.at[index, slot],
            recv_sem=recv.at[index, slot],
            device_id=device,
            device_id_type=MESH,
        )

    def stage(index, number):
        kind, start, length, x_first = chunks[index]
        rows = pl.ds(start, length)
        held, first, second, third = bufs[4 * index : 4 * index + 4]
        most = max(xs, ts) - 1
        if number == 0 and x_first:
            return [
                copy(
                    parts[kind].at[lax.rem(x + step, xs), :, :, rows],
                    first.at[step - 1],
                    index,
                    step - 1,
                    {"dp": 2 * lax.rem(x + step, xs) + core},
                )
                for step in range(1, xs)
            ]
        if number == 0:
            return [
                copy(
                    parts[kind].at[:, :, lax.rem(tensor + step, ts), rows],
                    first.at[step - 1],
                    index,
                    step - 1,
                    {"tensor": lax.rem(tensor + step, ts)},
                )
                for step in range(1, ts)
            ]
        if number == 1 and x_first:
            return [
                copy(
                    held.at[:, lax.rem(tensor + step, ts)],
                    second.at[step - 1],
                    index,
                    most + step - 1,
                    {"tensor": lax.rem(tensor + step, ts)},
                )
                for step in range(1, ts)
            ]
        if number == 1:
            return [
                copy(
                    held.at[lax.rem(x + step, xs)],
                    second.at[step - 1],
                    index,
                    most + step - 1,
                    {"dp": 2 * lax.rem(x + step, xs) + core},
                )
                for step in range(1, xs)
            ]
        copies = []
        for step in range(1, hs):
            other = lax.rem(head + step, hs)
            view = held.at[other, tensor] if x_first else held.at[x, other]
            copies.append(
                copy(view, third.at[step - 1], index, 2 * most + step - 1, {"head": other})
            )
        return copies

    def add(index, number):
        kind, start, length, x_first = chunks[index]
        held, first, second, third = bufs[4 * index : 4 * index + 4]
        if number == 0:

            @pl.loop(0, held.shape[0])
            def _(one):
                for two in range(held.shape[1]):
                    value = held[one, two].astype(F32)
                    for step in range(first.shape[0]):
                        value = value + first[step, one, two].astype(F32)
                    held[one, two] = value.astype(BF16)

        elif number == 1:

            @pl.loop(0, hs)
            def _(one):
                where = (one, tensor) if x_first else (x, one)
                value = held[where].astype(F32)
                for step in range(second.shape[0]):
                    value = value + second[step, one].astype(F32)
                held[where] = value.astype(BF16)

        else:
            where = (head, tensor) if x_first else (x, head)
            value = held[where].astype(F32)
            for step in range(third.shape[0]):
                value = value + third[step].astype(F32)
            outs[kind][start : start + length, :] = value

    small_slots = [1, xs - 1, ts - 1, hs - 1]
    small_base = [0, 1, xs, xs + ts - 1]

    def small_stage(number):
        copies = []
        for step in range(1, small_slots[number] + 1):
            slot = small_base[number] + step - 1
            device = (
                {"dp": 2 * x + 1 - core},
                {"dp": 2 * lax.rem(x + step, xs) + core},
                {"tensor": lax.rem(tensor + step, ts)},
                {"head": lax.rem(head + step, hs)},
            )[number]
            copies.append(
                pltpu.make_async_remote_copy(
                    src_ref=small if number == 0 else small_acc.at[number - 1],
                    dst_ref=small_in.at[slot],
                    send_sem=small_send.at[slot],
                    recv_sem=small_recv.at[slot],
                    device_id=device,
                    device_id_type=MESH,
                )
            )
        return copies

    def small_add(number):
        mine = small[...] if number == 0 else small_acc[number - 1]
        size = small_slots[number] + 1
        place = (core, x, tensor, head)[number]
        value = None
        for at in range(size):
            step = lax.rem(place - at + size, size)
            slot = small_base[number] + jnp.maximum(step - 1, 0)
            here = jnp.where(step == 0, mine, small_in[slot])
            value = here if value is None else value + here
        if number < 3:
            small_acc[number] = value
        else:
            small_out[...] = value

    for index in range(total):
        loads(index).start()
    enter_kernel(x, core, head, tensor, xs, hs, ts, True)
    ahead = 4
    for one in small_stage(0):
        one.start()
    for index in range(min(ahead, total)):
        for one in stage(index, 0):
            one.start()
    for tick in range(total + 4):
        for number in range(3):
            index = tick - 2 * number
            if 0 <= index < total:
                for one in stage(index, number):
                    one.wait_recv()
                if number == 0:
                    loads(index).wait()
                    if index + ahead < total:
                        for one in stage(index + ahead, 0):
                            one.start()
                add(index, number)
                if number < 2:
                    for one in stage(index, number + 1):
                        one.start()
        if tick < 4:
            for one in small_stage(tick):
                one.wait_recv()
            small_add(tick)
            if tick < 3:
                for one in small_stage(tick + 1):
                    one.start()
    for number in range(4):
        for one in small_stage(number):
            one.wait_send()
    for index in range(total):
        for number in range(3):
            for one in stage(index, number):
                one.wait_send()


def scatter_gradients(parts, small, sizes):
    xs, hs, ts = sizes
    kinds = len(parts)
    chunks = row_chunks(parts[0].shape[3], kinds, 4)
    scratch = []
    for kind, _, length, x_first in chunks:
        cols = parts[kind].shape[4]
        held = (hs, ts) if x_first else (xs, hs)
        near, far = (xs, ts) if x_first else (ts, xs)
        scratch += [
            pltpu.VMEM(held + (length, cols), BF16),
            pltpu.VMEM((near - 1,) + held + (length, cols), BF16),
            pltpu.VMEM((far - 1, hs, length, cols), BF16),
            pltpu.VMEM((hs - 1, length, cols), BF16),
        ]
    slots = 2 * (max(xs, ts) - 1) + hs - 1
    small_slots = xs + ts + hs - 2
    anywhere = pl.BlockSpec(memory_space=pl.ANY)
    whole = pl.BlockSpec(memory_space=pltpu.VMEM)
    return pl.pallas_call(
        functools.partial(scatter_kernel, sizes, chunks, kinds),
        out_shape=[jax.ShapeDtypeStruct(part.shape[3:], F32) for part in parts]
        + [jax.ShapeDtypeStruct(small.shape, F32)],
        in_specs=[anywhere] * kinds + [whole],
        out_specs=[whole] * (kinds + 1),
        scratch_shapes=scratch
        + [
            pltpu.VMEM((3,) + small.shape, F32),
            pltpu.VMEM((small_slots,) + small.shape, F32),
            pltpu.SemaphoreType.DMA((len(chunks), slots)),
            pltpu.SemaphoreType.DMA((len(chunks), slots)),
            pltpu.SemaphoreType.DMA((small_slots,)),
            pltpu.SemaphoreType.DMA((small_slots,)),
            pltpu.SemaphoreType.DMA((len(chunks),)),
        ],
        compiler_params=pltpu.CompilerParams(
            collective_id=1, has_side_effects=True, vmem_limit_bytes=VMEM_BYTES
        ),
    )(*parts, small)


def group_of(cols):
    return 1 if cols % 128 == 0 else 128 // cols if 128 % cols == 0 else 2


def local_params():
    return pltpu.CompilerParams(vmem_limit_bytes=VMEM_BYTES)


def onto_columns(rows, pieces):
    dps, hts, depth, cols = pieces.shape
    group = group_of(cols)
    count = rows.shape[0]

    def kernel(rows_ref, piece_ref, out_ref):
        for one in range(group):
            weights = piece_ref[:, one].reshape(dps * depth, cols)
            out_ref[:, one * cols : (one + 1) * cols] = jnp.dot(
                rows_ref[...], weights, preferred_element_type=F32
            )

    return pl.pallas_call(
        kernel,
        grid=(hts // group,),
        out_shape=jax.ShapeDtypeStruct((count, hts * cols), F32),
        in_specs=[
            pl.BlockSpec(rows.shape, lambda j: (0, 0)),
            pl.BlockSpec((dps, group, depth, cols), lambda j: (0, j, 0, 0)),
        ],
        out_specs=pl.BlockSpec((count, group * cols), lambda j: (0, j)),
        compiler_params=local_params(),
        cost_estimate=pl.CostEstimate(
            flops=2 * count * pieces.size, bytes_accessed=2 * pieces.size, transcendentals=0
        ),
    )(rows, pieces)


def back_from_columns(values, pieces):
    dps, hts, depth, cols = pieces.shape
    group = group_of(cols)
    count = values.shape[0]

    def kernel(value_ref, piece_ref, out_ref):
        @pl.when(pl.program_id(0) == 0)
        def _():
            out_ref[...] = jnp.zeros_like(out_ref)

        for one in range(group):
            weights = piece_ref[:, one].reshape(dps * depth, cols)
            out_ref[...] += lax.dot_general(
                value_ref[:, one * cols : (one + 1) * cols],
                weights,
                (((1,), (1,)), ((), ())),
                preferred_element_type=F32,
            )

    return pl.pallas_call(
        kernel,
        grid=(hts // group,),
        out_shape=jax.ShapeDtypeStruct((count, dps * depth), F32),
        in_specs=[
            pl.BlockSpec((count, group * cols), lambda j: (0, j)),
            pl.BlockSpec((dps, group, depth, cols), lambda j: (0, j, 0, 0)),
        ],
        out_specs=pl.BlockSpec((count, dps * depth), lambda j: (0, 0)),
        compiler_params=local_params(),
        cost_estimate=pl.CostEstimate(
            flops=2 * count * pieces.size, bytes_accessed=2 * pieces.size, transcendentals=0
        ),
    )(values, pieces)


def gradient_pieces(left, values, hts):
    xs, depth, count = left.shape
    cols = values.shape[1] // hts
    group = group_of(cols)

    def kernel(left_ref, value_ref, out_ref):
        for at in range(xs):
            for one in range(group):
                out_ref[at, one] = jnp.dot(
                    left_ref[at], value_ref[:, one * cols : (one + 1) * cols], preferred_element_type=F32
                ).astype(BF16)

    return pl.pallas_call(
        kernel,
        grid=(hts // group,),
        out_shape=jax.ShapeDtypeStruct((xs, hts, depth, cols), BF16),
        in_specs=[
            pl.BlockSpec(left.shape, lambda j: (0, 0, 0)),
            pl.BlockSpec((count, group * cols), lambda j: (0, j)),
        ],
        out_specs=pl.BlockSpec((xs, group, depth, cols), lambda j: (0, j, 0, 0)),
        compiler_params=local_params(),
        cost_estimate=pl.CostEstimate(
            flops=2 * left.size * values.shape[1], bytes_accessed=2 * values.size, transcendentals=0
        ),
    )(left, values)


def conv_before(ext, taps, bias, same):
    own = ext.shape[0] - HALO
    total = bias + taps[-1] * ext[HALO:]
    for back in range(1, taps.shape[0]):
        total = total + taps[-1 - back] * ext[HALO - back : HALO - back + own] * same[back - 1]
    return total


def conv_back(grad, ext, taps, same):
    own = grad.shape[0]
    width = taps.shape[0]
    below = jnp.zeros((HALO, grad.shape[1]), F32)
    total = jnp.concatenate([below, taps[-1] * grad], 0)
    rows = [jnp.sum(grad * ext[HALO:], axis=0)]
    for back in range(1, width):
        masked = grad * same[back - 1]
        rows.append(jnp.sum(masked * ext[HALO - back : HALO - back + own], axis=0))
        total = total + jnp.pad(
            taps[-1 - back] * masked, ((HALO - back, back), (0, 0))
        )
    return total, jnp.stack(rows[::-1], 0), jnp.sum(grad, axis=0)


def from_earlier(values, distance, size):
    return lax.ppermute(values, SEQ, [(i, i + distance) for i in range(size - distance)])


def from_later(values, distance, size):
    return lax.ppermute(values, SEQ, [(i + distance, i) for i in range(size - distance)])


def reach_over(shift, local, keep, size, need):
    total = shift(local.astype(BF16), 1, size).astype(F32)
    factor = shift(keep, 1, size)
    covered = 1
    while covered < min(need, size - 1):
        got = shift(total.astype(BF16), covered, size).astype(F32)
        total = total + factor[:, None, None] * got
        if covered * 2 < min(need, size - 1):
            factor = factor * shift(factor, covered, size)
        covered *= 2
    return total


def body(
    residual,
    segment_ids,
    norm_in_gain,
    w_zx,
    w_bc,
    w_dt,
    conv_x_weight,
    conv_x_bias,
    conv_bc_weight,
    conv_bc_bias,
    dt_bias,
    a_log,
    d_skip,
    norm_gain,
    w_out,
    cotangent,
):
    own, width = residual.shape
    dp_size = lax.axis_size("dp")
    size = lax.axis_size(SEQ)
    place = lax.axis_index(SEQ)
    dp_rows, _, cols = w_zx.shape
    heads_own = w_dt.shape[1]
    inner = cols * size
    heads = heads_own * size
    state2 = w_bc.shape[1]
    state = state2 // 2
    bc_cols = state2 // size
    chunks = own // CHUNK
    head_width = inner // heads

    sizes = (dp_size // 2, lax.axis_size("head"), lax.axis_size("tensor"))
    core = lax.rem(lax.axis_index("dp"), 2)
    bc_own = lax.dynamic_slice_in_dim(w_bc, place * bc_cols, bc_cols, 1)
    side = bc_cols + heads_own
    side_part = jnp.pad(jnp.concatenate([bc_own, w_dt], 1), ((0, 0), (0, 128 - side)))
    taps = conv_x_weight.shape[0]
    small_rows = [conv_x_weight, conv_x_bias[None], norm_gain[None]]
    head_rows = jnp.stack([dt_bias, a_log, d_skip])
    small = jnp.concatenate(small_rows + [jnp.pad(head_rows, ((0, 0), (0, cols - heads_own)))], 0)
    small = jnp.pad(small, ((0, 16 - small.shape[0]), (0, 0)))
    gathered = gather_weights([side_part, w_zx[:, 1], w_zx[:, 0], w_out], small, sizes)
    side_full, w_x, w_z, w_o, small_full = gathered

    def pieces(v):
        return v.reshape(dp_size, size, dp_rows, v.shape[-1])

    side_full, w_x, w_z, w_o = pieces(side_full), pieces(w_x), pieces(w_z), pieces(w_o)
    side_cols = jnp.moveaxis(side_full[..., :side], 1, 2).reshape(width, size, side)
    w_b = side_cols[:, :, :bc_cols].reshape(width, state2)
    w_d = side_cols[:, :, bc_cols:].reshape(width, heads)
    small_full = jnp.moveaxis(small_full.reshape(size, 16, cols), 0, 1)
    per_channel = small_full.reshape(16, inner)
    x_taps, x_bias, out_gain = per_channel[:taps], per_channel[taps], per_channel[taps + 1]
    per_head = small_full[taps + 2 : taps + 5, :, :heads_own].reshape(3, heads)
    dt_shift, log_rate, skip = per_head[0], per_head[1], per_head[2]
    rate = -jnp.exp(log_rate)
    skip_wide = jnp.repeat(skip, head_width)

    seg_all = jnp.pad(segment_ids[0], (HALO, 0), constant_values=-1)
    seg_ext = lax.dynamic_slice_in_dim(seg_all, place * own, own + HALO)
    seg = seg_ext[HALO:]
    same = [
        (seg_ext[HALO - back : HALO - back + own] == seg).astype(F32)[:, None]
        for back in range(1, taps)
    ]
    seg_chunk = seg.reshape(chunks, CHUNK)
    end_chunk = seg_chunk[:, -1]
    end_before = jnp.concatenate([seg_ext[HALO - 1 : HALO], end_chunk[:-1]])
    lower = jnp.tril(jnp.ones((CHUNK, CHUNK), F32))
    mask_bias = jnp.where(
        (seg_chunk[:, :, None] == seg_chunk[:, None, :]) & (lower > 0), 0.0, MASKED
    )

    rows_ext = jnp.concatenate([from_earlier(residual[-HALO:], 1, size), residual], 0).astype(F32)
    inv_ext = lax.rsqrt(jnp.mean(rows_ext * rows_ext, axis=1, keepdims=True) + EPSILON)
    normed = (rows_ext * inv_ext * norm_in_gain).astype(BF16)
    rows_in, inv_rms = rows_ext[HALO:], inv_ext[HALO:]
    x_ext = onto_columns(normed, w_x)
    z = onto_columns(normed[HALO:], w_z)
    bc_ext = dot16("td,dk->tk", normed, w_b)
    dt_raw = dot16("td,dk->tk", normed[HALO:], w_d)

    x_pre = conv_before(x_ext, x_taps, x_bias, same)
    bc_pre = conv_before(bc_ext, conv_bc_weight, conv_bc_bias, same)
    x = jax.nn.silu(x_pre)
    bc = jax.nn.silu(bc_pre).astype(BF16)
    dt = jax.nn.softplus(dt_raw + dt_shift)

    cum = jnp.einsum(
        "lm,cmh->clh", lower, (dt * rate).reshape(chunks, CHUNK, heads), precision=HIGHEST
    )
    b_chunk = bc[:, :state].reshape(chunks, CHUNK, state)
    c_chunk = bc[:, state:].reshape(chunks, CHUNK, state)

    def split(v):
        return v.reshape(chunks, CHUNK, heads, head_width)

    x4 = split(x)
    dt_chunk = dt.reshape(chunks, CHUNK, heads)
    xd = x4 * dt_chunk[..., None]
    xd16 = rounded(xd)
    coupling = dot16("cls,cms->clm", c_chunk, b_chunk)
    cum_t = jnp.moveaxis(cum, 2, 1)
    decay = jnp.exp(cum_t[:, :, :, None] - cum_t[:, :, None, :] + mask_bias[:, None])
    kernel = rounded(decay * coupling[:, None])
    y_within = dot16("chlm,cmhp->clhp", kernel, xd16)
    in_end = (seg_chunk == end_chunk[:, None]).astype(F32)[..., None]
    in_start = (seg_chunk == end_before[:, None]).astype(F32)[..., None]
    tail = jnp.exp(cum[:, -1:] - cum) * in_end
    entry = jnp.exp(cum) * in_start
    keep = jnp.exp(cum[:, -1]) * (end_before == end_chunk).astype(F32)[:, None]
    xt16 = rounded(xd * tail[..., None])
    added = dot16("cmhp,cms->chps", xt16, b_chunk)

    local, keep_local = added[0], keep[0]
    for c in range(1, chunks):
        local = added[c] + keep[c][:, None, None] * local
        keep_local = keep_local * keep[c]
    need = -(-(DOC_MOST - 1) // own)
    entering = [reach_over(from_earlier, local, keep_local, size, need)]
    for c in range(chunks - 1):
        entering.append(added[c] + keep[c][:, None, None] * entering[c])
    entering = jnp.stack(entering, 0)
    entering16 = entering.astype(BF16)
    y_entry = dot16("cls,chps->clhp", c_chunk, entering16)
    y = (y_within + y_entry * entry[..., None]).reshape(own, inner) + skip_wide * x

    z_gate = jax.nn.silu(z)
    gated = y * z_gate
    inv_gate = lax.rsqrt(jnp.mean(gated * gated, axis=1, keepdims=True) + EPSILON)
    gated_out = (gated * inv_gate * out_gain).astype(BF16)
    block_out = (rows_in + back_from_columns(gated_out, w_o)).astype(BF16)
    grad_gate = onto_columns(cotangent, w_o)
    grad_norm_gain = jnp.sum(grad_gate * gated * inv_gate, axis=0)
    scaled_gate = grad_gate * out_gain
    cross = jnp.sum(scaled_gate * gated, axis=1, keepdims=True)
    grad_gated = inv_gate * scaled_gate - gated * (inv_gate * inv_gate * inv_gate) * (cross / inner)

    dy = grad_gated * z_gate
    dz = grad_gated * y * silu_grad(z)
    grad_skip = jnp.sum((dy * x).reshape(own, heads, head_width), axis=(0, 2))

    dy4 = split(dy)
    dy16 = rounded(dy4)
    dye16 = rounded(dy4 * entry[..., None])
    back_added = dot16("clhp,cls->chps", dye16, c_chunk)
    back_local = back_added[-1]
    for c in range(chunks - 2, -1, -1):
        back_local = back_added[c] + keep[c][:, None, None] * back_local
    leaving = [reach_over(from_later, back_local, keep_local, size, need)]
    for c in range(chunks - 1, 0, -1):
        leaving.append(back_added[c] + keep[c][:, None, None] * leaving[-1])
    leaving = jnp.stack(leaving[::-1], 0)
    leaving16 = leaving.astype(BF16)
    dxd_within = dot16("chlm,clhp->cmhp", kernel, dy16)
    dxt = dot16("cms,chps->cmhp", b_chunk, leaving16)
    dxd = dxd_within + tail[..., None] * dxt
    dx = (dxd * dt_chunk[..., None]).reshape(own, inner) + skip_wide * dy
    dkernel = dot16("clhp,cmhp->chlm", dy16, xd16)
    dcoupling = jnp.sum(dkernel * decay, axis=1)
    dc = dot16("clm,cms->cls", dcoupling, b_chunk) + dot16("clhp,chps->cls", dye16, entering16)
    db = dot16("clm,cls->cms", dcoupling, c_chunk) + dot16("cmhp,chps->cms", xt16, leaving16)
    falls = jnp.sum(
        dy16.astype(F32) * y_within
        + dye16.astype(F32) * y_entry
        - xd16.astype(F32) * dxd_within,
        axis=3,
    )
    rises = jnp.sum(xt16.astype(F32) * dxt, axis=3)
    strict = lower - jnp.eye(CHUNK, dtype=F32)
    da = (
        jnp.einsum("lm,clh->cmh", lower, falls, precision=HIGHEST)
        + jnp.einsum("lm,cmh->clh", strict, rises, precision=HIGHEST)
        + (keep * jnp.sum(leaving * entering, axis=(2, 3)))[:, None]
    )
    ddt = jnp.sum(x4 * dxd, axis=3) + rate * da
    grad_log = rate * jnp.sum(dt_chunk * da, axis=(0, 1))
    ddt_raw = ddt.reshape(own, heads) * jax.nn.sigmoid(dt_raw + dt_shift)
    grad_shift = jnp.sum(ddt_raw, axis=0)

    gx, grad_taps, grad_bias = conv_back(dx * silu_grad(x_pre), x_ext, x_taps, same)
    dbc = jnp.concatenate([db, dc], 2).reshape(own, state2)
    gbc, grad_bc_taps, grad_bc_bias = conv_back(
        dbc * silu_grad(bc_pre), bc_ext, conv_bc_weight, same
    )
    low_x = gx.astype(BF16)
    low_bc = gbc.astype(BF16)
    low_z = dz.astype(BF16)
    low_dt = ddt_raw.astype(BF16)
    normed_own = normed[HALO:]

    own_part = back_from_columns(low_z, w_z) + dot16("tk,dk->td", low_dt, w_d)
    ext_part = back_from_columns(low_x, w_x) + dot16("tk,dk->td", low_bc, w_b)
    last = from_later(ext_part[:HALO], 1, size)
    grad_normed = own_part + ext_part[HALO:]
    grad_normed = grad_normed.at[own - HALO :].add(last)
    scaled_in = grad_normed * norm_in_gain
    input_grad = (
        cotangent.astype(F32)
        + inv_rms * scaled_in
        - rows_in * (inv_rms * inv_rms * inv_rms) * jnp.mean(scaled_in * rows_in, axis=1, keepdims=True)
    )
    grad_in_gain = jnp.sum(grad_normed * rows_in * inv_rms, axis=0)

    def to_pair(v):
        pairs = [(at, at ^ 1) for at in range(dp_size)]
        other = lax.ppermute(v, "dp", pairs)
        return jnp.where(core == 0, jnp.stack([v, other]), jnp.stack([other, v])).reshape(
            2 * v.shape[0], -1
        )

    def left_of(v):
        split_rows = v.T.reshape(dp_size // 2, 2, dp_rows, v.shape[0])
        return lax.dynamic_index_in_dim(split_rows, core, 1, keepdims=False)

    normed_pair = to_pair(normed)
    left_ext = left_of(normed_pair)
    low_z_ext = jnp.pad(low_z, ((HALO, 0), (0, 0)))
    low_side = jnp.concatenate(
        [
            low_bc.reshape(-1, size, bc_cols),
            jnp.pad(low_dt, ((HALO, 0), (0, 0))).reshape(-1, size, heads_own),
        ],
        2,
    )
    low_side = jnp.pad(low_side, ((0, 0), (0, 0), (0, 128 - side))).reshape(-1, size * 128)
    parts = [
        gradient_pieces(left_of(to_pair(cotangent)), to_pair(gated_out), size),
        gradient_pieces(left_ext, to_pair(low_z_ext), size),
        gradient_pieces(left_ext, to_pair(low_x), size),
        gradient_pieces(left_ext, to_pair(low_side), size),
    ]
    parts = [v.reshape((dp_size // 2,) + sizes[1:] + v.shape[2:]) for v in parts]
    head_sum = jnp.stack([grad_shift, grad_log, grad_skip], 0).reshape(-1)
    row = jnp.concatenate([grad_in_gain, grad_bc_taps.reshape(-1), grad_bc_bias])
    small_sum = jnp.concatenate(
        [
            grad_taps,
            grad_bias[None],
            grad_norm_gain[None],
            jnp.pad(row, (0, inner - row.shape[0]))[None],
            jnp.pad(head_sum, (0, inner - head_sum.shape[0]))[None],
        ],
        0,
    )
    grad_wo, grad_wz, grad_wx, grad_side, small_sum = scatter_gradients(parts, small_sum, sizes)
    grad_wzx = jnp.stack([grad_wz, grad_wx], 1)
    grad_wbc = lax.all_gather(grad_side[:, :bc_cols], SEQ, axis=1, tiled=True)
    grad_wdt = grad_side[:, bc_cols:side]
    channel_own = lax.dynamic_slice_in_dim(small_sum[: taps + 2], place * cols, cols, 1)
    row = small_sum[taps + 2]
    gain_sum = row[:width]
    taps_sum = row[width : width + taps * state2].reshape(taps, state2)
    bias_sum = row[width + taps * state2 : width + (taps + 1) * state2]
    head_sum = small_sum[taps + 3, : 3 * heads].reshape(3, heads)
    head_own = lax.dynamic_slice_in_dim(head_sum, place * heads_own, heads_own, 1)
    return (
        block_out,
        input_grad,
        gain_sum,
        grad_wzx,
        grad_wbc,
        grad_wdt,
        channel_own[:taps],
        channel_own[taps],
        taps_sum,
        bias_sum,
        head_own[0],
        head_own[1],
        head_own[2],
        channel_own[taps + 1],
        grad_wo,
    )


def solution(mesh):
    rows = P(ALL, None)
    in_specs = (
        rows,
        P("dp", None),
        P(),
        P("dp", None, SEQ),
        P("dp", None),
        P("dp", SEQ),
        P(None, SEQ),
        P(SEQ),
        P(),
        P(),
        P(SEQ),
        P(SEQ),
        P(SEQ),
        P(SEQ),
        P("dp", SEQ),
        rows,
    )
    out_specs = (
        rows,
        rows,
        P(),
        P("dp", None, SEQ),
        P("dp", None),
        P("dp", SEQ),
        P(None, SEQ),
        P(SEQ),
        P(),
        P(),
        P(SEQ),
        P(SEQ),
        P(SEQ),
        P(SEQ),
        P("dp", SEQ),
    )
    return jax.shard_map(
        body, mesh=mesh, in_specs=in_specs, out_specs=out_specs, check_vma=False
    )
```

```python
import functools

import jax
import jax.numpy as jnp
from jax import lax
from jax.experimental import pallas as pl
from jax.experimental.pallas import tpu as pltpu
from jax.sharding import PartitionSpec as P

EPSILON = 1e-05
DOC_MOST = 2000
CHUNK = 128
HALO = 16
MASKED = -1e30
HIGHEST = lax.Precision.HIGHEST
SEQ = ("head", "tensor")
ALL = ("dp", "head", "tensor")
BF16 = jnp.bfloat16
F32 = jnp.float32
MESH = pl.DeviceIdType.MESH
VMEM_BYTES = 56 << 20


def dot16(pattern, left, right):
    return jnp.einsum(pattern, left.astype(BF16), right.astype(BF16), preferred_element_type=F32)


def rounded(v):
    return lax.optimization_barrier(v.astype(BF16))


def silu_grad(v):
    gate = jax.nn.sigmoid(v)
    return gate * (1.0 + v * (1.0 - gate))


def coordinates():
    dp = lax.axis_index("dp")
    return lax.div(dp, 2), lax.rem(dp, 2), lax.axis_index("head"), lax.axis_index("tensor")


def enter_kernel(x, core, head, tensor, xs, hs, ts, sibling):
    barrier = pltpu.get_barrier_semaphore()
    count = 0
    for step in range(1, hs):
        pl.semaphore_signal(barrier, 1, device_id={"head": lax.rem(head + step, hs)}, device_id_type=MESH)
        count += 1
    for step in range(1, ts):
        pl.semaphore_signal(barrier, 1, device_id={"tensor": lax.rem(tensor + step, ts)}, device_id_type=MESH)
        count += 1
    for step in range(1, xs):
        other = 2 * lax.rem(x + step, xs) + core
        pl.semaphore_signal(barrier, 1, device_id={"dp": other}, device_id_type=MESH)
        count += 1
    if sibling:
        pl.semaphore_signal(barrier, 1, device_id={"dp": 2 * x + 1 - core}, device_id_type=MESH)
        count += 1
    pl.semaphore_wait(barrier, count)


def gather_kernel(sizes, chunks, kinds, *refs):
    xs, hs, ts = sizes
    parts, small = refs[:kinds], refs[kinds]
    fulls, small_full = refs[kinds + 1 : 2 * kinds + 1], refs[2 * kinds + 1]
    send, recv, small_send, small_recv, own_sem = refs[2 * kinds + 2 :]
    x, core, head, tensor = coordinates()
    dp = 2 * x + core
    for kind in range(kinds):
        pltpu.make_async_copy(
            parts[kind], fulls[kind].at[dp, head, tensor], own_sem.at[kind]
        ).start()
    pltpu.make_async_copy(small, small_full.at[head, tensor], own_sem.at[kinds]).start()
    enter_kernel(x, core, head, tensor, xs, hs, ts, True)

    def copy(src, dst, index, slot, device):
        return pltpu.make_async_remote_copy(
            src_ref=src,
            dst_ref=dst,
            send_sem=send.at[index, slot],
            recv_sem=recv.at[index, slot],
            device_id=device,
            device_id_type=MESH,
        )

    def along_head(index):
        kind, start, length, _ = chunks[index]
        rows = pl.ds(start, length)
        return [
            copy(
                parts[kind].at[rows],
                fulls[kind].at[dp, head, tensor, rows],
                index,
                step - 1,
                {"head": lax.rem(head + step, hs)},
            )
            for step in range(1, hs)
        ]

    def over(index, axis, second):
        kind, start, length, _ = chunks[index]
        rows = pl.ds(start, length)
        base = hs - 1 if second else hs - 1 + max(xs, ts)
        copies = []
        if axis == "tensor":
            homes = [dp] if second else [2 * home + core for home in range(xs)]
            for step in range(1, ts):
                for home in homes:
                    view = fulls[kind].at[home, :, tensor, rows]
                    device = {"tensor": lax.rem(tensor + step, ts)}
                    copies.append(copy(view, view, index, base + len(copies), device))
        else:
            for step in range(1, xs):
                view = fulls[kind].at[dp, :, tensor, rows] if second else fulls[kind].at[dp, :, :, rows]
                device = {"dp": 2 * lax.rem(x + step, xs) + core}
                copies.append(copy(view, view, index, base + len(copies), device))
        return copies

    def to_sibling(index):
        kind, start, length, _ = chunks[index]
        rows = pl.ds(start, length)
        base = hs - 1 + max(xs, ts) + max(xs, xs * ts)
        return [
            copy(
                fulls[kind].at[2 * home + core, :, :, rows],
                fulls[kind].at[2 * home + core, :, :, rows],
                index,
                base + home,
                {"dp": 2 * x + 1 - core},
            )
            for home in range(xs)
        ]

    def stage(index, number):
        tensor_first = chunks[index][3]
        if number == 0:
            return along_head(index)
        if number == 1:
            return over(index, "tensor" if tensor_first else "x", True)
        if number == 2:
            return over(index, "x" if tensor_first else "tensor", False)
        return to_sibling(index)

    small_tensor = [
        pltpu.make_async_remote_copy(
            src_ref=small,
            dst_ref=small_full.at[head, tensor],
            send_sem=small_send.at[step - 1],
            recv_sem=small_recv.at[step - 1],
            device_id={"tensor": lax.rem(tensor + step, ts)},
            device_id_type=MESH,
        )
        for step in range(1, ts)
    ]
    small_head = [
        pltpu.make_async_remote_copy(
            src_ref=small_full.at[head],
            dst_ref=small_full.at[head],
            send_sem=small_send.at[ts + step - 2],
            recv_sem=small_recv.at[ts + step - 2],
            device_id={"head": lax.rem(head + step, hs)},
            device_id_type=MESH,
        )
        for step in range(1, hs)
    ]
    total = len(chunks)
    ahead = 4
    for one in small_tensor:
        one.start()
    for index in range(min(ahead, total)):
        for one in stage(index, 0):
            one.start()
    for kind in range(kinds):
        pltpu.make_async_copy(
            parts[kind], fulls[kind].at[dp, head, tensor], own_sem.at[kind]
        ).wait()
    pltpu.make_async_copy(small, small_full.at[head, tensor], own_sem.at[kinds]).wait()
    for one in small_tensor:
        one.wait_recv()
    for one in small_head:
        one.start()
    for tick in range(total + 6):
        for number in range(4):
            index = tick - 2 * number
            if 0 <= index < total:
                for one in stage(index, number):
                    one.wait_recv()
                if number < 3:
                    for one in stage(index, number + 1):
                        one.start()
                if number == 0 and index + ahead < total:
                    for one in stage(index + ahead, 0):
                        one.start()
    for one in small_head:
        one.wait_recv()
    for one in small_tensor + small_head:
        one.wait_send()
    for index in range(total):
        for number in range(4):
            for one in stage(index, number):
                one.wait_send()


def row_chunks(rows, first, kinds, pieces):
    step = rows // pieces
    return [
        (kind, piece * step, step, piece % 2 == 1)
        for kind in range(first, kinds)
        for piece in range(pieces)
    ]


def gather_weights(parts, small, sizes):
    xs, hs, ts = sizes
    kinds = len(parts)
    chunks = [(0, 0, parts[0].shape[0], True)] + row_chunks(parts[1].shape[0], 1, kinds, 4)
    slots = hs - 1 + max(xs, ts) + max(xs, xs * ts) + xs
    full = [jax.ShapeDtypeStruct((2 * xs, hs, ts) + part.shape, part.dtype) for part in parts]
    full.append(jax.ShapeDtypeStruct((hs, ts) + small.shape, small.dtype))
    anywhere = pl.BlockSpec(memory_space=pl.ANY)
    return pl.pallas_call(
        functools.partial(gather_kernel, sizes, chunks, kinds),
        out_shape=full,
        in_specs=[anywhere] * (kinds + 1),
        out_specs=[anywhere] * (kinds + 1),
        scratch_shapes=[
            pltpu.SemaphoreType.DMA((len(chunks), slots)),
            pltpu.SemaphoreType.DMA((len(chunks), slots)),
            pltpu.SemaphoreType.DMA((hs + ts,)),
            pltpu.SemaphoreType.DMA((hs + ts,)),
            pltpu.SemaphoreType.DMA((kinds + 1,)),
        ],
        compiler_params=pltpu.CompilerParams(
            collective_id=0, has_side_effects=True, vmem_limit_bytes=VMEM_BYTES
        ),
        cost_estimate=busy(60),
    )(*parts, small)


def scatter_kernel(sizes, chunks, kinds, *refs):
    xs, hs, ts = sizes
    parts, small = refs[:kinds], refs[kinds]
    outs, small_out = refs[kinds + 1 : 2 * kinds + 1], refs[2 * kinds + 1]
    rest = refs[2 * kinds + 2 :]
    bufs, rest = rest[: 4 * len(chunks)], rest[4 * len(chunks) :]
    small_acc, small_in, send, recv, small_send, small_recv, own_sem, side_send, side_recv = rest
    x, core, head, tensor = coordinates()
    dp = 2 * x + core
    total = len(chunks)

    def loads(index):
        kind, start, length, x_first = chunks[index]
        rows = pl.ds(start, length)
        held = bufs[4 * index]
        view = parts[kind].at[x, :, :, rows] if x_first else parts[kind].at[:, :, tensor, rows]
        return pltpu.make_async_copy(view, held, own_sem.at[index])

    def copy(src, dst, index, slot, device):
        return pltpu.make_async_remote_copy(
            src_ref=src,
            dst_ref=dst,
            send_sem=send.at[index, slot],
            recv_sem=recv.at[index, slot],
            device_id=device,
            device_id_type=MESH,
        )

    def stage(index, number):
        kind, start, length, x_first = chunks[index]
        rows = pl.ds(start, length)
        held, first, second, third = bufs[4 * index : 4 * index + 4]
        most = max(xs, ts) - 1
        if number == 0 and x_first:
            return [
                copy(
                    parts[kind].at[lax.rem(x + step, xs), :, :, rows],
                    first.at[step - 1],
                    index,
                    step - 1,
                    {"dp": 2 * lax.rem(x + step, xs) + core},
                )
                for step in range(1, xs)
            ]
        if number == 0:
            return [
                copy(
                    parts[kind].at[:, :, lax.rem(tensor + step, ts), rows],
                    first.at[step - 1],
                    index,
                    step - 1,
                    {"tensor": lax.rem(tensor + step, ts)},
                )
                for step in range(1, ts)
            ]
        if number == 1 and x_first:
            return [
                copy(
                    held.at[:, lax.rem(tensor + step, ts)],
                    second.at[step - 1],
                    index,
                    most + step - 1,
                    {"tensor": lax.rem(tensor + step, ts)},
                )
                for step in range(1, ts)
            ]
        if number == 1:
            return [
                copy(
                    held.at[lax.rem(x + step, xs)],
                    second.at[step - 1],
                    index,
                    most + step - 1,
                    {"dp": 2 * lax.rem(x + step, xs) + core},
                )
                for step in range(1, xs)
            ]
        copies = []
        for step in range(1, hs):
            other = lax.rem(head + step, hs)
            view = held.at[other, tensor] if x_first else held.at[x, other]
            copies.append(
                copy(view, third.at[step - 1], index, 2 * most + step - 1, {"head": other})
            )
        return copies

    def add(index, number):
        kind, start, length, x_first = chunks[index]
        held, first, second, third = bufs[4 * index : 4 * index + 4]
        if number == 0:

            @pl.loop(0, held.shape[0])
            def _(one):
                for two in range(held.shape[1]):
                    value = held[one, two].astype(F32)
                    for step in range(first.shape[0]):
                        value = value + first[step, one, two].astype(F32)
                    held[one, two] = value.astype(BF16)

        elif number == 1:

            @pl.loop(0, hs)
            def _(one):
                where = (one, tensor) if x_first else (x, one)
                value = held[where].astype(F32)
                for step in range(second.shape[0]):
                    value = value + second[step, one].astype(F32)
                held[where] = value.astype(BF16)

        else:
            where = (head, tensor) if x_first else (x, head)
            value = held[where].astype(F32)
            for step in range(third.shape[0]):
                value = value + third[step].astype(F32)
            if kind == 0:
                outs[kind][head, tensor] = value
            else:
                outs[kind][start : start + length, :] = value

    def side_copy(view, slot, device):
        return pltpu.make_async_remote_copy(
            src_ref=view,
            dst_ref=view,
            send_sem=side_send.at[slot],
            recv_sem=side_recv.at[slot],
            device_id=device,
            device_id_type=MESH,
        )

    side_tensor = [
        side_copy(outs[0].at[head, tensor], step - 1, {"tensor": lax.rem(tensor + step, ts)})
        for step in range(1, ts)
    ]
    side_head = [
        side_copy(outs[0].at[head], ts + step - 2, {"head": lax.rem(head + step, hs)})
        for step in range(1, hs)
    ]

    small_slots = [1, xs - 1, ts - 1, hs - 1]
    small_base = [0, 1, xs, xs + ts - 1]

    def small_stage(number):
        copies = []
        for step in range(1, small_slots[number] + 1):
            slot = small_base[number] + step - 1
            device = (
                {"dp": 2 * x + 1 - core},
                {"dp": 2 * lax.rem(x + step, xs) + core},
                {"tensor": lax.rem(tensor + step, ts)},
                {"head": lax.rem(head + step, hs)},
            )[number]
            copies.append(
                pltpu.make_async_remote_copy(
                    src_ref=small if number == 0 else small_acc.at[number - 1],
                    dst_ref=small_in.at[slot],
                    send_sem=small_send.at[slot],
                    recv_sem=small_recv.at[slot],
                    device_id=device,
                    device_id_type=MESH,
                )
            )
        return copies

    def small_add(number):
        mine = small[...] if number == 0 else small_acc[number - 1]
        size = small_slots[number] + 1
        place = (core, x, tensor, head)[number]
        value = None
        for at in range(size):
            step = lax.rem(place - at + size, size)
            slot = small_base[number] + jnp.maximum(step - 1, 0)
            here = jnp.where(step == 0, mine, small_in[slot])
            value = here if value is None else value + here
        if number < 3:
            small_acc[number] = value
        else:
            small_out[...] = value

    for index in range(total):
        loads(index).start()
    enter_kernel(x, core, head, tensor, xs, hs, ts, True)
    ahead = 4
    for one in small_stage(0):
        one.start()
    for index in range(min(ahead, total)):
        for one in stage(index, 0):
            one.start()
    for tick in range(total + 4):
        for number in range(3):
            index = tick - 2 * number
            if 0 <= index < total:
                for one in stage(index, number):
                    one.wait_recv()
                if number == 0:
                    loads(index).wait()
                    if index + ahead < total:
                        for one in stage(index + ahead, 0):
                            one.start()
                add(index, number)
                if number < 2:
                    for one in stage(index, number + 1):
                        one.start()
        if tick == 4:
            for one in side_tensor:
                one.start()
        if tick == 6:
            for one in side_tensor:
                one.wait_recv()
            for one in side_head:
                one.start()
        if tick < 4:
            for one in small_stage(tick):
                one.wait_recv()
            small_add(tick)
            if tick < 3:
                for one in small_stage(tick + 1):
                    one.start()
    for one in side_head:
        one.wait_recv()
    for one in side_tensor + side_head:
        one.wait_send()
    for number in range(4):
        for one in small_stage(number):
            one.wait_send()
    for index in range(total):
        for number in range(3):
            for one in stage(index, number):
                one.wait_send()


def scatter_gradients(parts, small, sizes):
    xs, hs, ts = sizes
    kinds = len(parts)
    chunks = [(0, 0, parts[0].shape[3], True)] + row_chunks(parts[1].shape[3], 1, kinds, 4)
    scratch = []
    for kind, _, length, x_first in chunks:
        cols = parts[kind].shape[4]
        held = (hs, ts) if x_first else (xs, hs)
        near, far = (xs, ts) if x_first else (ts, xs)
        scratch += [
            pltpu.VMEM(held + (length, cols), BF16),
            pltpu.VMEM((near - 1,) + held + (length, cols), BF16),
            pltpu.VMEM((far - 1, hs, length, cols), BF16),
            pltpu.VMEM((hs - 1, length, cols), BF16),
        ]
    slots = 2 * (max(xs, ts) - 1) + hs - 1
    small_slots = xs + ts + hs - 2
    anywhere = pl.BlockSpec(memory_space=pl.ANY)
    whole = pl.BlockSpec(memory_space=pltpu.VMEM)
    return pl.pallas_call(
        functools.partial(scatter_kernel, sizes, chunks, kinds),
        out_shape=[jax.ShapeDtypeStruct((hs, ts) + parts[0].shape[3:], F32)]
        + [jax.ShapeDtypeStruct(part.shape[3:], F32) for part in parts[1:]]
        + [jax.ShapeDtypeStruct(small.shape, F32)],
        in_specs=[anywhere] * kinds + [whole],
        out_specs=[whole] * (kinds + 1),
        scratch_shapes=scratch
        + [
            pltpu.VMEM((3,) + small.shape, F32),
            pltpu.VMEM((small_slots,) + small.shape, F32),
            pltpu.SemaphoreType.DMA((len(chunks), slots)),
            pltpu.SemaphoreType.DMA((len(chunks), slots)),
            pltpu.SemaphoreType.DMA((small_slots,)),
            pltpu.SemaphoreType.DMA((small_slots,)),
            pltpu.SemaphoreType.DMA((len(chunks),)),
            pltpu.SemaphoreType.DMA((hs + ts,)),
            pltpu.SemaphoreType.DMA((hs + ts,)),
        ],
        compiler_params=pltpu.CompilerParams(
            collective_id=1, has_side_effects=True, vmem_limit_bytes=VMEM_BYTES
        ),
        cost_estimate=busy(60),
    )(*parts, small)


def group_of(cols):
    return 1 if cols % 128 == 0 else 128 // cols if 128 % cols == 0 else 2


def busy(microseconds):
    return pl.CostEstimate(flops=microseconds * 900_000_000, bytes_accessed=0, transcendentals=0)


def local_params():
    return pltpu.CompilerParams(vmem_limit_bytes=VMEM_BYTES)


def gradient_pieces(lefts, values, hts):
    kinds = len(lefts)
    left, value = lefts[0], values[0]
    xs, depth, count = left.shape
    cols = value.shape[1] // hts
    group = group_of(cols)

    def kernel(*refs):
        out_ref = refs[-1]
        for kind in range(kinds):
            left_ref, value_ref = refs[kind], refs[kinds + kind]
            for at in range(xs):
                for one in range(group):
                    out_ref[at, one, kind] = jnp.dot(
                        left_ref[at],
                        value_ref[:, one * cols : (one + 1) * cols],
                        preferred_element_type=F32,
                    ).astype(BF16)

    return pl.pallas_call(
        kernel,
        grid=(hts // group,),
        out_shape=jax.ShapeDtypeStruct((xs, hts, kinds, depth, cols), BF16),
        in_specs=[pl.BlockSpec(left.shape, lambda j: (0, 0, 0))] * kinds
        + [pl.BlockSpec((count, group * cols), lambda j: (0, j))] * kinds,
        out_specs=pl.BlockSpec((xs, group, kinds, depth, cols), lambda j: (0, j, 0, 0, 0)),
        compiler_params=local_params(),
        cost_estimate=busy(12 * kinds),
    )(*lefts, *values)


def silu_of(v):
    return v * jax.nn.sigmoid(v)


def dot_nt(left, right):
    return lax.dot_general(left, right, (((1,), (1,)), ((), ())), preferred_element_type=F32)


def dot_tn(left, right):
    return lax.dot_general(left, right, (((0,), (0,)), ((), ())), preferred_element_type=F32)


def dot_nn(left, right):
    return jnp.dot(left, right, preferred_element_type=F32)


def thirds(v):
    high = rounded(v)
    rest = v - high.astype(F32)
    middle = rounded(rest)
    return jnp.concatenate([high, middle, rounded(rest - middle.astype(F32))], 1)


def conv_pre(ext_ref, taps_ref, same_ref, own, width):
    total = taps_ref[width : width + 1] + taps_ref[width - 1 : width] * ext_ref[HALO:]
    for back in range(1, width):
        total = total + (
            taps_ref[width - 1 - back : width - back]
            * ext_ref[HALO - back : HALO - back + own]
            * same_ref[:, back - 1 : back]
        )
    return total


def lane_masks():
    lane = lax.broadcasted_iota(jnp.int32, (1, 128), 1)
    first = (lane < 64).astype(F32)
    return first, 1.0 - first


def two_apart(pair, masks):
    return jnp.concatenate([pair * masks[0].astype(BF16), pair * masks[1].astype(BF16)], 0)


def decay_pair(cum_ref, cumt_ref, bias, rows, pair):
    parts = []
    for head in (2 * pair, 2 * pair + 1):
        spread = cum_ref[0, rows, head : head + 1] - cumt_ref[0, head : head + 1, rows] + bias
        parts.append(jnp.exp(spread))
    return parts


class Scan:
    def __init__(self, own, sizes, rows, cols, heads_own, taps):
        self.own, self.ext, self.taps = own, own + HALO, taps
        self.dps, self.hts = 2 * sizes[0], sizes[1] * sizes[2]
        self.rows, self.cols = rows, cols
        self.group = group_of(cols)
        self.wide = self.group * cols
        self.heads = self.group * heads_own
        self.groups = self.hts // self.group
        self.chunks = own // CHUNK
        self.width = self.dps * rows
        self.inner = self.hts * cols
        self.pairs = self.wide // 128

    def call(self, kernel, ins, outs, scratch=()):
        arrays = [array for array, _ in ins]
        return pl.pallas_call(
            kernel,
            grid=(self.groups,),
            out_shape=[shape for shape, _ in outs],
            in_specs=[spec for _, spec in ins],
            out_specs=[spec for _, spec in outs],
            scratch_shapes=list(scratch),
            compiler_params=local_params(),
            cost_estimate=busy(22),
        )(*arrays)

    def full(self, array):
        return (array, pl.BlockSpec(array.shape, lambda j: (0,) * array.ndim))

    def pieces(self, array, kind=None):
        if kind is None:
            block = (self.dps, self.group, self.rows, self.cols)
            return (array, pl.BlockSpec(block, lambda j: (0, j, 0, 0)))
        block = (self.dps, self.group, None, self.rows, self.cols)
        return (array, pl.BlockSpec(block, lambda j: (0, j, kind, 0, 0)))

    def lanes(self, array):
        lead = array.shape[:-1]
        return (array, pl.BlockSpec(lead + (self.wide,), lambda j: (0,) * len(lead) + (j,)))

    def states(self, array):
        lead = array.shape[:-2]
        block = lead + (self.wide, array.shape[-1])
        return (array, pl.BlockSpec(block, lambda j: (0,) * len(lead) + (j, 0)))

    def grouped(self, array):
        block = (1,) + array.shape[1:]
        return (array, pl.BlockSpec(block, lambda j: (j,) + (0,) * (array.ndim - 1)))

    def project(self, rows_ref, piece_ref, out_ref):
        for one in range(self.group):
            weights = piece_ref[:, one].reshape(self.width, self.cols)
            out_ref[:, one * self.cols : (one + 1) * self.cols] = dot_nn(rows_ref, weights)

    def project_back(self, value_ref, piece_ref, out_ref):
        @pl.when(pl.program_id(0) == 0)
        def _():
            out_ref[...] = jnp.zeros_like(out_ref)

        for one in range(self.group):
            weights = piece_ref[:, one].reshape(self.width, self.cols)
            out_ref[...] += dot_nt(value_ref[:, one * self.cols : (one + 1) * self.cols], weights)

    def chunk_rows(self, c):
        return slice(c * CHUNK, (c + 1) * CHUNK)

    def lane_sums(self, v):
        total = v[:, :128]
        for pair in range(1, self.pairs):
            total = total + v[:, pair * 128 : (pair + 1) * 128]
        return total

    def head_sums(self, v, ones_ref):
        high = v.astype(BF16)
        low = (v - high.astype(F32)).astype(BF16)
        return dot_nn(high, ones_ref[...]) + dot_nn(low, ones_ref[...])

    def s1(self, normed, w_x, conv_rows, same, dt3, tail3, widen, cum_g, cumt_g, coupling, bias, bc, keep_cols):
        own, state = self.own, bc.shape[1] // 2

        def kernel(
            normed_ref, w_ref, conv_ref, same_ref, dt_ref, tail_ref, widen_ref, cum_ref, cumt_ref,
            coupling_ref, bias_ref, bc_ref, keep_ref, ext_ref, x_ref, within_ref, added_ref, local_ref, xd_ref, xt_ref,
        ):
            self.project(normed_ref[...], w_ref, ext_ref)
            x = silu_of(conv_pre(ext_ref, conv_ref, same_ref, own, self.taps))
            x_ref[...] = x
            xd = x * dot_nn(dt_ref[...], widen_ref[...])
            xd_ref[...] = xd.astype(BF16)
            xt_ref[...] = (xd * dot_nn(tail_ref[...], widen_ref[...])).astype(BF16)
            masks = lane_masks()
            held = None
            for c in range(self.chunks):
                rows = self.chunk_rows(c)
                for pair in range(self.pairs):
                    lanes = slice(pair * 128, (pair + 1) * 128)
                    first, second = decay_pair(cum_ref, cumt_ref, bias_ref[c], rows, pair)
                    mix = coupling_ref[c]
                    kernel16 = jnp.concatenate([(first * mix).astype(BF16), (second * mix).astype(BF16)], 1)
                    within_ref[rows, lanes] = dot_nn(kernel16, two_apart(xd_ref[rows, lanes], masks))
                added = dot_tn(xt_ref[rows], bc_ref[rows, :state])
                added_ref[c] = added
                held = added if held is None else added + keep_ref[:, c : c + 1] * held
            local_ref[...] = held.astype(BF16)

        f = jax.ShapeDtypeStruct
        return self.call(
            kernel,
            [
                self.full(normed), self.pieces(w_x), self.lanes(conv_rows), self.full(same), self.full(dt3),
                self.full(tail3), self.lanes(widen), self.grouped(cum_g), self.grouped(cumt_g),
                self.full(coupling), self.full(bias), self.full(bc), self.states(keep_cols),
            ],
            [
                self.lanes(f((self.ext, self.inner), F32)), self.lanes(f((own, self.inner), F32)),
                self.lanes(f((own, self.inner), F32)), self.states(f((self.chunks, self.inner, state), F32)),
                self.states(f((self.inner, state), BF16)),
            ],
            [pltpu.VMEM((own, self.wide), BF16), pltpu.VMEM((own, self.wide), BF16)],
        )

    def s2(self, normed_own, w_zo, within, x, skip_rows, entry3, widen, bc, entering, added, keep_cols):
        own, state = self.own, bc.shape[1] // 2

        def kernel(
            normed_ref, w_ref, within_ref, x_ref, skip_ref, entry_ref, widen_ref, bc_ref, entering_ref,
            added_ref, keep_ref, z_ref, y_ref, states_ref, squares_ref,
        ):
            self.project(normed_ref[...], w_ref, z_ref)
            entry = dot_nn(entry_ref[...], widen_ref[...])
            held = entering_ref[...]
            for c in range(self.chunks):
                rows = self.chunk_rows(c)
                held16 = held.astype(BF16)
                states_ref[c] = held16
                carried = dot_nt(bc_ref[rows, state:], held16)
                y_ref[rows] = within_ref[rows] + carried * entry[rows] + skip_ref[...] * x_ref[rows]
                if c + 1 < self.chunks:
                    held = added_ref[c] + keep_ref[:, c : c + 1] * held
            gated = y_ref[...] * silu_of(z_ref[...])
            squares = self.lane_sums(gated * gated)

            @pl.when(pl.program_id(0) == 0)
            def _():
                squares_ref[...] = squares

            @pl.when(pl.program_id(0) > 0)
            def _():
                squares_ref[...] += squares

        f = jax.ShapeDtypeStruct
        return self.call(
            kernel,
            [
                self.full(normed_own), self.pieces(w_zo, 0), self.lanes(within), self.lanes(x), self.lanes(skip_rows),
                self.full(entry3), self.lanes(widen), self.full(bc), self.states(entering), self.states(added),
                self.states(keep_cols),
            ],
            [
                self.lanes(f((own, self.inner), F32)), self.lanes(f((own, self.inner), F32)),
                self.states(f((self.chunks, self.inner, state), BF16)), self.full(f((own, 128), F32)),
            ],
        )

    def inv_gate(self, squares_ref):
        return lax.rsqrt(jnp.sum(squares_ref[...], axis=1, keepdims=True) / self.inner + EPSILON)

    def s3(self, y, z, squares, gain_row, w_zo, cotangent, residual):
        own = self.own

        def kernel(
            y_ref, z_ref, squares_ref, gain_ref, w_ref, cot_ref, residual_ref,
            gated_ref, grad_ref, cross_ref, gain_grad_ref, out_ref, sum_ref,
        ):
            inv = self.inv_gate(squares_ref)
            gated = y_ref[...] * silu_of(z_ref[...])
            normal = gated * inv
            gated_ref[...] = (normal * gain_ref[...]).astype(BF16)
            self.project_back(gated_ref, w_ref, sum_ref)
            self.project(cot_ref[...], w_ref, grad_ref)
            grad = grad_ref[...]
            gain_grad_ref[...] = jnp.broadcast_to(
                jnp.sum(grad * normal, axis=0, keepdims=True), gain_grad_ref.shape
            )
            cross = self.lane_sums(grad * gain_ref[...] * gated)

            @pl.when(pl.program_id(0) == 0)
            def _():
                cross_ref[...] = cross

            @pl.when(pl.program_id(0) > 0)
            def _():
                cross_ref[...] += cross

            @pl.when(pl.program_id(0) == self.groups - 1)
            def _():
                out_ref[...] = (residual_ref[...].astype(F32) + sum_ref[...]).astype(BF16)

        f = jax.ShapeDtypeStruct
        return self.call(
            kernel,
            [
                self.lanes(y), self.lanes(z), self.full(squares), self.lanes(gain_row), self.pieces(w_zo, 1),
                self.full(cotangent), self.full(residual),
            ],
            [
                self.lanes(f((own, self.inner), BF16)), self.lanes(f((own, self.inner), F32)),
                self.full(f((own, 128), F32)), self.lanes(f((8, self.inner), F32)),
                self.full(f((own, self.width), BF16)),
            ],
            [pltpu.VMEM((own, self.width), F32)],
        )

    def s4(self, y, z, squares, cross, gain_row, grad_gate, w_zo, entry3, widen, bc, keep_cols):
        own, state = self.own, bc.shape[1] // 2

        def kernel(
            y_ref, z_ref, squares_ref, cross_ref, gain_ref, grad_ref, w_ref, entry_ref, widen_ref, bc_ref,
            keep_ref, low_ref, dy_ref, back_ref, local_ref, through_ref, dye_ref,
        ):
            inv = self.inv_gate(squares_ref)
            cross_mean = jnp.sum(cross_ref[...], axis=1, keepdims=True) / self.inner
            z = z_ref[...]
            gate = jax.nn.sigmoid(z)
            z_gate = z * gate
            y = y_ref[...]
            grad_gated = inv * (grad_ref[...] * gain_ref[...]) - (y * z_gate) * (inv * inv * inv * cross_mean)
            dy = grad_gated * z_gate
            dy_ref[...] = dy
            low_ref[...] = (grad_gated * y * (gate * (1.0 + z * (1.0 - gate)))).astype(BF16)
            self.project_back(low_ref, w_ref, through_ref)
            dye_ref[...] = (dy * dot_nn(entry_ref[...], widen_ref[...])).astype(BF16)
            held = None
            for c in range(self.chunks - 1, -1, -1):
                rows = self.chunk_rows(c)
                added = dot_tn(dye_ref[rows], bc_ref[rows, state:])
                back_ref[c] = added
                held = added if held is None else added + keep_ref[:, c : c + 1] * held
            local_ref[...] = held.astype(BF16)

        f = jax.ShapeDtypeStruct
        return self.call(
            kernel,
            [
                self.lanes(y), self.lanes(z), self.full(squares), self.full(cross), self.lanes(gain_row),
                self.lanes(grad_gate), self.pieces(w_zo, 0), self.full(entry3), self.lanes(widen), self.full(bc),
                self.states(keep_cols),
            ],
            [
                self.lanes(f((own, self.inner), BF16)), self.lanes(f((own, self.inner), F32)),
                self.states(f((self.chunks, self.inner, state), F32)), self.states(f((self.inner, state), BF16)),
                self.full(f((own, self.width), F32)),
            ],
            [pltpu.VMEM((own, self.wide), BF16)],
        )

    def s5(
        self, dy, x_ext, within, conv_rows, skip_rows, same, dt3, tail3, entry3, widen, ones, cum_g, cumt_g, coupling,
        bias, bc, states, leaving, back_added, keep_cols, w_x,
    ):
        own, state = self.own, bc.shape[1] // 2
        taps = self.taps

        def kernel(
            dy_ref, ext_ref, within_ref, conv_ref, skip_ref, same_ref, dt_ref, tail_ref, entry_ref, widen_ref,
            ones_ref, cum_ref, cumt_ref, coupling_ref, bias_ref, bc_ref, states_ref, leaving_ref, back_ref, keep_ref,
            w_ref, low_ref, rows_ref, head_ref, dots_ref, dbc_ref, dmix_ref, through_ref,
            xd_ref, xt_ref, dy16_ref, dye_ref, dxd_ref, shift_ref,
        ):
            first_step = pl.program_id(0) == 0

            @pl.when(first_step)
            def _():
                dbc_ref[...] = jnp.zeros_like(dbc_ref)
                dmix_ref[...] = jnp.zeros_like(dmix_ref)

            pre = conv_pre(ext_ref, conv_ref, same_ref, own, taps)
            gate = jax.nn.sigmoid(pre)
            x = pre * gate
            dt = dot_nn(dt_ref[...], widen_ref[...])
            tail = dot_nn(tail_ref[...], widen_ref[...])
            xd = x * dt
            xd_ref[...] = xd.astype(BF16)
            xt_ref[...] = (xd * tail).astype(BF16)
            dy = dy_ref[...]
            dy16_ref[...] = dy.astype(BF16)
            entry = dot_nn(entry_ref[...], widen_ref[...])
            dye_ref[...] = (dy * entry).astype(BF16)
            masks = lane_masks()
            held = leaving_ref[...]
            for c in range(self.chunks - 1, -1, -1):
                rows = self.chunk_rows(c)
                held16 = held.astype(BF16)
                into16 = states_ref[c]
                product = held * into16.astype(F32)
                dots_ref[0, c] = jnp.sum(product.reshape(self.heads, 64, state), axis=1)
                spread_back = dot_nt(bc_ref[rows, :state], held16)
                dmix = dmix_ref[c]
                for pair in range(self.pairs):
                    lanes = slice(pair * 128, (pair + 1) * 128)
                    first, second = decay_pair(cum_ref, cumt_ref, bias_ref[c], rows, pair)
                    mix = coupling_ref[c]
                    kernel16 = jnp.concatenate([(first * mix).astype(BF16), (second * mix).astype(BF16)], 1)
                    dy_pair = dy16_ref[rows, lanes]
                    both = dot_tn(kernel16, dy_pair)
                    dxd_ref[rows, lanes] = both[:CHUNK] * masks[0] + both[CHUNK:] * masks[1]
                    dkernel = dot_nt(dy_pair, two_apart(xd_ref[rows, lanes], masks))
                    dmix = dmix + dkernel[:, :CHUNK] * first + dkernel[:, CHUNK:] * second
                dmix_ref[c] = dmix
                dxd_within = dxd_ref[rows]
                carried = dot_nt(bc_ref[rows, state:], into16)
                falls = (
                    dy16_ref[rows].astype(F32) * within_ref[rows]
                    + dye_ref[rows].astype(F32) * carried
                    - xd_ref[rows].astype(F32) * dxd_within
                )
                dxd = dxd_within + tail[rows] * spread_back
                dxd_ref[rows] = dxd
                head_ref[0, 0, rows] = self.head_sums(falls, ones_ref)
                head_ref[0, 1, rows] = self.head_sums(xt_ref[rows].astype(F32) * spread_back, ones_ref)
                head_ref[0, 2, rows] = self.head_sums(x[rows] * dxd, ones_ref)
                dbc_ref[rows, :state] += dot_nn(xt_ref[rows], held16)
                dbc_ref[rows, state:] += dot_nn(dye_ref[rows], into16)
                if c > 0:
                    held = back_ref[c] + keep_ref[:, c : c + 1] * held
            dx = dxd_ref[...] * dt + skip_ref[...] * dy
            grad = dx * (gate * (1.0 + pre * (1.0 - gate)))
            shift_ref[:HALO] = jnp.zeros((HALO, self.wide), F32)
            shift_ref[HALO + own :] = jnp.zeros((HALO, self.wide), F32)
            rows_ref[taps : taps + 1] = jnp.sum(grad, axis=0, keepdims=True)
            rows_ref[taps + 1 : taps + 2] = jnp.sum(dy * x, axis=0, keepdims=True)
            total = None
            for back in range(taps):
                masked = grad if back == 0 else grad * same_ref[:, back - 1 : back]
                shift_ref[HALO : HALO + own] = masked
                tap = conv_ref[taps - 1 - back : taps - back]
                piece = tap * shift_ref[back : back + own + HALO]
                total = piece if total is None else total + piece
                rows_ref[taps - 1 - back : taps - back] = jnp.sum(
                    masked * ext_ref[HALO - back : HALO - back + own], axis=0, keepdims=True
                )
            low_ref[...] = total.astype(BF16)
            self.project_back(low_ref, w_ref, through_ref)

        f = jax.ShapeDtypeStruct
        scratch16 = pltpu.VMEM((own, self.wide), BF16)
        return self.call(
            kernel,
            [
                self.lanes(dy), self.lanes(x_ext), self.lanes(within), self.lanes(conv_rows), self.lanes(skip_rows),
                self.full(same), self.full(dt3), self.full(tail3), self.full(entry3), self.lanes(widen),
                self.full(ones), self.grouped(cum_g), self.grouped(cumt_g), self.full(coupling), self.full(bias),
                self.full(bc), self.states(states), self.states(leaving), self.states(back_added),
                self.states(keep_cols), self.pieces(w_x),
            ],
            [
                self.lanes(f((self.ext, self.inner), BF16)), self.lanes(f((8, self.inner), F32)),
                self.grouped(f((self.groups, 3, own, 128), F32)),
                self.grouped(f((self.groups, self.chunks, self.heads, state), F32)),
                self.full(f((own, 2 * state), F32)), self.full(f((self.chunks, CHUNK, CHUNK), F32)),
                self.full(f((self.ext, self.width), F32)),
            ],
            [
                scratch16, scratch16, scratch16, scratch16, pltpu.VMEM((own, self.wide), F32),
                pltpu.VMEM((own + 2 * HALO, self.wide), F32),
            ],
        )


def conv_before(ext, taps, bias, same):
    own = ext.shape[0] - HALO
    total = bias + taps[-1] * ext[HALO:]
    for back in range(1, taps.shape[0]):
        total = total + taps[-1 - back] * ext[HALO - back : HALO - back + own] * same[back - 1]
    return total


def conv_back(grad, ext, taps, same):
    own = grad.shape[0]
    width = taps.shape[0]
    below = jnp.zeros((HALO, grad.shape[1]), F32)
    total = jnp.concatenate([below, taps[-1] * grad], 0)
    rows = [jnp.sum(grad * ext[HALO:], axis=0)]
    for back in range(1, width):
        masked = grad * same[back - 1]
        rows.append(jnp.sum(masked * ext[HALO - back : HALO - back + own], axis=0))
        total = total + jnp.pad(
            taps[-1 - back] * masked, ((HALO - back, back), (0, 0))
        )
    return total, jnp.stack(rows[::-1], 0), jnp.sum(grad, axis=0)


def from_earlier(values, distance, size):
    return lax.ppermute(values, SEQ, [(i, i + distance) for i in range(size - distance)])


def from_later(values, distance, size):
    return lax.ppermute(values, SEQ, [(i + distance, i) for i in range(size - distance)])


def reach_over(shift, local, keep, size, need):
    total = shift(local, 1, size).astype(F32)
    repeat = local.shape[0] // keep.shape[0]
    factor = shift(keep, 1, size)
    covered = 1
    while covered < min(need, size - 1):
        got = shift(total.astype(BF16), covered, size).astype(F32)
        total = total + jnp.repeat(factor, repeat)[:, None] * got
        if covered * 2 < min(need, size - 1):
            factor = factor * shift(factor, covered, size)
        covered *= 2
    return total


def body(
    residual,
    segment_ids,
    norm_in_gain,
    w_zx,
    w_bc,
    w_dt,
    conv_x_weight,
    conv_x_bias,
    conv_bc_weight,
    conv_bc_bias,
    dt_bias,
    a_log,
    d_skip,
    norm_gain,
    w_out,
    cotangent,
):
    own, width = residual.shape
    dp_size = lax.axis_size("dp")
    size = lax.axis_size(SEQ)
    place = lax.axis_index(SEQ)
    dp_rows, _, cols = w_zx.shape
    heads_own = w_dt.shape[1]
    inner = cols * size
    heads = heads_own * size
    state2 = w_bc.shape[1]
    state = state2 // 2
    bc_cols = state2 // size
    chunks = own // CHUNK
    head_width = inner // heads

    sizes = (dp_size // 2, lax.axis_size("head"), lax.axis_size("tensor"))
    core = lax.rem(lax.axis_index("dp"), 2)
    bc_own = lax.dynamic_slice_in_dim(w_bc, place * bc_cols, bc_cols, 1)
    side = bc_cols + heads_own
    side_rows = -(-side // 16) * 16
    side_part = jnp.pad(jnp.concatenate([bc_own, w_dt], 1).T, ((0, side_rows - side), (0, 0)))
    taps = conv_x_weight.shape[0]
    small_rows = [conv_x_weight, conv_x_bias[None], norm_gain[None]]
    head_rows = jnp.stack([dt_bias, a_log, d_skip])
    small = jnp.concatenate(small_rows + [jnp.pad(head_rows, ((0, 0), (0, cols - heads_own)))], 0)
    small = jnp.pad(small, ((0, 16 - small.shape[0]), (0, 0)))
    w_zo = lax.all_gather(jnp.stack([w_zx[:, 0], w_out]), ALL, axis=0, tiled=False)
    w_zo = w_zo.reshape(dp_size, size, 2, dp_rows, cols)
    side_full, w_x, small_full = gather_weights([side_part, w_zx[:, 1]], small, sizes)
    w_x = w_x.reshape(dp_size, size, dp_rows, cols)
    side_full = side_full.reshape(dp_size, size, side_rows, dp_rows)
    side_full = jnp.moveaxis(side_full[:, :, :side], 0, 2).reshape(size, side, width)
    w_b = side_full[:, :bc_cols].reshape(state2, width)
    w_d = side_full[:, bc_cols:].reshape(heads, width)
    small_full = jnp.moveaxis(small_full.reshape(size, 16, cols), 0, 1)
    per_channel = small_full.reshape(16, inner)
    x_taps, x_bias, out_gain = per_channel[:taps], per_channel[taps], per_channel[taps + 1]
    per_head = small_full[taps + 2 : taps + 5, :, :heads_own].reshape(3, heads)
    dt_shift, log_rate, skip = per_head[0], per_head[1], per_head[2]
    rate = -jnp.exp(log_rate)
    skip_wide = jnp.repeat(skip, head_width)

    seg_all = jnp.pad(segment_ids[0], (HALO, 0), constant_values=-1)
    seg_ext = lax.dynamic_slice_in_dim(seg_all, place * own, own + HALO)
    seg = seg_ext[HALO:]
    same = [
        (seg_ext[HALO - back : HALO - back + own] == seg).astype(F32)[:, None]
        for back in range(1, taps)
    ]
    seg_chunk = seg.reshape(chunks, CHUNK)
    end_chunk = seg_chunk[:, -1]
    end_before = jnp.concatenate([seg_ext[HALO - 1 : HALO], end_chunk[:-1]])
    lower = jnp.tril(jnp.ones((CHUNK, CHUNK), F32))
    mask_bias = jnp.where(
        (seg_chunk[:, :, None] == seg_chunk[:, None, :]) & (lower > 0), 0.0, MASKED
    )

    rows_ext = jnp.concatenate([from_earlier(residual[-HALO:], 1, size), residual], 0).astype(F32)
    inv_ext = lax.rsqrt(jnp.mean(rows_ext * rows_ext, axis=1, keepdims=True) + EPSILON)
    normed = (rows_ext * inv_ext * norm_in_gain).astype(BF16)
    normed_own = normed[HALO:]
    rows_in, inv_rms = rows_ext[HALO:], inv_ext[HALO:]
    bc_ext = dot16("td,kd->tk", normed, w_b)
    dt_raw = dot16("td,kd->tk", normed_own, w_d)
    bc_pre = conv_before(bc_ext, conv_bc_weight, conv_bc_bias, same)
    bc = rounded(jax.nn.silu(bc_pre))
    dt = jax.nn.softplus(dt_raw + dt_shift)

    scan = Scan(own, sizes, dp_rows, cols, heads_own, taps)
    dt_chunk = dt.reshape(chunks, CHUNK, heads)
    cum = jnp.einsum("lm,cmh->clh", lower, dt_chunk * rate, precision=HIGHEST)
    in_end = (seg_chunk == end_chunk[:, None]).astype(F32)[..., None]
    in_start = (seg_chunk == end_before[:, None]).astype(F32)[..., None]
    tail = (jnp.exp(cum[:, -1:] - cum) * in_end).reshape(own, heads)
    entry = (jnp.exp(cum) * in_start).reshape(own, heads)
    keep = jnp.exp(cum[:, -1]) * (end_before == end_chunk).astype(F32)[:, None]
    keep_local = jnp.prod(keep, axis=0)
    keep_cols = jnp.repeat(keep.T, head_width, axis=0)
    b_chunk = bc[:, :state].reshape(chunks, CHUNK, state)
    c_chunk = bc[:, state:].reshape(chunks, CHUNK, state)
    coupling = dot16("cls,cms->clm", c_chunk, b_chunk)
    cum_g = jnp.moveaxis(cum.reshape(own, scan.groups, scan.heads), 1, 0)
    cumt_g = jnp.moveaxis(cum_g, 1, 2)
    dt3, tail3, entry3 = thirds(dt), thirds(tail), thirds(entry)
    head_of = lax.broadcasted_iota(jnp.int32, (heads, inner), 1) // head_width
    widen = (head_of == lax.broadcasted_iota(jnp.int32, (heads, inner), 0)).astype(BF16)
    widen = jnp.concatenate([widen] * 3, 0)
    ones = (
        lax.broadcasted_iota(jnp.int32, (scan.wide, 128), 0) // head_width
        == lax.broadcasted_iota(jnp.int32, (scan.wide, 128), 1)
    ).astype(BF16)
    same_cols = jnp.pad(jnp.concatenate(same, 1), ((0, 0), (0, 8 - len(same))))
    conv_rows = jnp.concatenate([x_taps, x_bias[None]], 0)
    conv_rows = jnp.pad(conv_rows, ((0, 8 - conv_rows.shape[0]), (0, 0)))
    skip_rows, gain_row = skip_wide[None], out_gain[None]
    need = -(-(DOC_MOST - 1) // own)

    x_ext, x, within, added, local = scan.s1(
        normed, w_x, conv_rows, same_cols, dt3, tail3, widen, cum_g, cumt_g, coupling, mask_bias, bc, keep_cols
    )
    entering = reach_over(from_earlier, local, keep_local, size, need)
    z, y, states, squares = scan.s2(
        normed_own, w_zo, within, x, skip_rows, entry3, widen, bc, entering, added, keep_cols
    )
    gated_out, grad_gate, cross, gain_rows, block_out = scan.s3(
        y, z, squares, gain_row, w_zo, cotangent, residual
    )
    grad_norm_gain = gain_rows[0]
    low_z, dy, back_added, back_local, own_part = scan.s4(
        y, z, squares, cross, gain_row, grad_gate, w_zo, entry3, widen, bc, keep_cols
    )
    def as_left(v):
        return v.T.reshape(dp_size, dp_rows, v.shape[0])

    early = gradient_pieces(
        [as_left(normed_own), as_left(cotangent)], [low_z, gated_out], size
    )
    early = lax.psum_scatter(
        early.reshape((dp_size * size,) + early.shape[2:]), ALL, scatter_dimension=0, tiled=False
    ).astype(F32)
    leaving = reach_over(from_later, back_local, keep_local, size, need)
    low_x, conv_sums, head_sums, state_dots, dbc, dmix, through = scan.s5(
        dy, x_ext, within, conv_rows, skip_rows, same_cols, dt3, tail3, entry3, widen, ones, cum_g, cumt_g,
        coupling, mask_bias, bc, states, leaving, back_added, keep_cols, w_x
    )
    grad_taps, grad_bias = conv_sums[:taps], conv_sums[taps]
    grad_skip = jnp.sum(conv_sums[taps + 1].reshape(heads, head_width), axis=1)
    dbc = dbc + jnp.concatenate(
        [
            dot16("clm,cls->cms", dmix, c_chunk).reshape(own, state),
            dot16("clm,cms->cls", dmix, b_chunk).reshape(own, state),
        ],
        1,
    )
    head_sums = jnp.moveaxis(head_sums[..., : scan.heads], 0, 2).reshape(3, chunks, CHUNK, heads)
    falls, rises, direct = head_sums[0], head_sums[1], head_sums[2]
    state_dots = jnp.moveaxis(jnp.sum(state_dots, axis=3), 0, 1).reshape(chunks, heads)
    strict = lower - jnp.eye(CHUNK, dtype=F32)
    da = (
        jnp.einsum("lm,clh->cmh", lower, falls, precision=HIGHEST)
        + jnp.einsum("lm,cmh->clh", strict, rises, precision=HIGHEST)
        + (keep * state_dots)[:, None]
    )
    ddt = direct + rate * da
    grad_log = rate * jnp.sum(dt_chunk * da, axis=(0, 1))
    ddt_raw = ddt.reshape(own, heads) * jax.nn.sigmoid(dt_raw + dt_shift)
    grad_shift = jnp.sum(ddt_raw, axis=0)

    gbc, grad_bc_taps, grad_bc_bias = conv_back(
        dbc * silu_grad(bc_pre), bc_ext, conv_bc_weight, same
    )
    low_bc = gbc.astype(BF16)
    low_dt = ddt_raw.astype(BF16)

    own_part = own_part + dot16("tk,kd->td", low_dt, w_d)
    ext_part = through + dot16("tk,kd->td", low_bc, w_b)
    last = from_later(ext_part[:HALO], 1, size)
    grad_normed = own_part + ext_part[HALO:]
    grad_normed = grad_normed.at[own - HALO :].add(last)
    scaled_in = grad_normed * norm_in_gain
    input_grad = (
        cotangent.astype(F32)
        + inv_rms * scaled_in
        - rows_in * (inv_rms * inv_rms * inv_rms) * jnp.mean(scaled_in * rows_in, axis=1, keepdims=True)
    )
    grad_in_gain = jnp.sum(grad_normed * rows_in * inv_rms, axis=0)

    def to_pair(v):
        pairs = [(at, at ^ 1) for at in range(dp_size)]
        other = lax.ppermute(v, "dp", pairs)
        return jnp.where(core == 0, jnp.stack([v, other]), jnp.stack([other, v])).reshape(
            2 * v.shape[0], -1
        )

    def left_of(v):
        split_rows = v.T.reshape(dp_size // 2, 2, dp_rows, v.shape[0])
        return lax.dynamic_index_in_dim(split_rows, core, 1, keepdims=False)

    normed_pair = to_pair(normed)
    left_ext = left_of(normed_pair)
    low_side = jnp.concatenate(
        [
            low_bc.reshape(-1, size, bc_cols),
            jnp.pad(low_dt, ((HALO, 0), (0, 0))).reshape(-1, size, heads_own),
        ],
        2,
    )
    low_side = jnp.pad(low_side, ((0, 0), (0, 0), (0, side_rows - side))).reshape(-1, size * side_rows)
    side_pieces = dot16("tk,xdt->xkd", to_pair(low_side), left_ext).astype(BF16)
    x_pieces = gradient_pieces([left_ext], [to_pair(low_x)], size)
    grid = (dp_size // 2,) + sizes[1:]
    parts = [
        side_pieces.reshape(grid + (side_rows, dp_rows)),
        x_pieces.reshape(grid + (dp_rows, cols)),
    ]
    head_sum = jnp.stack([grad_shift, grad_log, grad_skip], 0).reshape(-1)
    row = jnp.concatenate([grad_in_gain, grad_bc_taps.reshape(-1), grad_bc_bias])
    small_sum = jnp.concatenate(
        [
            grad_taps,
            grad_bias[None],
            grad_norm_gain[None],
            jnp.pad(row, (0, inner - row.shape[0]))[None],
            jnp.pad(head_sum, (0, inner - head_sum.shape[0]))[None],
        ],
        0,
    )
    grad_side, grad_wx, small_sum = scatter_gradients(parts, small_sum, sizes)
    grad_wzx = jnp.stack([early[0], grad_wx], 1)
    grad_wo = early[1]
    grad_side = grad_side.reshape(size, side_rows, dp_rows)
    grad_wbc = grad_side[:, :bc_cols].reshape(state2, dp_rows).T
    grad_wdt = lax.dynamic_index_in_dim(grad_side, place, 0, keepdims=False)[bc_cols:side].T
    channel_own = lax.dynamic_slice_in_dim(small_sum[: taps + 2], place * cols, cols, 1)
    row = small_sum[taps + 2]
    gain_sum = row[:width]
    taps_sum = row[width : width + taps * state2].reshape(taps, state2)
    bias_sum = row[width + taps * state2 : width + (taps + 1) * state2]
    head_sum = small_sum[taps + 3, : 3 * heads].reshape(3, heads)
    head_own = lax.dynamic_slice_in_dim(head_sum, place * heads_own, heads_own, 1)
    return (
        block_out,
        input_grad,
        gain_sum,
        grad_wzx,
        grad_wbc,
        grad_wdt,
        channel_own[:taps],
        channel_own[taps],
        taps_sum,
        bias_sum,
        head_own[0],
        head_own[1],
        head_own[2],
        channel_own[taps + 1],
        grad_wo,
    )


def solution(mesh):
    rows = P(ALL, None)
    in_specs = (
        rows,
        P("dp", None),
        P(),
        P("dp", None, SEQ),
        P("dp", None),
        P("dp", SEQ),
        P(None, SEQ),
        P(SEQ),
        P(),
        P(),
        P(SEQ),
        P(SEQ),
        P(SEQ),
        P(SEQ),
        P("dp", SEQ),
        rows,
    )
    out_specs = (
        rows,
        rows,
        P(),
        P("dp", None, SEQ),
        P("dp", None),
        P("dp", SEQ),
        P(None, SEQ),
        P(SEQ),
        P(),
        P(),
        P(SEQ),
        P(SEQ),
        P(SEQ),
        P(SEQ),
        P("dp", SEQ),
    )
    return jax.shard_map(
        body, mesh=mesh, in_specs=in_specs, out_specs=out_specs, check_vma=False
    )
```

```python
import functools

import jax
import jax.numpy as jnp
from jax import lax
from jax.experimental import pallas as pl
from jax.experimental.pallas import tpu as pltpu
from jax.sharding import PartitionSpec as P

EPSILON = 1e-05
CHUNK = 128
HALO = 16
AHEAD = 2
LAGS = (0, 1, 3, 5)
CHUNK_ROWS = 48
MASKED = -1e30
HIGHEST = lax.Precision.HIGHEST
SEQ = ("head", "tensor")
ALL = ("dp", "head", "tensor")
BF16 = jnp.bfloat16
F32 = jnp.float32
MESH = pl.DeviceIdType.MESH
VMEM_BYTES = 56 << 20


def coordinates():
    dp = lax.axis_index("dp")
    return lax.div(dp, 2), lax.rem(dp, 2), lax.axis_index("head"), lax.axis_index("tensor")


def enter_kernel(x, core, head, tensor, xs, hs, ts, sibling):
    barrier = pltpu.get_barrier_semaphore()
    count = 0
    for step in range(1, hs):
        pl.semaphore_signal(barrier, 1, device_id={"head": lax.rem(head + step, hs)}, device_id_type=MESH)
        count += 1
    for step in range(1, ts):
        pl.semaphore_signal(barrier, 1, device_id={"tensor": lax.rem(tensor + step, ts)}, device_id_type=MESH)
        count += 1
    for step in range(1, xs):
        other = 2 * lax.rem(x + step, xs) + core
        pl.semaphore_signal(barrier, 1, device_id={"dp": other}, device_id_type=MESH)
        count += 1
    if sibling:
        pl.semaphore_signal(barrier, 1, device_id={"dp": 2 * x + 1 - core}, device_id_type=MESH)
        count += 1
    pl.semaphore_wait(barrier, count)


def gatherer(sizes, chunks, parts, fulls, sems):
    xs, hs, ts = sizes
    send, recv, own_sem = sems
    x, core, head, tensor = coordinates()
    dp = 2 * x + core
    total = len(chunks)
    ahead = 4

    def own():
        return [
            pltpu.make_async_copy(part, full.at[dp, head, tensor], own_sem.at[kind])
            for kind, (part, full) in enumerate(zip(parts, fulls))
        ]

    def copy(src, dst, index, slot, device):
        return pltpu.make_async_remote_copy(
            src_ref=src,
            dst_ref=dst,
            send_sem=send.at[index, slot],
            recv_sem=recv.at[index, slot],
            device_id=device,
            device_id_type=MESH,
        )

    def along_head(index):
        kind, start, length, _ = chunks[index]
        rows = pl.ds(start, length)
        return [
            copy(
                parts[kind].at[rows],
                fulls[kind].at[dp, head, tensor, rows],
                index,
                step - 1,
                {"head": lax.rem(head + step, hs)},
            )
            for step in range(1, hs)
        ]

    def over(index, axis, second):
        kind, start, length, _ = chunks[index]
        rows = pl.ds(start, length)
        base = hs - 1 if second else hs - 1 + max(xs, ts)
        copies = []
        if axis == "tensor":
            homes = [dp] if second else [2 * home + core for home in range(xs)]
            for step in range(1, ts):
                for home in homes:
                    view = fulls[kind].at[home, :, tensor, rows]
                    device = {"tensor": lax.rem(tensor + step, ts)}
                    copies.append(copy(view, view, index, base + len(copies), device))
        else:
            for step in range(1, xs):
                view = fulls[kind].at[dp, :, tensor, rows] if second else fulls[kind].at[dp, :, :, rows]
                device = {"dp": 2 * lax.rem(x + step, xs) + core}
                copies.append(copy(view, view, index, base + len(copies), device))
        return copies

    def to_sibling(index):
        kind, start, length, _ = chunks[index]
        rows = pl.ds(start, length)
        base = hs - 1 + max(xs, ts) + max(xs, xs * ts)
        return [
            copy(
                fulls[kind].at[2 * home + core, :, :, rows],
                fulls[kind].at[2 * home + core, :, :, rows],
                index,
                base + home,
                {"dp": 2 * x + 1 - core},
            )
            for home in range(xs)
        ]

    def stage(index, number):
        tensor_first = chunks[index][3]
        if number == 0:
            return along_head(index)
        if number == 1:
            return over(index, "tensor" if tensor_first else "x", True)
        if number == 2:
            return over(index, "x" if tensor_first else "tensor", False)
        return to_sibling(index)

    def start(first):
        if first:
            for one in own():
                one.start()
        else:
            for index in range(min(ahead, total)):
                for one in stage(index, 0):
                    one.start()
            for one in own():
                one.wait()

    def tick(at):
        for number in range(4):
            index = at - 2 * number
            if 0 <= index < total:
                for one in stage(index, number):
                    one.wait_recv()
                if number < 3:
                    for one in stage(index, number + 1):
                        one.start()
                if number == 0 and index + ahead < total:
                    for one in stage(index + ahead, 0):
                        one.start()

    def end():
        for index in range(total):
            for number in range(4):
                for one in stage(index, number):
                    one.wait_send()

    return start, tick, end, total + 6


def gatherer_scratch(sizes, chunks, kinds):
    xs, hs, ts = sizes
    slots = hs - 1 + max(xs, ts) + max(xs, xs * ts) + xs
    return [
        pltpu.SemaphoreType.DMA((len(chunks), slots)),
        pltpu.SemaphoreType.DMA((len(chunks), slots)),
        pltpu.SemaphoreType.DMA((kinds,)),
    ]


def gather_kernel(sizes, chunks, kinds, *refs):
    xs, hs, ts = sizes
    parts, small = refs[:kinds], refs[kinds]
    fulls, small_full = refs[kinds + 1 : 2 * kinds + 1], refs[2 * kinds + 1]
    sems, rest = refs[2 * kinds + 2 : 2 * kinds + 5], refs[2 * kinds + 5 :]
    small_send, small_recv, small_own = rest
    x, core, head, tensor = coordinates()
    begin, step_on, end, ticks = gatherer(sizes, chunks, parts, fulls, sems)
    begin(True)
    own_small = pltpu.make_async_copy(small, small_full.at[head, tensor], small_own.at[0])
    own_small.start()
    enter_kernel(x, core, head, tensor, xs, hs, ts, True)
    small_tensor = [
        pltpu.make_async_remote_copy(
            src_ref=small,
            dst_ref=small_full.at[head, tensor],
            send_sem=small_send.at[step - 1],
            recv_sem=small_recv.at[step - 1],
            device_id={"tensor": lax.rem(tensor + step, ts)},
            device_id_type=MESH,
        )
        for step in range(1, ts)
    ]
    small_head = [
        pltpu.make_async_remote_copy(
            src_ref=small_full.at[head],
            dst_ref=small_full.at[head],
            send_sem=small_send.at[ts + step - 2],
            recv_sem=small_recv.at[ts + step - 2],
            device_id={"head": lax.rem(head + step, hs)},
            device_id_type=MESH,
        )
        for step in range(1, hs)
    ]
    for one in small_tensor:
        one.start()
    begin(False)
    own_small.wait()
    for one in small_tensor:
        one.wait_recv()
    for one in small_head:
        one.start()
    for tick in range(ticks):
        step_on(tick)
    for one in small_head:
        one.wait_recv()
    for one in small_tensor + small_head:
        one.wait_send()
    end()


def row_chunks(rows, first, kinds, pieces):
    step = rows // pieces
    return [
        (kind, piece * step, step, piece % 2 == 1)
        for kind in range(first, kinds)
        for piece in range(pieces)
    ]


def gather_weights(parts, small, sizes):
    xs, hs, ts = sizes
    kinds = len(parts)
    count = parts[1].shape[0]
    chunks = [(0, 0, parts[0].shape[0], True)] + row_chunks(count, 1, kinds, count // CHUNK_ROWS)
    full = [jax.ShapeDtypeStruct((2 * xs, hs, ts) + part.shape, part.dtype) for part in parts]
    full.append(jax.ShapeDtypeStruct((hs, ts) + small.shape, small.dtype))
    anywhere = pl.BlockSpec(memory_space=pl.ANY)
    return pl.pallas_call(
        functools.partial(gather_kernel, sizes, chunks, kinds),
        out_shape=full,
        in_specs=[anywhere] * (kinds + 1),
        out_specs=[anywhere] * (kinds + 1),
        scratch_shapes=gatherer_scratch(sizes, chunks, kinds)
        + [
            pltpu.SemaphoreType.DMA((hs + ts,)),
            pltpu.SemaphoreType.DMA((hs + ts,)),
            pltpu.SemaphoreType.DMA((1,)),
        ],
        compiler_params=pltpu.CompilerParams(
            collective_id=0, has_side_effects=True, vmem_limit_bytes=VMEM_BYTES
        ),
        cost_estimate=busy(60),
    )(*parts, small)


def reducer(sizes, chunks, parts, bufs, sems, put):
    xs, hs, ts = sizes
    send, recv, own_sem = sems
    x, core, head, tensor = coordinates()
    total = len(chunks)

    def loads(index):
        kind, start, length, _ = chunks[index]
        rows = pl.ds(start, length)
        return [
            pltpu.make_async_copy(
                parts[kind].at[2 * home + core, :, :, rows],
                bufs[5 * index].at[home],
                own_sem.at[index, home],
            )
            for home in range(xs)
        ]

    def stage(index, number):
        kind, start, length, x_first = chunks[index]
        rows = pl.ds(start, length)
        held = bufs[5 * index]
        into = bufs[5 * index + 1 + number]
        slots = (0, xs, xs + max(xs, ts) - 1, xs + 2 * (max(xs, ts) - 1))
        by_x = [
            (lax.rem(x + step, xs), {"dp": 2 * lax.rem(x + step, xs) + core}) for step in range(1, xs)
        ]
        by_tensor = [
            (lax.rem(tensor + step, ts), {"tensor": lax.rem(tensor + step, ts)}) for step in range(1, ts)
        ]
        if number == 0:
            moves = [
                (parts[kind].at[2 * home + 1 - core, :, :, rows], into.at[home], {"dp": 2 * x + 1 - core})
                for home in range(xs)
            ]
        elif number == 1 and x_first:
            moves = [(held.at[to], into.at[at], device) for at, (to, device) in enumerate(by_x)]
        elif number == 1:
            moves = [(held.at[:, :, to], into.at[at], device) for at, (to, device) in enumerate(by_tensor)]
        elif number == 2 and x_first:
            moves = [(held.at[x, :, to], into.at[at], device) for at, (to, device) in enumerate(by_tensor)]
        elif number == 2:
            moves = [(held.at[to, :, tensor], into.at[at], device) for at, (to, device) in enumerate(by_x)]
        else:
            moves = []
            for step in range(1, hs):
                to = lax.rem(head + step, hs)
                moves.append((held.at[x, to, tensor], into.at[step - 1], {"head": to}))
        return [
            pltpu.make_async_remote_copy(
                src_ref=src,
                dst_ref=dst,
                send_sem=send.at[index, slots[number] + at],
                recv_sem=recv.at[index, slots[number] + at],
                device_id=device,
                device_id_type=MESH,
            )
            for at, (src, dst, device) in enumerate(moves)
        ]

    def add(index, number):
        kind, start, length, x_first = chunks[index]
        held = bufs[5 * index]
        into = bufs[5 * index + 1 + number]
        if number == 0:

            @pl.loop(0, xs * hs)
            def _(both):
                one, two = lax.div(both, hs), lax.rem(both, hs)
                value = held[one, two].astype(F32) + into[one, two].astype(F32)
                held[one, two] = value.astype(BF16)

        elif number == 1 and x_first:

            @pl.loop(0, hs)
            def _(one):
                value = held[x, one].astype(F32)
                for step in range(xs - 1):
                    value = value + into[step, one].astype(F32)
                held[x, one] = value.astype(BF16)

        elif number == 1:

            @pl.loop(0, xs * hs)
            def _(both):
                one, two = lax.div(both, hs), lax.rem(both, hs)
                value = held[one, two, tensor].astype(F32)
                for step in range(ts - 1):
                    value = value + into[step, one, two].astype(F32)
                held[one, two, tensor] = value.astype(BF16)

        elif number == 2:

            @pl.loop(0, hs)
            def _(one):
                value = held[x, one, tensor].astype(F32)
                for step in range(into.shape[0]):
                    value = value + into[step, one].astype(F32)
                held[x, one, tensor] = value.astype(BF16)

        else:
            value = held[x, head, tensor].astype(F32)
            for step in range(hs - 1):
                value = value + into[step].astype(F32)
            put(kind, start, length, value)

    def start(first):
        for index in range(total):
            if first:
                for one in loads(index):
                    one.start()
            elif index < AHEAD:
                for one in stage(index, 0):
                    one.start()

    def tick(at):
        for number, lag in enumerate(LAGS):
            index = at - lag
            if 0 <= index < total:
                for one in stage(index, number):
                    one.wait_recv()
                if number == 0:
                    if index + AHEAD < total:
                        for one in stage(index + AHEAD, 0):
                            one.start()
                    for one in loads(index):
                        one.wait()
                add(index, number)
                if number < 3:
                    for one in stage(index, number + 1):
                        one.start()

    def end():
        for index in range(total):
            for number in range(4):
                for one in stage(index, number):
                    one.wait_send()

    return start, tick, end, total + LAGS[3]


def reducer_scratch(sizes, chunks, parts):
    xs, hs, ts = sizes
    scratch = []
    for kind, _, length, x_first in chunks:
        block = (length, parts[kind].shape[4])
        kept = (hs, ts) if x_first else (xs, hs)
        near, far = (xs, ts) if x_first else (ts, xs)
        scratch += [
            pltpu.VMEM((xs, hs, ts) + block, BF16),
            pltpu.VMEM((xs, hs, ts) + block, BF16),
            pltpu.VMEM((near - 1,) + kept + block, BF16),
            pltpu.VMEM((far - 1, hs) + block, BF16),
            pltpu.VMEM((hs - 1,) + block, BF16),
        ]
    slots = xs + 2 * (max(xs, ts) - 1) + hs - 1
    return scratch + [
        pltpu.SemaphoreType.DMA((len(chunks), slots)),
        pltpu.SemaphoreType.DMA((len(chunks), slots)),
        pltpu.SemaphoreType.DMA((len(chunks), xs)),
    ]


def scatter_kernel(sizes, chunks, kinds, *refs):
    xs, hs, ts = sizes
    parts, small = refs[:kinds], refs[kinds]
    outs, small_out = refs[kinds + 1 : 2 * kinds + 1], refs[2 * kinds + 1]
    rest = refs[2 * kinds + 2 :]
    count = 5 * len(chunks)
    bufs, sems, rest = rest[:count], rest[count : count + 3], rest[count + 3 :]
    small_acc, small_in, small_send, small_recv, side_send, side_recv = rest
    x, core, head, tensor = coordinates()

    def put(kind, start, length, value):
        if kind == 0:
            outs[kind][head, tensor] = value.astype(BF16)
        else:
            outs[kind][start : start + length, :] = value

    begin, step_on, end, ticks = reducer(sizes, chunks, parts, bufs, sems, put)

    def side_copy(view, slot, device):
        return pltpu.make_async_remote_copy(
            src_ref=view,
            dst_ref=view,
            send_sem=side_send.at[slot],
            recv_sem=side_recv.at[slot],
            device_id=device,
            device_id_type=MESH,
        )

    side_tensor = [
        side_copy(outs[0].at[head, tensor], step - 1, {"tensor": lax.rem(tensor + step, ts)})
        for step in range(1, ts)
    ]
    side_head = [
        side_copy(outs[0].at[head], ts + step - 2, {"head": lax.rem(head + step, hs)})
        for step in range(1, hs)
    ]
    small_slots = [1, xs - 1, ts - 1, hs - 1]
    small_base = [0, 1, xs, xs + ts - 1]

    def small_stage(number):
        copies = []
        for step in range(1, small_slots[number] + 1):
            slot = small_base[number] + step - 1
            device = (
                {"dp": 2 * x + 1 - core},
                {"dp": 2 * lax.rem(x + step, xs) + core},
                {"tensor": lax.rem(tensor + step, ts)},
                {"head": lax.rem(head + step, hs)},
            )[number]
            copies.append(
                pltpu.make_async_remote_copy(
                    src_ref=small if number == 0 else small_acc.at[number - 1],
                    dst_ref=small_in.at[slot],
                    send_sem=small_send.at[slot],
                    recv_sem=small_recv.at[slot],
                    device_id=device,
                    device_id_type=MESH,
                )
            )
        return copies

    def small_add(number):
        mine = small[...] if number == 0 else small_acc[number - 1]
        size = small_slots[number] + 1
        place = (core, x, tensor, head)[number]
        value = None
        for at in range(size):
            step = lax.rem(place - at + size, size)
            slot = small_base[number] + jnp.maximum(step - 1, 0)
            here = jnp.where(step == 0, mine, small_in[slot])
            value = here if value is None else value + here
        if number < 3:
            small_acc[number] = value
        else:
            small_out[...] = value

    begin(True)
    enter_kernel(x, core, head, tensor, xs, hs, ts, True)
    for one in small_stage(0):
        one.start()
    begin(False)
    for tick in range(max(ticks, 9)):
        step_on(tick)
        if tick == 5:
            for one in side_tensor:
                one.start()
        if tick == 7:
            for one in side_tensor:
                one.wait_recv()
            for one in side_head:
                one.start()
        if tick in (0, 2, 4, 6):
            number = tick // 2
            for one in small_stage(number):
                one.wait_recv()
            small_add(number)
            if number < 3:
                for one in small_stage(number + 1):
                    one.start()
    for one in side_head:
        one.wait_recv()
    for one in side_tensor + side_head:
        one.wait_send()
    for number in range(4):
        for one in small_stage(number):
            one.wait_send()
    end()


def scatter_gradients(parts, small, sizes):
    xs, hs, ts = sizes
    kinds = len(parts)
    count = parts[1].shape[3]
    chunks = [(0, 0, parts[0].shape[3], True)] + row_chunks(count, 1, kinds, count // CHUNK_ROWS)
    small_slots = xs + ts + hs - 2
    anywhere = pl.BlockSpec(memory_space=pl.ANY)
    whole = pl.BlockSpec(memory_space=pltpu.VMEM)
    return pl.pallas_call(
        functools.partial(scatter_kernel, sizes, chunks, kinds),
        out_shape=[jax.ShapeDtypeStruct((hs, ts) + parts[0].shape[3:], BF16)]
        + [jax.ShapeDtypeStruct(part.shape[3:], F32) for part in parts[1:]]
        + [jax.ShapeDtypeStruct(small.shape, F32)],
        in_specs=[anywhere] * kinds + [whole],
        out_specs=[whole] * (kinds + 1),
        scratch_shapes=reducer_scratch(sizes, chunks, parts)
        + [
            pltpu.VMEM((3,) + small.shape, F32),
            pltpu.VMEM((small_slots,) + small.shape, F32),
            pltpu.SemaphoreType.DMA((small_slots,)),
            pltpu.SemaphoreType.DMA((small_slots,)),
            pltpu.SemaphoreType.DMA((hs + ts,)),
            pltpu.SemaphoreType.DMA((hs + ts,)),
        ],
        compiler_params=pltpu.CompilerParams(
            collective_id=1, has_side_effects=True, vmem_limit_bytes=VMEM_BYTES
        ),
        cost_estimate=busy(60),
    )(*parts, small)


def exchange_kernel(sizes, forward, chunks, *refs):
    xs, hs, ts = sizes
    size = hs * ts
    hosts = bool(chunks)
    local, keep = refs[:2]
    parts, out = refs[2 : 2 + hosts], refs[2 + hosts]
    outs, rest = refs[3 + hosts : 3 + 2 * hosts], refs[3 + 2 * hosts :]
    got, keeps, sums, sems, keep_sems, back_sems = rest[:6]
    x, core, head, tensor = coordinates()
    me = head * ts + tensor

    def put(kind, start, length, value):
        outs[kind][start : start + length, :] = value

    ticks = 0
    if hosts:
        begin, step_on, end, ticks = reducer(sizes, chunks, parts, rest[6:-3], rest[-3:], put)
        begin(True)
    barrier = pltpu.get_barrier_semaphore()
    peers = []
    for step in range(1, size):
        to = lax.rem(me + step, size)
        peers.append((to, {"head": lax.div(to, ts), "tensor": lax.rem(to, ts)}))
    others = [device for _, device in peers]
    if hosts:
        others += [{"dp": 2 * lax.rem(x + step, xs) + core} for step in range(1, xs)]
        others.append({"dp": 2 * x + 1 - core})
    for device in others:
        pl.semaphore_signal(barrier, 1, device_id=device, device_id_type=MESH)
    pl.semaphore_wait(barrier, len(others))

    def copies(src, dst, pair):
        return [
            pltpu.make_async_remote_copy(
                src_ref=src.at[to],
                dst_ref=dst.at[me],
                send_sem=pair.at[0, at],
                recv_sem=pair.at[1, at],
                device_id=device,
                device_id_type=MESH,
            )
            for at, (to, device) in enumerate(peers)
        ]

    factors = copies(keep, keeps, keep_sems)
    states = copies(local, got, sems)
    for one in factors + states:
        one.start()
    if hosts:
        begin(False)
    got[me] = local[me]
    keeps[me] = keep[me]
    for tick in range(min(3, ticks)):
        step_on(tick)
    for one in factors + states:
        one.wait_recv()
    third = lax.broadcasted_iota(jnp.int32, (keep.shape[1], local.shape[2]), 0) < 3
    third = third.astype(BF16)
    held = jnp.zeros(local.shape[1:], F32)
    order = range(size) if forward else range(size - 1, -1, -1)
    for at in order:
        sums[at] = held.astype(BF16)
        held = got[at].astype(F32) + dot_tn(keeps[at], third) * held
    back = copies(sums, out, back_sems)
    for one in back:
        one.start()
    out[me] = sums[me]
    for tick in range(3, ticks):
        step_on(tick)
    for one in back:
        one.wait_recv()
    for one in factors + states + back:
        one.wait_send()
    if hosts:
        end()


def exchange_states(local, keep, sizes, forward, parts=()):
    _, hs, ts = sizes
    size = hs * ts
    inner, state = local.shape
    blocks = (size, inner // size, state)
    whole = pl.BlockSpec(memory_space=pltpu.VMEM)
    anywhere = pl.BlockSpec(memory_space=pl.ANY)
    pair = pltpu.SemaphoreType.DMA((2, size))
    chunks, scratch = [], []
    if parts:
        count = parts[0].shape[3]
        chunks = row_chunks(count, 0, 1, count // CHUNK_ROWS)
        scratch = reducer_scratch(sizes, chunks, parts)
    out = pl.pallas_call(
        functools.partial(exchange_kernel, sizes, forward, chunks),
        out_shape=[jax.ShapeDtypeStruct(blocks, BF16)]
        + [jax.ShapeDtypeStruct(part.shape[3:], F32) for part in parts],
        in_specs=[whole, whole] + [anywhere] * len(parts),
        out_specs=[whole] * (1 + len(parts)),
        scratch_shapes=[
            pltpu.VMEM(blocks, BF16),
            pltpu.VMEM(keep.shape, BF16),
            pltpu.VMEM(blocks, BF16),
            pair,
            pair,
            pair,
        ]
        + scratch,
        compiler_params=pltpu.CompilerParams(
            collective_id=2 if forward else 3, has_side_effects=True, vmem_limit_bytes=VMEM_BYTES
        ),
        cost_estimate=busy(60),
    )(local.reshape(blocks), keep, *parts)
    return (out[0].reshape(inner, state),) + tuple(out[1:])


def group_of(cols):
    return 1 if cols % 128 == 0 else 128 // cols if 128 % cols == 0 else 2


def busy(microseconds):
    return pl.CostEstimate(flops=microseconds * 900_000_000, bytes_accessed=0, transcendentals=0)


def local_params():
    return pltpu.CompilerParams(vmem_limit_bytes=VMEM_BYTES)


def silu_of(v):
    return v * jax.nn.sigmoid(v)


def dot_nt(left, right):
    return lax.dot_general(left, right, (((1,), (1,)), ((), ())), preferred_element_type=F32)


def dot_tn(left, right):
    return lax.dot_general(left, right, (((0,), (0,)), ((), ())), preferred_element_type=F32)


def dot_nn(left, right):
    return jnp.dot(left, right, preferred_element_type=F32)


def dot_exact(left, right):
    return jnp.dot(left, right, preferred_element_type=F32, precision=HIGHEST)


def thirds(v):
    high = v.astype(BF16)
    rest = v - high.astype(F32)
    middle = rest.astype(BF16)
    return high, middle, (rest - middle.astype(F32)).astype(BF16)


def places(shape):
    return lax.broadcasted_iota(jnp.int32, shape, 0), lax.broadcasted_iota(jnp.int32, shape, 1)


def one_hot(hit):
    return hit.astype(F32).astype(BF16)


def conv_pre(ext_ref, taps_ref, same_ref, own, width):
    total = taps_ref[width : width + 1] + taps_ref[width - 1 : width] * ext_ref[HALO:]
    for back in range(1, width):
        total = total + (
            taps_ref[width - 1 - back : width - back]
            * ext_ref[HALO - back : HALO - back + own]
            * same_ref[:, back - 1 : back]
        )
    return total


def lane_masks():
    lane = lax.broadcasted_iota(jnp.int32, (1, 128), 1)
    first = (lane < 64).astype(F32)
    return first, 1.0 - first


def two_apart(pair, masks):
    return jnp.concatenate([pair * masks[0].astype(BF16), pair * masks[1].astype(BF16)], 0)


def decay_pair(cum_ref, cumt_ref, bias, rows, pair):
    parts = []
    for head in (2 * pair, 2 * pair + 1):
        spread = cum_ref[0, rows, head : head + 1] - cumt_ref[0, head : head + 1, rows] + bias
        parts.append(jnp.exp(spread))
    return parts


class Scan:
    def __init__(self, own, sizes, rows, cols, heads_own, taps):
        self.own, self.ext, self.taps = own, own + HALO, taps
        self.dps, self.hts = 2 * sizes[0], sizes[1] * sizes[2]
        self.rows, self.cols = rows, cols
        self.group = group_of(cols)
        self.wide = self.group * cols
        self.heads = self.group * heads_own
        self.groups = self.hts // self.group
        self.chunks = own // CHUNK
        self.width = self.dps * rows
        self.inner = self.hts * cols
        self.pairs = self.wide // 128

    def call(self, kernel, ins, outs, scratch=()):
        arrays = [array for array, _ in ins]
        return pl.pallas_call(
            kernel,
            grid=(self.groups,),
            out_shape=[shape for shape, _ in outs],
            in_specs=[spec for _, spec in ins],
            out_specs=[spec for _, spec in outs],
            scratch_shapes=list(scratch),
            compiler_params=local_params(),
            cost_estimate=busy(22),
        )(*arrays)

    def full(self, array):
        return (array, pl.BlockSpec(array.shape, lambda j: (0,) * array.ndim))

    def pieces(self, array):
        block = (self.dps, self.group, self.rows, self.cols)
        return (array, pl.BlockSpec(block, lambda j: (0, j, 0, 0)))

    def lanes(self, array):
        lead = array.shape[:-1]
        return (array, pl.BlockSpec(lead + (self.wide,), lambda j: (0,) * len(lead) + (j,)))

    def states(self, array):
        lead = array.shape[:-2]
        block = lead + (self.wide, array.shape[-1])
        return (array, pl.BlockSpec(block, lambda j: (0,) * len(lead) + (j, 0)))

    def grouped(self, array):
        block = (1,) + array.shape[1:]
        return (array, pl.BlockSpec(block, lambda j: (j,) + (0,) * (array.ndim - 1)))

    def project(self, rows_ref, piece_ref, out_ref):
        for one in range(self.group):
            weights = piece_ref[:, one].reshape(self.width, self.cols)
            out_ref[:, one * self.cols : (one + 1) * self.cols] = dot_nn(rows_ref, weights)

    def project_back(self, value_ref, piece_ref, out_ref):
        @pl.when(pl.program_id(0) == 0)
        def _():
            out_ref[...] = jnp.zeros_like(out_ref)

        for one in range(self.group):
            weights = piece_ref[:, one].reshape(self.width, self.cols)
            out_ref[...] += dot_nt(value_ref[:, one * self.cols : (one + 1) * self.cols], weights)

    def chunk_rows(self, c):
        return slice(c * CHUNK, (c + 1) * CHUNK)

    def lane_sums(self, v):
        total = v[:, :128]
        for pair in range(1, self.pairs):
            total = total + v[:, pair * 128 : (pair + 1) * 128]
        return total

    def widen(self):
        count = self.heads * self.groups
        row, lane = places((3 * count, self.wide))
        row = row - jnp.where(row >= 2 * count, 2 * count, jnp.where(row >= count, count, 0))
        return one_hot(row == pl.program_id(0) * self.heads + lax.div(lane, 64))

    def heads_of(self):
        row, lane = places((self.wide, 128))
        return one_hot(lane == pl.program_id(0) * self.heads + lax.div(row, 64))

    def keep_columns(self, keep_ref, widen):
        return dot_tn(widen, keep_ref[...])

    def halves(self, v):
        high = v.astype(BF16)
        return high, (v - high.astype(F32)).astype(BF16)

    def head_sums(self, v, heads_of):
        high, low = self.halves(v)
        return dot_nn(high, heads_of) + dot_nn(low, heads_of)

    def gradient(self, left_ref, value_ref, out_ref):
        for at in range(self.dps):
            for one in range(self.group):
                value = value_ref[:, one * self.cols : (one + 1) * self.cols]
                out_ref[at, one] = dot_nn(left_ref[at], value).astype(BF16)

    def piece_shape(self):
        return jax.ShapeDtypeStruct((self.dps, self.hts, self.rows, self.cols), BF16)

    def s1(self, normed, w_x, conv_rows, same, dt3, tail3, cum_g, cumt_g, coupling, bias, bc, keep3):
        own, state = self.own, bc.shape[1] // 2

        def kernel(
            normed_ref, w_ref, conv_ref, same_ref, dt_ref, tail_ref, cum_ref, cumt_ref,
            coupling_ref, bias_ref, bc_ref, keep_ref, ext_ref, x_ref, within_ref, added_ref, local_ref, xd_ref, xt_ref,
        ):
            self.project(normed_ref[...], w_ref, ext_ref)
            widen = self.widen()
            keep = self.keep_columns(keep_ref, widen)
            x = silu_of(conv_pre(ext_ref, conv_ref, same_ref, own, self.taps))
            x_ref[...] = x
            xd = x * dot_nn(dt_ref[...], widen)
            xd_ref[...] = xd.astype(BF16)
            xt_ref[...] = (xd * dot_nn(tail_ref[...], widen)).astype(BF16)
            masks = lane_masks()
            held = None
            for c in range(self.chunks):
                rows = self.chunk_rows(c)
                for pair in range(self.pairs):
                    lanes = slice(pair * 128, (pair + 1) * 128)
                    first, second = decay_pair(cum_ref, cumt_ref, bias_ref[c], rows, pair)
                    mix = coupling_ref[c]
                    kernel16 = jnp.concatenate([(first * mix).astype(BF16), (second * mix).astype(BF16)], 1)
                    within_ref[rows, lanes] = dot_nn(kernel16, two_apart(xd_ref[rows, lanes], masks))
                added = dot_tn(xt_ref[rows], bc_ref[rows, :state])
                added_ref[c] = added
                held = added if held is None else added + keep[:, c : c + 1] * held
            local_ref[...] = held.astype(BF16)

        f = jax.ShapeDtypeStruct
        return self.call(
            kernel,
            [
                self.full(normed), self.pieces(w_x), self.lanes(conv_rows), self.full(same), self.full(dt3),
                self.full(tail3), self.grouped(cum_g), self.grouped(cumt_g),
                self.full(coupling), self.full(bias), self.full(bc), self.full(keep3),
            ],
            [
                self.lanes(f((self.ext, self.inner), F32)), self.lanes(f((own, self.inner), F32)),
                self.lanes(f((own, self.inner), F32)), self.states(f((self.chunks, self.inner, state), F32)),
                self.states(f((self.inner, state), BF16)),
            ],
            [pltpu.VMEM((own, self.wide), BF16), pltpu.VMEM((own, self.wide), BF16)],
        )

    def s2(self, normed_own, w_z, within, x, skip_rows, entry3, bc, entering, added, keep3):
        own, state = self.own, bc.shape[1] // 2

        def kernel(
            normed_ref, w_ref, within_ref, x_ref, skip_ref, entry_ref, bc_ref, entering_ref,
            added_ref, keep_ref, z_ref, y_ref, states_ref, squares_ref,
        ):
            self.project(normed_ref[...], w_ref, z_ref)
            widen = self.widen()
            keep = self.keep_columns(keep_ref, widen)
            entry = dot_nn(entry_ref[...], widen)
            held = entering_ref[...].astype(F32)
            for c in range(self.chunks):
                rows = self.chunk_rows(c)
                held16 = held.astype(BF16)
                states_ref[c] = held16
                carried = dot_nt(bc_ref[rows, state:], held16)
                y_ref[rows] = within_ref[rows] + carried * entry[rows] + skip_ref[...] * x_ref[rows]
                if c + 1 < self.chunks:
                    held = added_ref[c] + keep[:, c : c + 1] * held
            gated = y_ref[...] * silu_of(z_ref[...])
            squares = self.lane_sums(gated * gated)

            @pl.when(pl.program_id(0) == 0)
            def _():
                squares_ref[...] = squares

            @pl.when(pl.program_id(0) > 0)
            def _():
                squares_ref[...] += squares

        f = jax.ShapeDtypeStruct
        return self.call(
            kernel,
            [
                self.full(normed_own), self.pieces(w_z), self.lanes(within), self.lanes(x), self.lanes(skip_rows),
                self.full(entry3), self.full(bc), self.states(entering), self.states(added),
                self.full(keep3),
            ],
            [
                self.lanes(f((own, self.inner), F32)), self.lanes(f((own, self.inner), F32)),
                self.states(f((self.chunks, self.inner, state), BF16)), self.full(f((own, 128), F32)),
            ],
        )

    def inv_gate(self, squares_ref):
        return lax.rsqrt(jnp.sum(squares_ref[...], axis=1, keepdims=True) / self.inner + EPSILON)

    def s3(self, y, z, squares, gain_row, w_o, cotangent, residual, cot_left):
        own = self.own

        def kernel(
            y_ref, z_ref, squares_ref, gain_ref, w_ref, cot_ref, residual_ref, left_ref,
            grad_ref, cross_ref, gain_grad_ref, out_ref, pieces_ref, gated_ref, sum_ref,
        ):
            inv = self.inv_gate(squares_ref)
            gated = y_ref[...] * silu_of(z_ref[...])
            normal = gated * inv
            gated_ref[...] = (normal * gain_ref[...]).astype(BF16)
            self.project_back(gated_ref, w_ref, sum_ref)
            self.gradient(left_ref, gated_ref, pieces_ref)
            self.project(cot_ref[...], w_ref, grad_ref)
            grad = grad_ref[...]
            gain_grad_ref[...] = jnp.broadcast_to(
                jnp.sum(grad * normal, axis=0, keepdims=True), gain_grad_ref.shape
            )
            cross = self.lane_sums(grad * gain_ref[...] * gated)

            @pl.when(pl.program_id(0) == 0)
            def _():
                cross_ref[...] = cross

            @pl.when(pl.program_id(0) > 0)
            def _():
                cross_ref[...] += cross

            @pl.when(pl.program_id(0) == self.groups - 1)
            def _():
                out_ref[...] = (residual_ref[...].astype(F32) + sum_ref[...]).astype(BF16)

        f = jax.ShapeDtypeStruct
        return self.call(
            kernel,
            [
                self.lanes(y), self.lanes(z), self.full(squares), self.lanes(gain_row), self.pieces(w_o),
                self.full(cotangent), self.full(residual), self.full(cot_left),
            ],
            [
                self.lanes(f((own, self.inner), F32)), self.full(f((own, 128), F32)),
                self.lanes(f((8, self.inner), F32)), self.full(f((own, self.width), BF16)),
                self.pieces(self.piece_shape()),
            ],
            [pltpu.VMEM((own, self.wide), BF16), pltpu.VMEM((own, self.width), F32)],
        )

    def s4(self, y, z, squares, cross, gain_row, grad_gate, w_z, entry3, bc, keep3, left):
        own, state = self.own, bc.shape[1] // 2

        def kernel(
            y_ref, z_ref, squares_ref, cross_ref, gain_ref, grad_ref, w_ref, entry_ref, bc_ref,
            keep_ref, left_ref, dy_ref, back_ref, local_ref, through_ref, pieces_ref, low_ref, dye_ref,
        ):
            inv = self.inv_gate(squares_ref)
            cross_mean = jnp.sum(cross_ref[...], axis=1, keepdims=True) / self.inner
            z = z_ref[...]
            gate = jax.nn.sigmoid(z)
            z_gate = z * gate
            y = y_ref[...]
            grad_gated = inv * (grad_ref[...] * gain_ref[...]) - (y * z_gate) * (inv * inv * inv * cross_mean)
            dy = grad_gated * z_gate
            dy_ref[...] = dy
            low_ref[...] = (grad_gated * y * (gate * (1.0 + z * (1.0 - gate)))).astype(BF16)
            self.project_back(low_ref, w_ref, through_ref)
            self.gradient(left_ref, low_ref, pieces_ref)
            widen = self.widen()
            keep = self.keep_columns(keep_ref, widen)
            dye_ref[...] = (dy * dot_nn(entry_ref[...], widen)).astype(BF16)
            held = None
            for c in range(self.chunks - 1, -1, -1):
                rows = self.chunk_rows(c)
                added = dot_tn(dye_ref[rows], bc_ref[rows, state:])
                back_ref[c] = added
                held = added if held is None else added + keep[:, c : c + 1] * held
            local_ref[...] = held.astype(BF16)

        f = jax.ShapeDtypeStruct
        return self.call(
            kernel,
            [
                self.lanes(y), self.lanes(z), self.full(squares), self.full(cross), self.lanes(gain_row),
                self.lanes(grad_gate), self.pieces(w_z), self.full(entry3), self.full(bc),
                self.full(keep3), self.full(left),
            ],
            [
                self.lanes(f((own, self.inner), F32)),
                self.states(f((self.chunks, self.inner, state), F32)), self.states(f((self.inner, state), BF16)),
                self.full(f((own, self.width), F32)), self.pieces(self.piece_shape()),
            ],
            [pltpu.VMEM((own, self.wide), BF16), pltpu.VMEM((own, self.wide), BF16)],
        )

    def s5(
        self, dy, x_ext, within, conv_rows, skip_rows, same, dt3, tail3, entry3, cum_g, cumt_g, coupling,
        bias, bc, states, leaving, back_added, keep3, w_x, left,
    ):
        own, state = self.own, bc.shape[1] // 2
        taps = self.taps

        def kernel(
            dy_ref, ext_ref, within_ref, conv_ref, skip_ref, same_ref, dt_ref, tail_ref, entry_ref,
            cum_ref, cumt_ref, coupling_ref, bias_ref, bc_ref, states_ref, leaving_ref, back_ref, keep_ref,
            w_ref, left_ref, rows_ref, head_ref, dots_ref, dbc_ref, dmix_ref, through_ref, pieces_ref,
            low_ref, xd_ref, xt_ref, dy16_ref, dye_ref, dxd_ref, shift_ref,
        ):
            first_step = pl.program_id(0) == 0

            @pl.when(first_step)
            def _():
                dbc_ref[...] = jnp.zeros_like(dbc_ref)
                dmix_ref[...] = jnp.zeros_like(dmix_ref)
                head_ref[...] = jnp.zeros_like(head_ref)
                dots_ref[...] = jnp.zeros_like(dots_ref)

            widen, heads_of = self.widen(), self.heads_of()
            keep = self.keep_columns(keep_ref, widen)
            pre = conv_pre(ext_ref, conv_ref, same_ref, own, taps)
            gate = jax.nn.sigmoid(pre)
            x = pre * gate
            dt = dot_nn(dt_ref[...], widen)
            tail = dot_nn(tail_ref[...], widen)
            xd = x * dt
            xd_ref[...] = xd.astype(BF16)
            xt_ref[...] = (xd * tail).astype(BF16)
            dy = dy_ref[...]
            dy16_ref[...] = dy.astype(BF16)
            entry = dot_nn(entry_ref[...], widen)
            dye_ref[...] = (dy * entry).astype(BF16)
            masks = lane_masks()
            held = leaving_ref[...].astype(F32)
            for c in range(self.chunks - 1, -1, -1):
                rows = self.chunk_rows(c)
                held16 = held.astype(BF16)
                into16 = states_ref[c]
                product = held * into16.astype(F32)
                high, low = self.halves(product)
                dots_ref[c] += dot_tn(high, heads_of) + dot_tn(low, heads_of)
                spread_back = dot_nt(bc_ref[rows, :state], held16)
                dmix = dmix_ref[c]
                for pair in range(self.pairs):
                    lanes = slice(pair * 128, (pair + 1) * 128)
                    first, second = decay_pair(cum_ref, cumt_ref, bias_ref[c], rows, pair)
                    mix = coupling_ref[c]
                    kernel16 = jnp.concatenate([(first * mix).astype(BF16), (second * mix).astype(BF16)], 1)
                    dy_pair = dy16_ref[rows, lanes]
                    both = dot_tn(kernel16, dy_pair)
                    dxd_ref[rows, lanes] = both[:CHUNK] * masks[0] + both[CHUNK:] * masks[1]
                    dkernel = dot_nt(dy_pair, two_apart(xd_ref[rows, lanes], masks))
                    dmix = dmix + dkernel[:, :CHUNK] * first + dkernel[:, CHUNK:] * second
                dmix_ref[c] = dmix
                dxd_within = dxd_ref[rows]
                carried = dot_nt(bc_ref[rows, state:], into16)
                falls = (
                    dy16_ref[rows].astype(F32) * within_ref[rows]
                    + dye_ref[rows].astype(F32) * carried
                    - xd_ref[rows].astype(F32) * dxd_within
                )
                dxd = dxd_within + tail[rows] * spread_back
                dxd_ref[rows] = dxd
                head_ref[0, rows] += self.head_sums(falls, heads_of)
                head_ref[1, rows] += self.head_sums(xt_ref[rows].astype(F32) * spread_back, heads_of)
                head_ref[2, rows] += self.head_sums(x[rows] * dxd, heads_of)
                dbc_ref[rows, :state] += dot_nn(xt_ref[rows], held16)
                dbc_ref[rows, state:] += dot_nn(dye_ref[rows], into16)
                if c > 0:
                    held = back_ref[c] + keep[:, c : c + 1] * held
            dx = dxd_ref[...] * dt + skip_ref[...] * dy
            grad = dx * (gate * (1.0 + pre * (1.0 - gate)))
            shift_ref[:HALO] = jnp.zeros((HALO, self.wide), F32)
            shift_ref[HALO + own :] = jnp.zeros((HALO, self.wide), F32)
            rows_ref[taps : taps + 1] = jnp.sum(grad, axis=0, keepdims=True)
            rows_ref[taps + 1 : taps + 2] = jnp.sum(dy * x, axis=0, keepdims=True)
            total = None
            for back in range(taps):
                masked = grad if back == 0 else grad * same_ref[:, back - 1 : back]
                shift_ref[HALO : HALO + own] = masked
                tap = conv_ref[taps - 1 - back : taps - back]
                piece = tap * shift_ref[back : back + own + HALO]
                total = piece if total is None else total + piece
                rows_ref[taps - 1 - back : taps - back] = jnp.sum(
                    masked * ext_ref[HALO - back : HALO - back + own], axis=0, keepdims=True
                )
            low_ref[...] = total.astype(BF16)
            self.project_back(low_ref, w_ref, through_ref)
            self.gradient(left_ref, low_ref, pieces_ref)

        f = jax.ShapeDtypeStruct
        scratch16 = pltpu.VMEM((own, self.wide), BF16)
        return self.call(
            kernel,
            [
                self.lanes(dy), self.lanes(x_ext), self.lanes(within), self.lanes(conv_rows), self.lanes(skip_rows),
                self.full(same), self.full(dt3), self.full(tail3), self.full(entry3),
                self.grouped(cum_g), self.grouped(cumt_g), self.full(coupling), self.full(bias),
                self.full(bc), self.states(states), self.states(leaving), self.states(back_added),
                self.full(keep3), self.pieces(w_x), self.full(left),
            ],
            [
                self.lanes(f((8, self.inner), F32)), self.full(f((3, own, 128), F32)),
                self.full(f((self.chunks, state, 128), F32)),
                self.full(f((own, 2 * state), F32)), self.full(f((self.chunks, CHUNK, CHUNK), F32)),
                self.full(f((self.ext, self.width), F32)), self.pieces(self.piece_shape()),
            ],
            [
                pltpu.VMEM((self.ext, self.wide), BF16), scratch16, scratch16, scratch16, scratch16, pltpu.VMEM((own, self.wide), F32),
                pltpu.VMEM((own + 2 * HALO, self.wide), F32),
            ],
        )

    def alone(self, kernel, ins, outs, scratch, microseconds):
        whole = pl.BlockSpec(memory_space=pltpu.VMEM)
        return pl.pallas_call(
            kernel,
            out_shape=outs,
            in_specs=[whole] * len(ins),
            out_specs=[whole] * len(outs),
            scratch_shapes=scratch,
            compiler_params=local_params(),
            cost_estimate=busy(microseconds),
        )(*ins)

    def prepare(self, normed, cotangent, side, seg_col, seg_row, bc_rows, head_rows, bc_cols, heads_own):
        own, taps, chunks = self.own, self.taps, self.chunks
        heads = heads_own * self.hts
        state2 = bc_cols * self.hts
        state = state2 // 2
        wide = self.hts * side.shape[2]

        def kernel(
            normed_ref, cot_ref, side_ref, seg_ref, segr_ref, bcw_ref, headw_ref,
            ext_left_ref, own_left_ref, cot_left_ref, w_ref, bce_ref, bc_ref, same_ref, dt_ref, sig_ref, cum_ref, cumt_ref, dt3_ref, tail3_ref, entry3_ref,
            keep_ref, keep3_ref, send_ref, mix_ref, bias_ref, raw_ref,
        ):
            row, lane = places((heads, self.hts * 16))
            pick = one_hot(lane == lax.div(row, heads_own) * 16 + lax.rem(row, heads_own))
            w_ref[...] = jnp.zeros_like(w_ref)
            for at in range(self.dps):
                cols = slice(at * self.rows, (at + 1) * self.rows)
                ext_left_ref[at] = normed_ref[:, cols].T
                own_left_ref[at] = normed_ref[HALO:, cols].T
                cot_left_ref[at] = cot_ref[:, cols].T
            for at in range(self.dps):
                cols = slice(at * self.rows, (at + 1) * self.rows)
                for one in range(self.hts):
                    w_ref[one * bc_cols : (one + 1) * bc_cols, cols] = side_ref[at, one, :bc_cols]
                padded = jnp.concatenate(
                    [side_ref[at, one, bc_cols : bc_cols + 16] for one in range(self.hts)], 0
                )
                w_ref[state2 : state2 + heads, cols] = dot_nn(pick, padded).astype(BF16)
            bce_ref[...] = dot_nt(normed_ref[...], w_ref[:state2])
            raw_ref[...] = dot_nt(normed_ref[HALO:], w_ref[state2 : state2 + 128])
            mine = seg_ref[HALO:]
            same_ref[...] = jnp.zeros_like(same_ref)
            for back in range(1, taps):
                hit = seg_ref[HALO - back : HALO - back + own] == mine
                same_ref[:, back - 1 : back] = hit.astype(F32)
            bc_ref[...] = silu_of(conv_pre(bce_ref, bcw_ref, same_ref, own, taps)).astype(BF16)
            shifted = raw_ref[:, :heads] + headw_ref[0:1]
            dt = jnp.maximum(shifted, 0.0) + jnp.log1p(jnp.exp(-jnp.abs(shifted)))
            dt_ref[...] = dt
            sig_ref[...] = jax.nn.sigmoid(shifted)
            rate = -jnp.exp(headw_ref[1:2])
            row, lane = places((CHUNK, CHUNK))
            lower = row >= lane
            triangle = lower.astype(F32)

            def put_thirds(ref, rows, v):
                for at, part in enumerate(thirds(v)):
                    ref[rows, at * heads : (at + 1) * heads] = part

            put_thirds(dt3_ref, slice(0, own), dt)
            keep_all = None
            for c in range(chunks):
                rows = self.chunk_rows(c)
                seg = mine[rows]
                before = seg_ref[HALO + c * CHUNK - 1 : HALO + c * CHUNK]
                end = seg_ref[HALO + (c + 1) * CHUNK - 1 : HALO + (c + 1) * CHUNK]
                cum = dot_exact(triangle, dt_ref[rows] * rate)
                last = cum[CHUNK - 1 : CHUNK]
                put_thirds(tail3_ref, rows, jnp.exp(last - cum) * (seg == end).astype(F32))
                put_thirds(entry3_ref, rows, jnp.exp(cum) * (seg == before).astype(F32))
                keep = jnp.exp(last) * (before == end).astype(F32)
                keep_ref[c : c + 1] = keep
                keep_all = keep if keep_all is None else keep_all * keep
                flipped = cum.T
                for j in range(self.groups):
                    cum_ref[j, rows] = cum[:, j * self.heads : (j + 1) * self.heads]
                    cumt_ref[j, :, rows] = flipped[j * self.heads : (j + 1) * self.heads]
                mix_ref[c] = dot_nt(bc_ref[rows, state:], bc_ref[rows, :state])
                bias_ref[c] = jnp.where((seg == segr_ref[0:1, rows]) & lower, 0.0, MASKED)
            keep_ref[chunks:] = jnp.zeros((8 - chunks, heads), F32)
            for at, part in enumerate(thirds(keep_ref[...].T)):
                keep3_ref[at * heads : (at + 1) * heads] = part
            first, second, third = thirds(keep_all)
            row, _ = places((16, heads))
            stacked = jnp.where(
                row == 0,
                first.astype(F32),
                jnp.where(row == 1, second.astype(F32), jnp.where(row == 2, third.astype(F32), 0.0)),
            ).astype(BF16)
            row, lane = places((heads, self.cols))
            for one in range(self.hts):
                spread = one_hot(row == one * heads_own + lax.div(lane, 64))
                send_ref[one] = dot_nn(stacked, spread).astype(BF16)

        f = jax.ShapeDtypeStruct
        return self.alone(
            kernel,
            [normed, cotangent, side, seg_col, seg_row, bc_rows, head_rows],
            [
                f((self.dps, self.rows, self.ext), BF16), f((self.dps, self.rows, own), BF16),
                f((self.dps, self.rows, own), BF16),
                f((wide, self.width), BF16), f((self.ext, state2), F32), f((own, state2), BF16), f((own, 8), F32),
                f((own, heads), F32), f((own, heads), F32), f((self.groups, own, self.heads), F32),
                f((self.groups, self.heads, own), F32), f((own, 3 * heads), BF16), f((own, 3 * heads), BF16),
                f((own, 3 * heads), BF16), f((8, heads), F32), f((3 * heads, 8), BF16),
                f((self.hts, 16, self.cols), BF16), f((chunks, CHUNK, CHUNK), F32), f((chunks, CHUNK, CHUNK), F32),
            ],
            [pltpu.VMEM((own, 128), F32)],
            10,
        )

    def finish(
        self, dbc, dmix, bc, bc_ext, bc_rows, same, head_sums, dots, keep, dt, sig, head_rows, w_side, through,
        own_part, normed,
    ):
        own, taps, chunks = self.own, self.taps, self.chunks
        heads = dt.shape[1]
        state2 = bc.shape[1]
        state = state2 // 2
        wide = w_side.shape[0]

        def kernel(
            dbc_ref, dmix_ref, bc_ref, bce_ref, bcw_ref, same_ref, sums_ref, dots_ref, keep_ref, dt_ref, sig_ref,
            headw_ref, w_ref, through_ref, own_ref, normed_ref,
            part_ref, halo_ref, taps_ref, heads_ref, pieces_ref, low_ref, shift_ref, full_ref,
        ):
            rate = -jnp.exp(headw_ref[1:2])
            row, lane = places((CHUNK, CHUNK))
            upper = (row <= lane).astype(F32)
            strict = (row > lane).astype(F32)
            low_ref[...] = jnp.zeros_like(low_ref)
            grad_shift = jnp.zeros((1, heads), F32)
            grad_log = jnp.zeros((1, heads), F32)
            for c in range(chunks):
                rows = self.chunk_rows(c)
                dmix16 = dmix_ref[c].astype(BF16)
                full_ref[rows, :state] = dbc_ref[rows, :state] + dot_tn(dmix16, bc_ref[rows, state:])
                full_ref[rows, state:] = dbc_ref[rows, state:] + dot_nn(dmix16, bc_ref[rows, :state])
                crossing = jnp.sum(dots_ref[c], axis=0, keepdims=True)[:, :heads]
                da = (
                    dot_exact(upper, sums_ref[0, rows, :heads])
                    + dot_exact(strict, sums_ref[1, rows, :heads])
                    + keep_ref[c : c + 1] * crossing
                )
                grad_log = grad_log + jnp.sum(dt_ref[rows] * da, axis=0, keepdims=True)
                ddt_raw = (sums_ref[2, rows, :heads] + rate * da) * sig_ref[rows]
                grad_shift = grad_shift + jnp.sum(ddt_raw, axis=0, keepdims=True)
                low_ref[HALO + c * CHUNK : HALO + (c + 1) * CHUNK, state2 : state2 + heads] = ddt_raw.astype(BF16)
            heads_ref[...] = jnp.zeros_like(heads_ref)
            heads_ref[0:1] = grad_shift
            heads_ref[1:2] = rate * grad_log
            pre = conv_pre(bce_ref, bcw_ref, same_ref, own, taps)
            gate = jax.nn.sigmoid(pre)
            grad = full_ref[...] * (gate * (1.0 + pre * (1.0 - gate)))
            shift_ref[:HALO] = jnp.zeros((HALO, state2), F32)
            shift_ref[HALO + own :] = jnp.zeros((HALO, state2), F32)
            taps_ref[...] = jnp.zeros_like(taps_ref)
            taps_ref[taps : taps + 1] = jnp.sum(grad, axis=0, keepdims=True)
            total = None
            for back in range(taps):
                masked = grad if back == 0 else grad * same_ref[:, back - 1 : back]
                shift_ref[HALO : HALO + own] = masked
                piece = bcw_ref[taps - 1 - back : taps - back] * shift_ref[back : back + own + HALO]
                total = piece if total is None else total + piece
                taps_ref[taps - 1 - back : taps - back] = jnp.sum(
                    masked * bce_ref[HALO - back : HALO - back + own], axis=0, keepdims=True
                )
            low_ref[:, :state2] = total.astype(BF16)
            part = through_ref[...] + dot_nn(low_ref[...], w_ref[...])
            part_ref[...] = part[HALO:] + own_ref[...]
            halo_ref[...] = part[:HALO]
            for at in range(self.dps):
                cols = slice(at * self.rows, (at + 1) * self.rows)
                pieces_ref[at] = dot_tn(low_ref[...], normed_ref[:, cols]).astype(BF16)

        f = jax.ShapeDtypeStruct
        return self.alone(
            kernel,
            [
                dbc, dmix, bc, bc_ext, bc_rows, same, head_sums, dots, keep, dt, sig, head_rows, w_side, through,
                own_part, normed,
            ],
            [
                f((own, self.width), F32), f((HALO, self.width), F32), f((8, state2), F32), f((8, heads), F32),
                f((self.dps, wide, self.rows), BF16),
            ],
            [
                pltpu.VMEM((self.ext, wide), BF16), pltpu.VMEM((own + 2 * HALO, state2), F32),
                pltpu.VMEM((own, state2), F32),
            ],
            12,
        )


def from_earlier(values, distance, size):
    return lax.ppermute(values, SEQ, [(i, i + distance) for i in range(size - distance)])


def from_later(values, distance, size):
    return lax.ppermute(values, SEQ, [(i + distance, i) for i in range(size - distance)])


def body(
    residual,
    segment_ids,
    norm_in_gain,
    w_zx,
    w_bc,
    w_dt,
    conv_x_weight,
    conv_x_bias,
    conv_bc_weight,
    conv_bc_bias,
    dt_bias,
    a_log,
    d_skip,
    norm_gain,
    w_out,
    cotangent,
):
    own, width = residual.shape
    dp_size = lax.axis_size("dp")
    size = lax.axis_size(SEQ)
    place = lax.axis_index(SEQ)
    dp_rows, _, cols = w_zx.shape
    heads_own = w_dt.shape[1]
    inner = cols * size
    heads = heads_own * size
    state2 = w_bc.shape[1]
    bc_cols = state2 // size
    head_width = inner // heads

    sizes = (dp_size // 2, lax.axis_size("head"), lax.axis_size("tensor"))
    taps = conv_x_weight.shape[0]
    bc_own = lax.dynamic_slice_in_dim(w_bc, place * bc_cols, bc_cols, 1)
    side_part = jnp.concatenate([bc_own, w_dt], 1).T
    side_part = jnp.pad(side_part, ((0, bc_cols + 16 - side_part.shape[0]), (0, 0)))
    small_rows = [conv_x_weight, conv_x_bias[None], norm_gain[None]]
    head_rows = jnp.stack([dt_bias, a_log, d_skip])
    small = jnp.concatenate(small_rows + [jnp.pad(head_rows, ((0, 0), (0, cols - heads_own)))], 0)
    small = jnp.pad(small, ((0, 16 - small.shape[0]), (0, 0)))

    def gathered(part):
        full = lax.all_gather(part, ALL, axis=0, tiled=False)
        return full.reshape(dp_size, size, dp_rows, cols)

    rows_ext = jnp.concatenate([from_earlier(residual[-HALO:], 1, size), residual], 0).astype(F32)
    inv_ext = lax.rsqrt(jnp.mean(rows_ext * rows_ext, axis=1, keepdims=True) + EPSILON)
    normed = (rows_ext * inv_ext * norm_in_gain).astype(BF16)
    normed_own = normed[HALO:]
    rows_in, inv_rms = rows_ext[HALO:], inv_ext[HALO:]

    seg_all = jnp.pad(segment_ids[0], (HALO, 0), constant_values=-1).astype(F32)
    seg_ext = lax.dynamic_slice_in_dim(seg_all, place * own, own + HALO)
    seg_row = jnp.broadcast_to(seg_ext[None, HALO:], (8, own))
    bc_rows = jnp.concatenate([conv_bc_weight, conv_bc_bias[None]], 0)
    bc_rows = jnp.pad(bc_rows, ((0, 8 - bc_rows.shape[0]), (0, 0)))

    w_z = gathered(w_zx[:, 0])
    side_full, w_x, small_full = gather_weights([side_part, w_zx[:, 1]], small, sizes)
    w_out_later, small_full = lax.optimization_barrier((w_out, small_full))
    w_o = gathered(w_out_later)
    w_x = w_x.reshape(dp_size, size, dp_rows, cols)
    side_full = side_full.reshape(dp_size, size, bc_cols + 16, dp_rows)
    small_full = jnp.moveaxis(small_full.reshape(size, 16, cols), 0, 1)
    per_channel = small_full.reshape(16, inner)
    per_head = small_full[taps + 2 : taps + 5, :, :heads_own].reshape(3, heads)
    conv_rows = per_channel[:8]
    gain_row = per_channel[taps + 1 : taps + 2]
    head_rows = jnp.pad(per_head[:2], ((0, 6), (0, 0)))
    skip_rows = jnp.repeat(per_head[2], head_width)[None]

    scan = Scan(own, sizes, dp_rows, cols, heads_own, taps)
    (
        ext_left, own_left, cot_left, w_side, bc_ext, bc, same, dt, sig, cum_g, cumt_g, dt3, tail3, entry3, keep, keep3, keep_send, coupling, bias,
    ) = scan.prepare(normed, cotangent, side_full, seg_ext[:, None], seg_row, bc_rows, head_rows, bc_cols, heads_own)
    x_ext, x, within, added, local = scan.s1(
        normed, w_x, conv_rows, same, dt3, tail3, cum_g, cumt_g, coupling, bias, bc, keep3
    )
    (entering,) = exchange_states(local, keep_send, sizes, True)
    z, y, states, squares = scan.s2(
        normed_own, w_z, within, x, skip_rows, entry3, bc, entering, added, keep3
    )
    grad_gate, cross, gain_rows, block_out, out_pieces = scan.s3(
        y, z, squares, gain_row, w_o, cotangent, residual, cot_left
    )
    dy, back_added, back_local, own_part, z_pieces = scan.s4(
        y, z, squares, cross, gain_row, grad_gate, w_z, entry3, bc, keep3, own_left
    )

    def scattered(pieces):
        pieces = pieces.reshape(dp_size * size, dp_rows, cols)
        return lax.psum_scatter(pieces, ALL, scatter_dimension=0, tiled=False).astype(F32)

    grid = (dp_size,) + sizes[1:]
    grad_wo = scattered(out_pieces)
    leaving, grad_wz = exchange_states(
        back_local, keep_send, sizes, False, (z_pieces.reshape(grid + (dp_rows, cols)),)
    )
    conv_sums, head_sums, dots, dbc, dmix, through, x_pieces = scan.s5(
        dy, x_ext, within, conv_rows, skip_rows, same, dt3, tail3, entry3, cum_g, cumt_g, coupling, bias, bc,
        states, leaving, back_added, keep3, w_x, ext_left
    )
    part, halo, bc_sums, scan_sums, side_pieces = scan.finish(
        dbc, dmix, bc, bc_ext, bc_rows, same, head_sums, dots, keep, dt, sig, head_rows, w_side, through, own_part,
        normed
    )

    grad_normed = part.at[own - HALO :].add(from_later(halo, 1, size))
    scaled_in = grad_normed * norm_in_gain
    input_grad = (
        cotangent.astype(F32)
        + inv_rms * scaled_in
        - rows_in * (inv_rms * inv_rms * inv_rms) * jnp.mean(scaled_in * rows_in, axis=1, keepdims=True)
    )
    grad_in_gain = jnp.sum(grad_normed * rows_in * inv_rms, axis=0)

    grad_skip = jnp.sum(conv_sums[taps + 1].reshape(heads, head_width), axis=1)
    head_sum = jnp.concatenate([scan_sums[0], scan_sums[1], grad_skip])
    row = jnp.concatenate([grad_in_gain, bc_sums[: taps + 1].reshape(-1)])
    small_sum = jnp.concatenate(
        [
            conv_sums[: taps + 1],
            gain_rows[:1],
            jnp.pad(row, (0, inner - row.shape[0]))[None],
            jnp.pad(head_sum, (0, inner - head_sum.shape[0]))[None],
        ],
        0,
    )
    grad_side, grad_wx, small_sum = scatter_gradients(
        [side_pieces.reshape(grid + (-1, dp_rows)), x_pieces.reshape(grid + (dp_rows, cols))], small_sum, sizes
    )
    grad_wzx = jnp.stack([grad_wz, grad_wx], 1)
    grad_side = grad_side.reshape(-1, dp_rows).astype(F32)
    grad_wbc = grad_side[:state2].T
    grad_wdt = lax.dynamic_slice_in_dim(grad_side, state2 + place * heads_own, heads_own, 0).T
    channel_own = lax.dynamic_slice_in_dim(small_sum[: taps + 2], place * cols, cols, 1)
    row = small_sum[taps + 2]
    gain_sum = row[:width]
    taps_sum = row[width : width + taps * state2].reshape(taps, state2)
    bias_sum = row[width + taps * state2 : width + (taps + 1) * state2]
    head_sum = small_sum[taps + 3, : 3 * heads].reshape(3, heads)
    head_own = lax.dynamic_slice_in_dim(head_sum, place * heads_own, heads_own, 1)
    return (
        block_out,
        input_grad,
        gain_sum,
        grad_wzx,
        grad_wbc,
        grad_wdt,
        channel_own[:taps],
        channel_own[taps],
        taps_sum,
        bias_sum,
        head_own[0],
        head_own[1],
        head_own[2],
        channel_own[taps + 1],
        grad_wo,
    )


def solution(mesh):
    rows = P(ALL, None)
    in_specs = (
        rows,
        P("dp", None),
        P(),
        P("dp", None, SEQ),
        P("dp", None),
        P("dp", SEQ),
        P(None, SEQ),
        P(SEQ),
        P(),
        P(),
        P(SEQ),
        P(SEQ),
        P(SEQ),
        P(SEQ),
        P("dp", SEQ),
        rows,
    )
    out_specs = (
        rows,
        rows,
        P(),
        P("dp", None, SEQ),
        P("dp", None),
        P("dp", SEQ),
        P(None, SEQ),
        P(SEQ),
        P(),
        P(),
        P(SEQ),
        P(SEQ),
        P(SEQ),
        P(SEQ),
        P("dp", SEQ),
    )
    return jax.shard_map(
        body, mesh=mesh, in_specs=in_specs, out_specs=out_specs, check_vma=False
    )
```

```python
import functools

import jax
import jax.numpy as jnp
from jax import lax
from jax.experimental import pallas as pl
from jax.experimental.pallas import tpu as pltpu
from jax.sharding import PartitionSpec as P

EPSILON = 1e-05
CHUNK = 128
HALO = 16
AHEAD = 2
LAGS = (0, 1, 3, 5)
HOSTED_LAGS = (0, 4, 6, 8)
SLOTS = 2
CHUNK_ROWS = 48
MASKED = -1e30
HIGHEST = lax.Precision.HIGHEST
SEQ = ("head", "tensor")
ALL = ("dp", "head", "tensor")
BF16 = jnp.bfloat16
F32 = jnp.float32
MESH = pl.DeviceIdType.MESH
VMEM_BYTES = 56 << 20


def coordinates():
    dp = lax.axis_index("dp")
    return lax.div(dp, 2), lax.rem(dp, 2), lax.axis_index("head"), lax.axis_index("tensor")


def enter_kernel(x, core, head, tensor, xs, hs, ts, sibling):
    barrier = pltpu.get_barrier_semaphore()
    count = 0
    for step in range(1, hs):
        pl.semaphore_signal(barrier, 1, device_id={"head": lax.rem(head + step, hs)}, device_id_type=MESH)
        count += 1
    for step in range(1, ts):
        pl.semaphore_signal(barrier, 1, device_id={"tensor": lax.rem(tensor + step, ts)}, device_id_type=MESH)
        count += 1
    for step in range(1, xs):
        other = 2 * lax.rem(x + step, xs) + core
        pl.semaphore_signal(barrier, 1, device_id={"dp": other}, device_id_type=MESH)
        count += 1
    if sibling:
        pl.semaphore_signal(barrier, 1, device_id={"dp": 2 * x + 1 - core}, device_id_type=MESH)
        count += 1
    pl.semaphore_wait(barrier, count)


def gatherer(sizes, chunks, parts, fulls, sems):
    xs, hs, ts = sizes
    send, recv, own_sem = sems
    x, core, head, tensor = coordinates()
    dp = 2 * x + core
    total = len(chunks)
    ahead = 4

    def own():
        return [
            pltpu.make_async_copy(part, full.at[dp, head, tensor], own_sem.at[kind])
            for kind, (part, full) in enumerate(zip(parts, fulls))
        ]

    def copy(src, dst, index, slot, device):
        return pltpu.make_async_remote_copy(
            src_ref=src,
            dst_ref=dst,
            send_sem=send.at[index, slot],
            recv_sem=recv.at[index, slot],
            device_id=device,
            device_id_type=MESH,
        )

    def along_head(index):
        kind, start, length, _ = chunks[index]
        rows = pl.ds(start, length)
        return [
            copy(
                parts[kind].at[rows],
                fulls[kind].at[dp, head, tensor, rows],
                index,
                step - 1,
                {"head": lax.rem(head + step, hs)},
            )
            for step in range(1, hs)
        ]

    def over(index, axis, second):
        kind, start, length, _ = chunks[index]
        rows = pl.ds(start, length)
        base = hs - 1 if second else hs - 1 + max(xs, ts)
        copies = []
        if axis == "tensor":
            homes = [dp] if second else [2 * home + core for home in range(xs)]
            for step in range(1, ts):
                for home in homes:
                    view = fulls[kind].at[home, :, tensor, rows]
                    device = {"tensor": lax.rem(tensor + step, ts)}
                    copies.append(copy(view, view, index, base + len(copies), device))
        else:
            for step in range(1, xs):
                view = fulls[kind].at[dp, :, tensor, rows] if second else fulls[kind].at[dp, :, :, rows]
                device = {"dp": 2 * lax.rem(x + step, xs) + core}
                copies.append(copy(view, view, index, base + len(copies), device))
        return copies

    def to_sibling(index):
        kind, start, length, _ = chunks[index]
        rows = pl.ds(start, length)
        base = hs - 1 + max(xs, ts) + max(xs, xs * ts)
        return [
            copy(
                fulls[kind].at[2 * home + core, :, :, rows],
                fulls[kind].at[2 * home + core, :, :, rows],
                index,
                base + home,
                {"dp": 2 * x + 1 - core},
            )
            for home in range(xs)
        ]

    def stage(index, number):
        tensor_first = chunks[index][3]
        if number == 0:
            return along_head(index)
        if number == 1:
            return over(index, "tensor" if tensor_first else "x", True)
        if number == 2:
            return over(index, "x" if tensor_first else "tensor", False)
        return to_sibling(index)

    def start(first):
        if first:
            for one in own():
                one.start()
        else:
            for index in range(min(ahead, total)):
                for one in stage(index, 0):
                    one.start()
            for one in own():
                one.wait()

    def tick(at):
        for number in range(4):
            index = at - 2 * number
            if 0 <= index < total:
                for one in stage(index, number):
                    one.wait_recv()
                if number < 3:
                    for one in stage(index, number + 1):
                        one.start()
                if number == 0 and index + ahead < total:
                    for one in stage(index + ahead, 0):
                        one.start()

    def end():
        for index in range(total):
            for number in range(4):
                for one in stage(index, number):
                    one.wait_send()

    return start, tick, end, total + 6


def gatherer_scratch(sizes, chunks, kinds):
    xs, hs, ts = sizes
    slots = hs - 1 + max(xs, ts) + max(xs, xs * ts) + xs
    return [
        pltpu.SemaphoreType.DMA((len(chunks), slots)),
        pltpu.SemaphoreType.DMA((len(chunks), slots)),
        pltpu.SemaphoreType.DMA((kinds,)),
    ]


def gather_kernel(sizes, chunks, kinds, *refs):
    xs, hs, ts = sizes
    parts, small = refs[:kinds], refs[kinds]
    fulls, small_full = refs[kinds + 1 : 2 * kinds + 1], refs[2 * kinds + 1]
    sems, rest = refs[2 * kinds + 2 : 2 * kinds + 5], refs[2 * kinds + 5 :]
    small_send, small_recv, small_own = rest
    x, core, head, tensor = coordinates()
    begin, step_on, end, ticks = gatherer(sizes, chunks, parts, fulls, sems)
    begin(True)
    own_small = pltpu.make_async_copy(small, small_full.at[head, tensor], small_own.at[0])
    own_small.start()
    enter_kernel(x, core, head, tensor, xs, hs, ts, True)
    small_tensor = [
        pltpu.make_async_remote_copy(
            src_ref=small,
            dst_ref=small_full.at[head, tensor],
            send_sem=small_send.at[step - 1],
            recv_sem=small_recv.at[step - 1],
            device_id={"tensor": lax.rem(tensor + step, ts)},
            device_id_type=MESH,
        )
        for step in range(1, ts)
    ]
    small_head = [
        pltpu.make_async_remote_copy(
            src_ref=small_full.at[head],
            dst_ref=small_full.at[head],
            send_sem=small_send.at[ts + step - 2],
            recv_sem=small_recv.at[ts + step - 2],
            device_id={"head": lax.rem(head + step, hs)},
            device_id_type=MESH,
        )
        for step in range(1, hs)
    ]
    for one in small_tensor:
        one.start()
    begin(False)
    own_small.wait()
    for one in small_tensor:
        one.wait_recv()
    for one in small_head:
        one.start()
    for tick in range(ticks):
        step_on(tick)
    for one in small_head:
        one.wait_recv()
    for one in small_tensor + small_head:
        one.wait_send()
    end()


def row_chunks(rows, first, kinds, pieces):
    step = rows // pieces
    return [
        (kind, piece * step, step, piece % 2 == 1)
        for kind in range(first, kinds)
        for piece in range(pieces)
    ]


def gather_weights(parts, small, sizes):
    xs, hs, ts = sizes
    kinds = len(parts)
    count = parts[1].shape[0]
    chunks = [(0, 0, parts[0].shape[0], True)] + row_chunks(count, 1, kinds, count // CHUNK_ROWS)
    full = [jax.ShapeDtypeStruct((2 * xs, hs, ts) + part.shape, part.dtype) for part in parts]
    full.append(jax.ShapeDtypeStruct((hs, ts) + small.shape, small.dtype))
    anywhere = pl.BlockSpec(memory_space=pl.ANY)
    return pl.pallas_call(
        functools.partial(gather_kernel, sizes, chunks, kinds),
        out_shape=full,
        in_specs=[anywhere] * (kinds + 1),
        out_specs=[anywhere] * (kinds + 1),
        scratch_shapes=gatherer_scratch(sizes, chunks, kinds)
        + [
            pltpu.SemaphoreType.DMA((hs + ts,)),
            pltpu.SemaphoreType.DMA((hs + ts,)),
            pltpu.SemaphoreType.DMA((1,)),
        ],
        compiler_params=pltpu.CompilerParams(
            collective_id=0, has_side_effects=True, vmem_limit_bytes=VMEM_BYTES
        ),
        cost_estimate=busy(60),
    )(*parts, small)


def reducer(sizes, chunks, parts, bufs, sems, put, lags=LAGS):
    xs, hs, ts = sizes
    send, recv, own_sem = sems
    x, core, head, tensor = coordinates()
    total = len(chunks)

    def loads(index):
        kind, start, length, _ = chunks[index]
        rows = pl.ds(start, length)
        return [
            pltpu.make_async_copy(
                parts[kind].at[2 * home + core, :, :, rows],
                bufs[5 * index].at[home],
                own_sem.at[index, home],
            )
            for home in range(xs)
        ]

    def stage(index, number):
        kind, start, length, x_first = chunks[index]
        rows = pl.ds(start, length)
        held = bufs[5 * index]
        into = bufs[5 * index + 1 + number]
        slots = (0, xs, xs + max(xs, ts) - 1, xs + 2 * (max(xs, ts) - 1))
        by_x = [
            (lax.rem(x + step, xs), {"dp": 2 * lax.rem(x + step, xs) + core}) for step in range(1, xs)
        ]
        by_tensor = [
            (lax.rem(tensor + step, ts), {"tensor": lax.rem(tensor + step, ts)}) for step in range(1, ts)
        ]
        if number == 0:
            moves = [
                (parts[kind].at[2 * home + 1 - core, :, :, rows], into.at[home], {"dp": 2 * x + 1 - core})
                for home in range(xs)
            ]
        elif number == 1 and x_first:
            moves = [(held.at[to], into.at[at], device) for at, (to, device) in enumerate(by_x)]
        elif number == 1:
            moves = [(held.at[:, :, to], into.at[at], device) for at, (to, device) in enumerate(by_tensor)]
        elif number == 2 and x_first:
            moves = [(held.at[x, :, to], into.at[at], device) for at, (to, device) in enumerate(by_tensor)]
        elif number == 2:
            moves = [(held.at[to, :, tensor], into.at[at], device) for at, (to, device) in enumerate(by_x)]
        else:
            moves = []
            for step in range(1, hs):
                to = lax.rem(head + step, hs)
                moves.append((held.at[x, to, tensor], into.at[step - 1], {"head": to}))
        return [
            pltpu.make_async_remote_copy(
                src_ref=src,
                dst_ref=dst,
                send_sem=send.at[index, slots[number] + at],
                recv_sem=recv.at[index, slots[number] + at],
                device_id=device,
                device_id_type=MESH,
            )
            for at, (src, dst, device) in enumerate(moves)
        ]

    def add(index, number):
        kind, start, length, x_first = chunks[index]
        held = bufs[5 * index]
        into = bufs[5 * index + 1 + number]
        def plus(own, others):
            if len(others) == 1:
                return own + others[0]
            value = own.astype(F32)
            for one in others:
                value = value + one.astype(F32)
            return value.astype(BF16)

        if number == 0:

            @pl.loop(0, xs * hs)
            def _(both):
                one, two = lax.div(both, hs), lax.rem(both, hs)
                held[one, two] = plus(held[one, two], [into[one, two]])

        elif number == 1 and x_first:

            @pl.loop(0, hs)
            def _(one):
                held[x, one] = plus(held[x, one], [into[step, one] for step in range(xs - 1)])

        elif number == 1:

            @pl.loop(0, xs * hs)
            def _(both):
                one, two = lax.div(both, hs), lax.rem(both, hs)
                held[one, two, tensor] = plus(
                    held[one, two, tensor], [into[step, one, two] for step in range(ts - 1)]
                )

        elif number == 2:

            @pl.loop(0, hs)
            def _(one):
                held[x, one, tensor] = plus(
                    held[x, one, tensor], [into[step, one] for step in range(into.shape[0])]
                )

        else:
            value = held[x, head, tensor].astype(F32)
            for step in range(hs - 1):
                value = value + into[step].astype(F32)
            put(kind, start, length, value)

    def start(first):
        for index in range(total):
            if first:
                for one in loads(index):
                    one.start()
            elif index < AHEAD:
                for one in stage(index, 0):
                    one.start()

    def tick(at):
        for number, lag in enumerate(lags):
            index = at - lag
            if 0 <= index < total:
                for one in stage(index, number):
                    one.wait_recv()
                if number == 0:
                    if index + AHEAD < total:
                        for one in stage(index + AHEAD, 0):
                            one.start()
                    for one in loads(index):
                        one.wait()
                add(index, number)
                if number < 3:
                    for one in stage(index, number + 1):
                        one.start()

    def end():
        for index in range(total):
            for number in range(4):
                for one in stage(index, number):
                    one.wait_send()

    return start, tick, end, total + lags[3]


def reducer_scratch(sizes, chunks, parts):
    xs, hs, ts = sizes
    scratch = []
    for kind, _, length, x_first in chunks:
        block = (length, parts[kind].shape[4])
        kept = (hs, ts) if x_first else (xs, hs)
        near, far = (xs, ts) if x_first else (ts, xs)
        scratch += [
            pltpu.VMEM((xs, hs, ts) + block, BF16),
            pltpu.VMEM((xs, hs, ts) + block, BF16),
            pltpu.VMEM((near - 1,) + kept + block, BF16),
            pltpu.VMEM((far - 1, hs) + block, BF16),
            pltpu.VMEM((hs - 1,) + block, BF16),
        ]
    slots = xs + 2 * (max(xs, ts) - 1) + hs - 1
    return scratch + [
        pltpu.SemaphoreType.DMA((len(chunks), slots)),
        pltpu.SemaphoreType.DMA((len(chunks), slots)),
        pltpu.SemaphoreType.DMA((len(chunks), xs)),
    ]


def scatter_kernel(sizes, chunks, kinds, *refs):
    xs, hs, ts = sizes
    parts, small = refs[:kinds], refs[kinds]
    outs, small_out = refs[kinds + 1 : 2 * kinds + 1], refs[2 * kinds + 1]
    rest = refs[2 * kinds + 2 :]
    count = 5 * len(chunks)
    bufs, sems, rest = rest[:count], rest[count : count + 3], rest[count + 3 :]
    small_acc, small_in, small_send, small_recv, side_send, side_recv = rest
    x, core, head, tensor = coordinates()

    def put(kind, start, length, value):
        if kind == 0:
            outs[kind][head, tensor] = value.astype(BF16)
        else:
            outs[kind][start : start + length, :] = value

    begin, step_on, end, ticks = reducer(sizes, chunks, parts, bufs, sems, put)

    def side_copy(view, slot, device):
        return pltpu.make_async_remote_copy(
            src_ref=view,
            dst_ref=view,
            send_sem=side_send.at[slot],
            recv_sem=side_recv.at[slot],
            device_id=device,
            device_id_type=MESH,
        )

    side_tensor = [
        side_copy(outs[0].at[head, tensor], step - 1, {"tensor": lax.rem(tensor + step, ts)})
        for step in range(1, ts)
    ]
    side_head = [
        side_copy(outs[0].at[head], ts + step - 2, {"head": lax.rem(head + step, hs)})
        for step in range(1, hs)
    ]
    small_slots = [1, xs - 1, ts - 1, hs - 1]
    small_base = [0, 1, xs, xs + ts - 1]

    def small_stage(number):
        copies = []
        for step in range(1, small_slots[number] + 1):
            slot = small_base[number] + step - 1
            device = (
                {"dp": 2 * x + 1 - core},
                {"dp": 2 * lax.rem(x + step, xs) + core},
                {"tensor": lax.rem(tensor + step, ts)},
                {"head": lax.rem(head + step, hs)},
            )[number]
            copies.append(
                pltpu.make_async_remote_copy(
                    src_ref=small if number == 0 else small_acc.at[number - 1],
                    dst_ref=small_in.at[slot],
                    send_sem=small_send.at[slot],
                    recv_sem=small_recv.at[slot],
                    device_id=device,
                    device_id_type=MESH,
                )
            )
        return copies

    def small_add(number):
        mine = small[...] if number == 0 else small_acc[number - 1]
        size = small_slots[number] + 1
        place = (core, x, tensor, head)[number]
        value = None
        for at in range(size):
            step = lax.rem(place - at + size, size)
            slot = small_base[number] + jnp.maximum(step - 1, 0)
            here = jnp.where(step == 0, mine, small_in[slot])
            value = here if value is None else value + here
        if number < 3:
            small_acc[number] = value
        else:
            small_out[...] = value

    begin(True)
    enter_kernel(x, core, head, tensor, xs, hs, ts, True)
    for one in small_stage(0):
        one.start()
    begin(False)
    for tick in range(max(ticks, 9)):
        step_on(tick)
        if tick == 5:
            for one in side_tensor:
                one.start()
        if tick == 7:
            for one in side_tensor:
                one.wait_recv()
            for one in side_head:
                one.start()
        if tick in (0, 2, 4, 6):
            number = tick // 2
            for one in small_stage(number):
                one.wait_recv()
            small_add(number)
            if number < 3:
                for one in small_stage(number + 1):
                    one.start()
    for one in side_head:
        one.wait_recv()
    for one in side_tensor + side_head:
        one.wait_send()
    for number in range(4):
        for one in small_stage(number):
            one.wait_send()
    end()


def scatter_gradients(parts, small, sizes):
    xs, hs, ts = sizes
    kinds = len(parts)
    count = parts[1].shape[3]
    chunks = [(0, 0, parts[0].shape[3], True)] + row_chunks(count, 1, kinds, count // CHUNK_ROWS)
    small_slots = xs + ts + hs - 2
    anywhere = pl.BlockSpec(memory_space=pl.ANY)
    whole = pl.BlockSpec(memory_space=pltpu.VMEM)
    return pl.pallas_call(
        functools.partial(scatter_kernel, sizes, chunks, kinds),
        out_shape=[jax.ShapeDtypeStruct((hs, ts) + parts[0].shape[3:], BF16)]
        + [jax.ShapeDtypeStruct(part.shape[3:], F32) for part in parts[1:]]
        + [jax.ShapeDtypeStruct(small.shape, F32)],
        in_specs=[anywhere] * kinds + [whole],
        out_specs=[whole] * (kinds + 1),
        scratch_shapes=reducer_scratch(sizes, chunks, parts)
        + [
            pltpu.VMEM((3,) + small.shape, F32),
            pltpu.VMEM((small_slots,) + small.shape, F32),
            pltpu.SemaphoreType.DMA((small_slots,)),
            pltpu.SemaphoreType.DMA((small_slots,)),
            pltpu.SemaphoreType.DMA((hs + ts,)),
            pltpu.SemaphoreType.DMA((hs + ts,)),
        ],
        compiler_params=pltpu.CompilerParams(
            collective_id=1, has_side_effects=True, vmem_limit_bytes=VMEM_BYTES
        ),
        cost_estimate=busy(60),
    )(*parts, small)


def exchange_kernel(sizes, forward, chunks, *refs):
    xs, hs, ts = sizes
    size = hs * ts
    hosts = bool(chunks)
    local, keep = refs[:2]
    parts, out = refs[2 : 2 + hosts], refs[2 + hosts]
    outs, rest = refs[3 + hosts : 3 + 2 * hosts], refs[3 + 2 * hosts :]
    got, keeps, sums, sems, keep_sems, back_sems = rest[:6]
    x, core, head, tensor = coordinates()
    me = head * ts + tensor

    def put(kind, start, length, value):
        outs[kind][start : start + length, :] = value

    ticks = 0
    if hosts:
        begin, step_on, end, ticks = reducer(sizes, chunks, parts, rest[6:-3], rest[-3:], put)
        begin(True)
    barrier = pltpu.get_barrier_semaphore()
    peers = []
    for step in range(1, size):
        to = lax.rem(me + step, size)
        peers.append((to, {"head": lax.div(to, ts), "tensor": lax.rem(to, ts)}))
    others = [device for _, device in peers]
    if hosts:
        others += [{"dp": 2 * lax.rem(x + step, xs) + core} for step in range(1, xs)]
        others.append({"dp": 2 * x + 1 - core})
    for device in others:
        pl.semaphore_signal(barrier, 1, device_id=device, device_id_type=MESH)
    pl.semaphore_wait(barrier, len(others))

    def copies(src, dst, pair):
        return [
            pltpu.make_async_remote_copy(
                src_ref=src.at[to],
                dst_ref=dst.at[me],
                send_sem=pair.at[0, at],
                recv_sem=pair.at[1, at],
                device_id=device,
                device_id_type=MESH,
            )
            for at, (to, device) in enumerate(peers)
        ]

    factors = copies(keep, keeps, keep_sems)
    states = copies(local, got, sems)
    for one in factors + states:
        one.start()
    if hosts:
        begin(False)
    got[me] = local[me]
    keeps[me] = keep[me]
    for tick in range(min(3, ticks)):
        step_on(tick)
    for one in factors + states:
        one.wait_recv()
    third = lax.broadcasted_iota(jnp.int32, (keep.shape[1], local.shape[2]), 0) < 3
    third = third.astype(BF16)
    held = jnp.zeros(local.shape[1:], F32)
    order = range(size) if forward else range(size - 1, -1, -1)
    for at in order:
        sums[at] = held.astype(BF16)
        held = got[at].astype(F32) + dot_tn(keeps[at], third) * held
    back = copies(sums, out, back_sems)
    for one in back:
        one.start()
    out[me] = sums[me]
    for tick in range(3, ticks):
        step_on(tick)
    for one in back:
        one.wait_recv()
    for one in factors + states + back:
        one.wait_send()
    if hosts:
        end()


def exchange_states(local, keep, sizes, forward, parts=()):
    _, hs, ts = sizes
    size = hs * ts
    inner, state = local.shape
    blocks = (size, inner // size, state)
    whole = pl.BlockSpec(memory_space=pltpu.VMEM)
    anywhere = pl.BlockSpec(memory_space=pl.ANY)
    pair = pltpu.SemaphoreType.DMA((2, size))
    chunks, scratch = [], []
    if parts:
        count = parts[0].shape[3]
        chunks = row_chunks(count, 0, 1, count // CHUNK_ROWS)
        scratch = reducer_scratch(sizes, chunks, parts)
    out = pl.pallas_call(
        functools.partial(exchange_kernel, sizes, forward, chunks),
        out_shape=[jax.ShapeDtypeStruct(blocks, BF16)]
        + [jax.ShapeDtypeStruct(part.shape[3:], F32) for part in parts],
        in_specs=[whole, whole] + [anywhere] * len(parts),
        out_specs=[whole] * (1 + len(parts)),
        scratch_shapes=[
            pltpu.VMEM(blocks, BF16),
            pltpu.VMEM(keep.shape, BF16),
            pltpu.VMEM(blocks, BF16),
            pair,
            pair,
            pair,
        ]
        + scratch,
        compiler_params=pltpu.CompilerParams(
            collective_id=2 if forward else 3, has_side_effects=True, vmem_limit_bytes=VMEM_BYTES
        ),
        cost_estimate=busy(60),
    )(local.reshape(blocks), keep, *parts)
    return (out[0].reshape(inner, state),) + tuple(out[1:])


def group_of(cols):
    return 1 if cols % 128 == 0 else 128 // cols if 128 % cols == 0 else 2


def busy(microseconds):
    return pl.CostEstimate(flops=microseconds * 900_000_000, bytes_accessed=0, transcendentals=0)


def remote_params(collective):
    return pltpu.CompilerParams(
        collective_id=collective, has_side_effects=True, vmem_limit_bytes=VMEM_BYTES
    )


def local_params():
    return pltpu.CompilerParams(vmem_limit_bytes=VMEM_BYTES)


def silu_of(v):
    return v * jax.nn.sigmoid(v)


def dot_nt(left, right):
    return lax.dot_general(left, right, (((1,), (1,)), ((), ())), preferred_element_type=F32)


def dot_tn(left, right):
    return lax.dot_general(left, right, (((0,), (0,)), ((), ())), preferred_element_type=F32)


def dot_nn(left, right):
    return jnp.dot(left, right, preferred_element_type=F32)


def dot_exact(left, right):
    return jnp.dot(left, right, preferred_element_type=F32, precision=HIGHEST)


def thirds(v):
    high = v.astype(BF16)
    rest = v - high.astype(F32)
    middle = rest.astype(BF16)
    return high, middle, (rest - middle.astype(F32)).astype(BF16)


def places(shape):
    return lax.broadcasted_iota(jnp.int32, shape, 0), lax.broadcasted_iota(jnp.int32, shape, 1)


def one_hot(hit):
    return hit.astype(F32).astype(BF16)


def tiles(count, step=32):
    return [slice(at, min(at + step, count)) for at in range(0, count, step)]


def moved(rows, by):
    return slice(rows.start + by, rows.stop + by)


def conv_pre(ext_ref, taps_ref, same_ref, rows, width):
    total = taps_ref[width : width + 1] + taps_ref[width - 1 : width] * ext_ref[moved(rows, HALO)]
    for back in range(1, width):
        total = total + (
            taps_ref[width - 1 - back : width - back]
            * ext_ref[moved(rows, HALO - back)]
            * same_ref[moved(rows, HALO), back - 1 : back]
        )
    return total


def lane_masks():
    lane = lax.broadcasted_iota(jnp.int32, (1, 128), 1)
    first = (lane < 64).astype(F32)
    return first, 1.0 - first


def two_apart(pair, masks):
    return jnp.concatenate([pair * masks[0].astype(BF16), pair * masks[1].astype(BF16)], 0)


def decay_pair(cum_ref, cumt_ref, bias, rows, pair):
    parts = []
    for head in (2 * pair, 2 * pair + 1):
        spread = cum_ref[0, rows, head : head + 1] - cumt_ref[0, head : head + 1, rows] + bias
        parts.append(jnp.exp(spread))
    return parts


class Scan:
    def __init__(self, own, sizes, rows, cols, heads_own, taps):
        self.own, self.ext, self.taps = own, own + HALO, taps
        self.dps, self.hts = 2 * sizes[0], sizes[1] * sizes[2]
        self.rows, self.cols = rows, cols
        self.group = group_of(cols)
        self.wide = self.group * cols
        self.heads = self.group * heads_own
        self.groups = self.hts // self.group
        self.chunks = own // CHUNK
        self.width = self.dps * rows
        self.inner = self.hts * cols
        self.pairs = self.wide // 128

    def call(self, kernel, ins, outs, scratch=(), collective=None):
        arrays = [array for array, _ in ins]
        return pl.pallas_call(
            kernel,
            grid=(self.groups,),
            out_shape=[shape for shape, _ in outs],
            in_specs=[spec for _, spec in ins],
            out_specs=[spec for _, spec in outs],
            scratch_shapes=list(scratch),
            compiler_params=local_params() if collective is None else remote_params(collective),
            cost_estimate=busy(22),
        )(*arrays)

    def full(self, array):
        mode = None if isinstance(array, jax.ShapeDtypeStruct) else pl.Buffered(1)
        return (array, pl.BlockSpec(array.shape, lambda j: (0,) * array.ndim, pipeline_mode=mode))

    def pieces(self, array):
        block = (self.dps, self.group, self.rows, self.cols)
        return (array, pl.BlockSpec(block, lambda j: (0, j, 0, 0)))

    def lanes(self, array):
        lead = array.shape[:-1]
        return (array, pl.BlockSpec(lead + (self.wide,), lambda j: (0,) * len(lead) + (j,)))

    def states(self, array):
        lead = array.shape[:-2]
        block = lead + (self.wide, array.shape[-1])
        return (array, pl.BlockSpec(block, lambda j: (0,) * len(lead) + (j, 0)))

    def grouped(self, array):
        block = (1,) + array.shape[1:]
        return (array, pl.BlockSpec(block, lambda j: (j,) + (0,) * (array.ndim - 1)))

    def project(self, rows_ref, piece_ref, out_ref):
        for one in range(self.group):
            weights = piece_ref[:, one].reshape(self.width, self.cols)
            out_ref[:, one * self.cols : (one + 1) * self.cols] = dot_nn(rows_ref, weights)

    def project_back(self, value_ref, piece_ref, out_ref):
        @pl.when(pl.program_id(0) == 0)
        def _():
            out_ref[...] = jnp.zeros_like(out_ref)

        for one in range(self.group):
            weights = piece_ref[:, one].reshape(self.width, self.cols)
            out_ref[...] += dot_nt(value_ref[:, one * self.cols : (one + 1) * self.cols], weights)

    def chunk_rows(self, c):
        return slice(c * CHUNK, (c + 1) * CHUNK)

    def lane_sums(self, v):
        total = v[:, :128]
        for pair in range(1, self.pairs):
            total = total + v[:, pair * 128 : (pair + 1) * 128]
        return total

    def widen(self):
        count = self.heads * self.groups
        row, lane = places((3 * count, self.wide))
        row = row - jnp.where(row >= 2 * count, 2 * count, jnp.where(row >= count, count, 0))
        return one_hot(row == pl.program_id(0) * self.heads + lax.div(lane, 64))

    def heads_of(self):
        row, lane = places((self.wide, 128))
        return one_hot(lane == pl.program_id(0) * self.heads + lax.div(row, 64))

    def keep_columns(self, keep_ref, widen):
        return dot_tn(widen, keep_ref[...])

    def halves(self, v):
        high = v.astype(BF16)
        return high, (v - high.astype(F32)).astype(BF16)

    def head_sums(self, v, heads_of):
        high, low = self.halves(v)
        return dot_nn(high, heads_of) + dot_nn(low, heads_of)

    def gradient(self, left_ref, value_ref, out_ref):
        for at in range(self.dps):
            for one in range(self.group):
                value = value_ref[:, one * self.cols : (one + 1) * self.cols]
                out_ref[at, one] = dot_nn(left_ref[at], value).astype(BF16)

    def piece_shape(self):
        return jax.ShapeDtypeStruct((self.dps, self.hts, self.rows, self.cols), BF16)

    def s1(self, normed, w_x, conv_rows, same, dt3, tail3, cum_g, cumt_g, coupling, bias, bc, keep3):
        own, state = self.own, bc.shape[1] // 2

        def kernel(
            normed_ref, w_ref, conv_ref, same_ref, dt_ref, tail_ref, cum_ref, cumt_ref,
            coupling_ref, bias_ref, bc_ref, keep_ref, ext_ref, x_ref, within_ref, added_ref, local_ref, xd_ref, xt_ref,
            dtw_ref, tailw_ref,
        ):
            self.project(normed_ref[...], w_ref, ext_ref)
            widen = self.widen()
            keep = self.keep_columns(keep_ref, widen)
            dtw_ref[...] = dot_nn(dt_ref[...], widen)
            tailw_ref[...] = dot_nn(tail_ref[...], widen)
            for rows in tiles(own):
                x = silu_of(conv_pre(ext_ref, conv_ref, same_ref, rows, self.taps))
                x_ref[rows] = x
                xd = x * dtw_ref[rows]
                xd_ref[rows] = xd.astype(BF16)
                xt_ref[rows] = (xd * tailw_ref[rows]).astype(BF16)
            masks = lane_masks()
            held = None
            for c in range(self.chunks):
                rows = self.chunk_rows(c)
                for pair in range(self.pairs):
                    lanes = slice(pair * 128, (pair + 1) * 128)
                    first, second = decay_pair(cum_ref, cumt_ref, bias_ref[c], rows, pair)
                    mix = coupling_ref[c]
                    kernel16 = jnp.concatenate([(first * mix).astype(BF16), (second * mix).astype(BF16)], 1)
                    within_ref[rows, lanes] = dot_nn(kernel16, two_apart(xd_ref[rows, lanes], masks))
                added = dot_tn(xt_ref[rows], bc_ref[rows, :state])
                added_ref[c] = added
                held = added if held is None else added + keep[:, c : c + 1] * held
            local_ref[...] = held.astype(BF16)

        f = jax.ShapeDtypeStruct
        return self.call(
            kernel,
            [
                self.full(normed), self.pieces(w_x), self.lanes(conv_rows), self.full(same), self.full(dt3),
                self.full(tail3), self.grouped(cum_g), self.grouped(cumt_g),
                self.full(coupling), self.full(bias), self.full(bc), self.full(keep3),
            ],
            [
                self.lanes(f((self.ext, self.inner), F32)), self.lanes(f((own, self.inner), F32)),
                self.lanes(f((own, self.inner), F32)), self.states(f((self.chunks, self.inner, state), F32)),
                self.states(f((self.inner, state), BF16)),
            ],
            [pltpu.VMEM((own, self.wide), BF16)] * 2 + [pltpu.VMEM((own, self.wide), F32)] * 2,
        )

    def s2(self, normed_own, w_z, within, x, skip_rows, entry3, bc, entering, added, keep3):
        own, state = self.own, bc.shape[1] // 2

        def kernel(
            normed_ref, w_ref, within_ref, x_ref, skip_ref, entry_ref, bc_ref, entering_ref,
            added_ref, keep_ref, z_ref, y_ref, states_ref, squares_ref, entry_wide_ref, carried_ref,
        ):
            self.project(normed_ref[...], w_ref, z_ref)
            widen = self.widen()
            keep = self.keep_columns(keep_ref, widen)
            entry_wide_ref[...] = dot_nn(entry_ref[...], widen)
            held = entering_ref[...].astype(F32)
            for c in range(self.chunks):
                rows = self.chunk_rows(c)
                held16 = held.astype(BF16)
                states_ref[c] = held16
                carried_ref[rows] = dot_nt(bc_ref[rows, state:], held16)
                if c + 1 < self.chunks:
                    held = added_ref[c] + keep[:, c : c + 1] * held

            @pl.when(pl.program_id(0) == 0)
            def _():
                squares_ref[...] = jnp.zeros_like(squares_ref)

            for rows in tiles(own):
                y = within_ref[rows] + carried_ref[rows] * entry_wide_ref[rows] + skip_ref[...] * x_ref[rows]
                y_ref[rows] = y
                gated = y * silu_of(z_ref[rows])
                squares_ref[rows] += self.lane_sums(gated * gated)

        f = jax.ShapeDtypeStruct
        return self.call(
            kernel,
            [
                self.full(normed_own), self.pieces(w_z), self.lanes(within), self.lanes(x), self.lanes(skip_rows),
                self.full(entry3), self.full(bc), self.states(entering), self.states(added),
                self.full(keep3),
            ],
            [
                self.lanes(f((own, self.inner), F32)), self.lanes(f((own, self.inner), F32)),
                self.states(f((self.chunks, self.inner, state), BF16)), self.full(f((own, 128), F32)),
            ],
            [pltpu.VMEM((own, self.wide), F32)] * 2,
        )

    def inv_gate(self, squares_ref, rows):
        return lax.rsqrt(jnp.sum(squares_ref[rows], axis=1, keepdims=True) / self.inner + EPSILON)

    def s3(self, y, z, squares, gain_row, w_o, cotangent, residual, cot_left):
        own = self.own

        def kernel(
            y_ref, z_ref, squares_ref, gain_ref, w_ref, cot_ref, residual_ref, left_ref,
            grad_ref, cross_ref, gain_grad_ref, out_ref, pieces_ref, gated_ref, sum_ref, normal_ref,
        ):
            for rows in tiles(own):
                normal = y_ref[rows] * silu_of(z_ref[rows]) * self.inv_gate(squares_ref, rows)
                normal_ref[rows] = normal
                gated_ref[rows] = (normal * gain_ref[...]).astype(BF16)
            self.project_back(gated_ref, w_ref, sum_ref)
            self.gradient(left_ref, gated_ref, pieces_ref)
            self.project(cot_ref[...], w_ref, grad_ref)

            @pl.when(pl.program_id(0) == 0)
            def _():
                cross_ref[...] = jnp.zeros_like(cross_ref)

            gain_grad = None
            for rows in tiles(own):
                product = grad_ref[rows] * normal_ref[rows]
                summed = jnp.sum(product, axis=0, keepdims=True)
                gain_grad = summed if gain_grad is None else gain_grad + summed
                cross_ref[rows] += self.lane_sums(product * gain_ref[...])
            gain_grad_ref[...] = jnp.broadcast_to(gain_grad, gain_grad_ref.shape)

            @pl.when(pl.program_id(0) == self.groups - 1)
            def _():
                out_ref[...] = (residual_ref[...].astype(F32) + sum_ref[...]).astype(BF16)

        f = jax.ShapeDtypeStruct
        return self.call(
            kernel,
            [
                self.lanes(y), self.lanes(z), self.full(squares), self.lanes(gain_row), self.pieces(w_o),
                self.full(cotangent), self.full(residual), self.full(cot_left),
            ],
            [
                self.lanes(f((own, self.inner), F32)), self.full(f((own, 128), F32)),
                self.lanes(f((8, self.inner), F32)), self.full(f((own, self.width), BF16)),
                self.pieces(self.piece_shape()),
            ],
            [
                pltpu.VMEM((own, self.wide), BF16), pltpu.VMEM((own, self.width), F32),
                pltpu.VMEM((own, self.wide), F32),
            ],
        )

    def s4(self, y, z, squares, cross, gain_row, grad_gate, w_z, entry3, bc, keep3, left):
        own, state = self.own, bc.shape[1] // 2

        def kernel(
            y_ref, z_ref, squares_ref, cross_ref, gain_ref, grad_ref, w_ref, entry_ref, bc_ref,
            keep_ref, left_ref, dy_ref, back_ref, local_ref, through_ref, pieces_ref, low_ref, dye_ref,
            entry_wide_ref,
        ):
            widen = self.widen()
            keep = self.keep_columns(keep_ref, widen)
            entry_wide_ref[...] = dot_nn(entry_ref[...], widen)
            for rows in tiles(own):
                inv = self.inv_gate(squares_ref, rows)
                cross_mean = jnp.sum(cross_ref[rows], axis=1, keepdims=True) / self.inner
                z = z_ref[rows]
                gate = jax.nn.sigmoid(z)
                z_gate = z * gate
                y = y_ref[rows]
                grad_gated = inv * (grad_ref[rows] * gain_ref[...]) - (y * z_gate) * (inv * inv * cross_mean)
                dy = grad_gated * z_gate
                dy_ref[rows] = dy
                low_ref[rows] = (grad_gated * y * (gate * (1.0 + z * (1.0 - gate)))).astype(BF16)
                dye_ref[rows] = (dy * entry_wide_ref[rows]).astype(BF16)
            self.project_back(low_ref, w_ref, through_ref)
            self.gradient(left_ref, low_ref, pieces_ref)
            held = None
            for c in range(self.chunks - 1, -1, -1):
                rows = self.chunk_rows(c)
                added = dot_tn(dye_ref[rows], bc_ref[rows, state:])
                back_ref[c] = added
                held = added if held is None else added + keep[:, c : c + 1] * held
            local_ref[...] = held.astype(BF16)

        f = jax.ShapeDtypeStruct
        return self.call(
            kernel,
            [
                self.lanes(y), self.lanes(z), self.full(squares), self.full(cross), self.lanes(gain_row),
                self.lanes(grad_gate), self.pieces(w_z), self.full(entry3), self.full(bc),
                self.full(keep3), self.full(left),
            ],
            [
                self.lanes(f((own, self.inner), F32)),
                self.states(f((self.chunks, self.inner, state), F32)), self.states(f((self.inner, state), BF16)),
                self.full(f((own, self.width), F32)), self.pieces(self.piece_shape()),
            ],
            [pltpu.VMEM((own, self.wide), BF16)] * 2 + [pltpu.VMEM((own, self.wide), F32)],
        )

    def s5(
        self, dy, x_ext, within, conv_rows, skip_rows, same, dt3, tail3, entry3, cum_g, cumt_g, coupling,
        bias, bc, states, leaving, back_added, keep3, w_x, left, others, sizes,
    ):
        own, state = self.own, bc.shape[1] // 2
        taps = self.taps
        xs, hs, ts = sizes
        others = [other.reshape((self.dps, hs, ts) + other.shape[2:]) for other in others]
        kinds = len(others)
        moving = row_chunks(self.rows, 0, kinds, self.rows // CHUNK_ROWS)
        buffers = reducer_scratch(sizes, moving, others)
        anywhere = pl.BlockSpec(memory_space=pl.ANY)

        def kernel(
            dy_ref, ext_ref, within_ref, conv_ref, skip_ref, same_ref, dt_ref, tail_ref, entry_ref,
            cum_ref, cumt_ref, coupling_ref, bias_ref, bc_ref, states_ref, leaving_ref, back_ref, keep_ref,
            w_ref, left_ref, *rest,
        ):
            other_refs, rest = rest[:kinds], rest[kinds:]
            rows_ref, head_ref, dots_ref, dbc_ref, dmix_ref, through_ref, pieces_ref = rest[:7]
            sum_refs, rest = rest[7 : 7 + kinds], rest[7 + kinds :]
            low_ref, xd_ref, xt_ref, dy16_ref, dye_ref, halves_ref, shift_ref, dxd_ref = rest[:8]
            dtw_ref, tailw_ref, pre_ref, spread_ref, carried_ref = rest[8:13]
            bufs = rest[13:]
            x_at, core, head, tensor = coordinates()

            def put(kind, start, length, value):
                sum_refs[kind][start : start + length, :] = value

            begin, step_on, end, ticks = reducer(
                sizes, moving, other_refs, bufs[:-3], bufs[-3:], put, HOSTED_LAGS
            )

            def scatter_on(slot):
                for step in range(self.groups):
                    if slot < SLOTS and SLOTS * step + slot < ticks:

                        @pl.when(pl.program_id(0) == step)
                        def _(at=SLOTS * step + slot):
                            step_on(at)

            @pl.when(pl.program_id(0) == 0)
            def _():
                begin(True)
                enter_kernel(x_at, core, head, tensor, xs, hs, ts, True)
                begin(False)

            first_step = pl.program_id(0) == 0

            @pl.when(first_step)
            def _():
                dbc_ref[...] = jnp.zeros_like(dbc_ref)
                dmix_ref[...] = jnp.zeros_like(dmix_ref)
                head_ref[...] = jnp.zeros_like(head_ref)
                dots_ref[...] = jnp.zeros_like(dots_ref)

            widen, heads_of = self.widen(), self.heads_of()
            keep = self.keep_columns(keep_ref, widen)
            dtw_ref[...] = dot_nn(dt_ref[...], widen)
            tailw_ref[...] = dot_nn(tail_ref[...], widen)
            spread_ref[...] = dot_nn(entry_ref[...], widen)
            for rows in tiles(own):
                pre = conv_pre(ext_ref, conv_ref, same_ref, rows, taps)
                pre_ref[rows] = pre
                xd = silu_of(pre) * dtw_ref[rows]
                xd_ref[rows] = xd.astype(BF16)
                xt_ref[rows] = (xd * tailw_ref[rows]).astype(BF16)
                dy = dy_ref[rows]
                dy16_ref[rows] = dy.astype(BF16)
                dye_ref[rows] = (dy * spread_ref[rows]).astype(BF16)
            scatter_on(0)
            masks = lane_masks()
            held = leaving_ref[...].astype(F32)
            for c in range(self.chunks - 1, -1, -1):
                rows = self.chunk_rows(c)
                held16 = held.astype(BF16)
                into16 = states_ref[c]
                product = held * into16.astype(F32)
                high, low = self.halves(product)
                dots_ref[c] += dot_tn(high, heads_of) + dot_tn(low, heads_of)
                spread_ref[rows] = dot_nt(bc_ref[rows, :state], held16)
                carried_ref[rows] = dot_nt(bc_ref[rows, state:], into16)
                dmix = dmix_ref[c]
                for pair in range(self.pairs):
                    lanes = slice(pair * 128, (pair + 1) * 128)
                    first, second = decay_pair(cum_ref, cumt_ref, bias_ref[c], rows, pair)
                    mix = coupling_ref[c]
                    kernel16 = jnp.concatenate([(first * mix).astype(BF16), (second * mix).astype(BF16)], 1)
                    dy_pair = dy16_ref[rows, lanes]
                    both = dot_tn(kernel16, dy_pair)
                    dxd_ref[rows, lanes] = both[:CHUNK] * masks[0] + both[CHUNK:] * masks[1]
                    dkernel = dot_nt(dy_pair, two_apart(xd_ref[rows, lanes], masks))
                    dmix = dmix + dkernel[:, :CHUNK] * first + dkernel[:, CHUNK:] * second
                dmix_ref[c] = dmix
                dbc_ref[rows, :state] += dot_nn(xt_ref[rows], held16)
                dbc_ref[rows, state:] += dot_nn(dye_ref[rows], into16)
                if c > 0:
                    held = back_ref[c] + keep[:, c : c + 1] * held
            scatter_on(1)
            halves = (
                (dy16_ref, dye_ref), (xd_ref, xt_ref), (low_ref.at[:own], halves_ref),
            )
            shift_ref[:HALO] = jnp.zeros((HALO, self.wide), F32)
            shift_ref[HALO + own :] = jnp.zeros((HALO, self.wide), F32)
            sums = [None] * (taps + 2)

            def add_to(at, v):
                v = jnp.sum(v, axis=0, keepdims=True)
                sums[at] = v if sums[at] is None else sums[at] + v

            for rows in tiles(own):
                dxd_within = dxd_ref[rows]
                falls = (
                    dy16_ref[rows].astype(F32) * within_ref[rows]
                    + dye_ref[rows].astype(F32) * carried_ref[rows]
                    - xd_ref[rows].astype(F32) * dxd_within
                )
                dxd = dxd_within + tailw_ref[rows] * spread_ref[rows]
                pre, dy = pre_ref[rows], dy_ref[rows]
                gate = jax.nn.sigmoid(pre)
                x = pre * gate
                rises = xt_ref[rows].astype(F32) * spread_ref[rows]
                for part, (high_ref, low_part_ref) in zip((falls, rises, x * dxd), halves):
                    high_ref[rows], low_part_ref[rows] = self.halves(part)
                slope = gate * (1.0 + pre * (1.0 - gate))
                grad = (dxd * dtw_ref[rows] + skip_ref[...] * dy) * slope
                shift_ref[moved(rows, HALO)] = grad
                add_to(taps, grad)
                add_to(taps + 1, dy * x)
                add_to(taps - 1, grad * ext_ref[moved(rows, HALO)])
                for back in range(1, taps):
                    masked = grad * same_ref[moved(rows, HALO), back - 1 : back]
                    add_to(taps - 1 - back, masked * ext_ref[moved(rows, HALO - back)])
            for at in range(taps + 2):
                rows_ref[at : at + 1] = sums[at]
            for at, (high_ref, low_part_ref) in enumerate(halves):
                head_ref[at] += dot_nn(high_ref[...], heads_of) + dot_nn(low_part_ref[...], heads_of)
            for rows in tiles(own + HALO):
                total = conv_ref[taps - 1 : taps] * shift_ref[rows]
                for back in range(1, taps):
                    total = total + (
                        conv_ref[taps - 1 - back : taps - back]
                        * shift_ref[moved(rows, back)]
                        * same_ref[moved(rows, back), back - 1 : back]
                    )
                low_ref[rows] = total.astype(BF16)
            scatter_on(2)
            self.project_back(low_ref, w_ref, through_ref)
            self.gradient(left_ref, low_ref, pieces_ref)

            @pl.when(pl.program_id(0) == self.groups - 1)
            def _():
                for at in range(SLOTS * self.groups, ticks):
                    step_on(at)
                end()

        f = jax.ShapeDtypeStruct
        scratch16 = pltpu.VMEM((own, self.wide), BF16)
        return self.call(
            kernel,
            [
                self.lanes(dy), self.lanes(x_ext), self.lanes(within), self.lanes(conv_rows), self.lanes(skip_rows),
                self.full(same), self.full(dt3), self.full(tail3), self.full(entry3),
                self.grouped(cum_g), self.grouped(cumt_g), self.full(coupling), self.full(bias),
                self.full(bc), self.states(states), self.states(leaving), self.states(back_added),
                self.full(keep3), self.pieces(w_x), self.full(left),
            ]
            + [(other, anywhere) for other in others],
            [
                self.lanes(f((8, self.inner), F32)), self.full(f((3, own, 128), F32)),
                self.full(f((self.chunks, state, 128), F32)),
                self.full(f((own, 2 * state), F32)), self.full(f((self.chunks, CHUNK, CHUNK), F32)),
                self.full(f((self.ext, self.width), F32)), self.pieces(self.piece_shape()),
            ]
            + [self.full(f((self.rows, self.cols), F32))] * kinds,
            [
                pltpu.VMEM((self.ext, self.wide), BF16), scratch16, scratch16, scratch16, scratch16,
                pltpu.VMEM((own, self.wide), BF16), pltpu.VMEM((own + 2 * HALO, self.wide), F32),
            ]
            + [pltpu.VMEM((own, self.wide), F32)] * 6
            + buffers,
            4,
        )

    def alone(self, kernel, ins, outs, scratch, microseconds):
        whole = pl.BlockSpec(memory_space=pltpu.VMEM)
        return pl.pallas_call(
            kernel,
            out_shape=outs,
            in_specs=[whole] * len(ins),
            out_specs=[whole] * len(outs),
            scratch_shapes=scratch,
            compiler_params=local_params(),
            cost_estimate=busy(microseconds),
        )(*ins)

    def prepare(self, normed, cotangent, side, seg_col, seg_row, bc_rows, head_rows, bc_cols, heads_own):
        own, taps, chunks = self.own, self.taps, self.chunks
        heads = heads_own * self.hts
        state2 = bc_cols * self.hts
        state = state2 // 2
        wide = self.hts * side.shape[2]

        def kernel(
            normed_ref, cot_ref, side_ref, seg_ref, segr_ref, bcw_ref, headw_ref,
            ext_left_ref, own_left_ref, cot_left_ref, w_ref, bce_ref, bc_ref, same_ref, dt_ref, sig_ref, cum_ref, cumt_ref, dt3_ref, tail3_ref, entry3_ref,
            keep_ref, keep3_ref, send_ref, mix_ref, bias_ref, raw_ref,
        ):
            row, lane = places((heads, self.hts * 16))
            pick = one_hot(lane == lax.div(row, heads_own) * 16 + lax.rem(row, heads_own))
            w_ref[...] = jnp.zeros_like(w_ref)
            for at in range(self.dps):
                cols = slice(at * self.rows, (at + 1) * self.rows)
                ext_left_ref[at] = normed_ref[:, cols].T
                own_left_ref[at] = normed_ref[HALO:, cols].T
                cot_left_ref[at] = cot_ref[:, cols].T
            for at in range(self.dps):
                cols = slice(at * self.rows, (at + 1) * self.rows)
                for one in range(self.hts):
                    w_ref[one * bc_cols : (one + 1) * bc_cols, cols] = side_ref[at, one, :bc_cols]
                padded = jnp.concatenate(
                    [side_ref[at, one, bc_cols : bc_cols + 16] for one in range(self.hts)], 0
                )
                w_ref[state2 : state2 + heads, cols] = dot_nn(pick, padded).astype(BF16)
            bce_ref[...] = dot_nt(normed_ref[...], w_ref[:state2])
            raw_ref[...] = dot_nt(normed_ref[HALO:], w_ref[state2 : state2 + 128])
            mine = seg_ref[HALO:]
            same_ref[...] = jnp.zeros_like(same_ref)
            for back in range(1, taps):
                hit = seg_ref[HALO - back : HALO - back + own] == mine
                same_ref[HALO : HALO + own, back - 1 : back] = hit.astype(F32)
            bc_ref[...] = silu_of(conv_pre(bce_ref, bcw_ref, same_ref, slice(0, own), taps)).astype(BF16)
            shifted = raw_ref[:, :heads] + headw_ref[0:1]
            dt = jnp.maximum(shifted, 0.0) + jnp.log1p(jnp.exp(-jnp.abs(shifted)))
            dt_ref[...] = dt
            sig_ref[...] = jax.nn.sigmoid(shifted)
            rate = -jnp.exp(headw_ref[1:2])
            row, lane = places((CHUNK, CHUNK))
            lower = row >= lane
            triangle = lower.astype(F32)

            def put_thirds(ref, rows, v):
                for at, part in enumerate(thirds(v)):
                    ref[rows, at * heads : (at + 1) * heads] = part

            put_thirds(dt3_ref, slice(0, own), dt)
            keep_all = None
            for c in range(chunks):
                rows = self.chunk_rows(c)
                seg = mine[rows]
                before = seg_ref[HALO + c * CHUNK - 1 : HALO + c * CHUNK]
                end = seg_ref[HALO + (c + 1) * CHUNK - 1 : HALO + (c + 1) * CHUNK]
                cum = dot_exact(triangle, dt_ref[rows] * rate)
                last = cum[CHUNK - 1 : CHUNK]
                put_thirds(tail3_ref, rows, jnp.exp(last - cum) * (seg == end).astype(F32))
                put_thirds(entry3_ref, rows, jnp.exp(cum) * (seg == before).astype(F32))
                keep = jnp.exp(last) * (before == end).astype(F32)
                keep_ref[c : c + 1] = keep
                keep_all = keep if keep_all is None else keep_all * keep
                flipped = cum.T
                for j in range(self.groups):
                    cum_ref[j, rows] = cum[:, j * self.heads : (j + 1) * self.heads]
                    cumt_ref[j, :, rows] = flipped[j * self.heads : (j + 1) * self.heads]
                mix_ref[c] = dot_nt(bc_ref[rows, state:], bc_ref[rows, :state])
                bias_ref[c] = jnp.where((seg == segr_ref[0:1, rows]) & lower, 0.0, MASKED)
            keep_ref[chunks:] = jnp.zeros((8 - chunks, heads), F32)
            for at, part in enumerate(thirds(keep_ref[...].T)):
                keep3_ref[at * heads : (at + 1) * heads] = part
            first, second, third = thirds(keep_all)
            row, _ = places((16, heads))
            stacked = jnp.where(
                row == 0,
                first.astype(F32),
                jnp.where(row == 1, second.astype(F32), jnp.where(row == 2, third.astype(F32), 0.0)),
            ).astype(BF16)
            row, lane = places((heads, self.cols))
            for one in range(self.hts):
                spread = one_hot(row == one * heads_own + lax.div(lane, 64))
                send_ref[one] = dot_nn(stacked, spread).astype(BF16)

        f = jax.ShapeDtypeStruct
        return self.alone(
            kernel,
            [normed, cotangent, side, seg_col, seg_row, bc_rows, head_rows],
            [
                f((self.dps, self.rows, self.ext), BF16), f((self.dps, self.rows, own), BF16),
                f((self.dps, self.rows, own), BF16),
                f((wide, self.width), BF16), f((self.ext, state2), F32), f((own, state2), BF16), f((own + 2 * HALO, 8), F32),
                f((own, heads), F32), f((own, heads), F32), f((self.groups, own, self.heads), F32),
                f((self.groups, self.heads, own), F32), f((own, 3 * heads), BF16), f((own, 3 * heads), BF16),
                f((own, 3 * heads), BF16), f((8, heads), F32), f((3 * heads, 8), BF16),
                f((self.hts, 16, self.cols), BF16), f((chunks, CHUNK, CHUNK), F32), f((chunks, CHUNK, CHUNK), F32),
            ],
            [pltpu.VMEM((own, 128), F32)],
            10,
        )

    def finish(
        self, dbc, dmix, bc, bc_ext, bc_rows, same, head_sums, dots, keep, dt, sig, head_rows, w_side, through,
        own_part, normed,
    ):
        own, taps, chunks = self.own, self.taps, self.chunks
        heads = dt.shape[1]
        state2 = bc.shape[1]
        state = state2 // 2
        wide = w_side.shape[0]

        def kernel(
            dbc_ref, dmix_ref, bc_ref, bce_ref, bcw_ref, same_ref, sums_ref, dots_ref, keep_ref, dt_ref, sig_ref,
            headw_ref, w_ref, through_ref, own_ref, normed_ref,
            part_ref, halo_ref, taps_ref, heads_ref, pieces_ref, low_ref, shift_ref, full_ref,
        ):
            rate = -jnp.exp(headw_ref[1:2])
            row, lane = places((CHUNK, CHUNK))
            upper = (row <= lane).astype(F32)
            strict = (row > lane).astype(F32)
            low_ref[...] = jnp.zeros_like(low_ref)
            grad_shift = jnp.zeros((1, heads), F32)
            grad_log = jnp.zeros((1, heads), F32)
            for c in range(chunks):
                rows = self.chunk_rows(c)
                dmix16 = dmix_ref[c].astype(BF16)
                full_ref[rows, :state] = dbc_ref[rows, :state] + dot_tn(dmix16, bc_ref[rows, state:])
                full_ref[rows, state:] = dbc_ref[rows, state:] + dot_nn(dmix16, bc_ref[rows, :state])
                crossing = jnp.sum(dots_ref[c], axis=0, keepdims=True)[:, :heads]
                da = (
                    dot_exact(upper, sums_ref[0, rows, :heads])
                    + dot_exact(strict, sums_ref[1, rows, :heads])
                    + keep_ref[c : c + 1] * crossing
                )
                grad_log = grad_log + jnp.sum(dt_ref[rows] * da, axis=0, keepdims=True)
                ddt_raw = (sums_ref[2, rows, :heads] + rate * da) * sig_ref[rows]
                grad_shift = grad_shift + jnp.sum(ddt_raw, axis=0, keepdims=True)
                low_ref[HALO + c * CHUNK : HALO + (c + 1) * CHUNK, state2 : state2 + heads] = ddt_raw.astype(BF16)
            heads_ref[...] = jnp.zeros_like(heads_ref)
            heads_ref[0:1] = grad_shift
            heads_ref[1:2] = rate * grad_log
            pre = conv_pre(bce_ref, bcw_ref, same_ref, slice(0, own), taps)
            gate = jax.nn.sigmoid(pre)
            grad = full_ref[...] * (gate * (1.0 + pre * (1.0 - gate)))
            shift_ref[:HALO] = jnp.zeros((HALO, state2), F32)
            shift_ref[HALO + own :] = jnp.zeros((HALO, state2), F32)
            taps_ref[...] = jnp.zeros_like(taps_ref)
            taps_ref[taps : taps + 1] = jnp.sum(grad, axis=0, keepdims=True)
            total = None
            for back in range(taps):
                masked = grad if back == 0 else grad * same_ref[HALO : HALO + own, back - 1 : back]
                shift_ref[HALO : HALO + own] = masked
                piece = bcw_ref[taps - 1 - back : taps - back] * shift_ref[back : back + own + HALO]
                total = piece if total is None else total + piece
                taps_ref[taps - 1 - back : taps - back] = jnp.sum(
                    masked * bce_ref[HALO - back : HALO - back + own], axis=0, keepdims=True
                )
            low_ref[:, :state2] = total.astype(BF16)
            part = through_ref[...] + dot_nn(low_ref[...], w_ref[...])
            part_ref[...] = part[HALO:] + own_ref[...]
            halo_ref[...] = part[:HALO]
            for at in range(self.dps):
                cols = slice(at * self.rows, (at + 1) * self.rows)
                pieces_ref[at] = dot_tn(low_ref[...], normed_ref[:, cols]).astype(BF16)

        f = jax.ShapeDtypeStruct
        return self.alone(
            kernel,
            [
                dbc, dmix, bc, bc_ext, bc_rows, same, head_sums, dots, keep, dt, sig, head_rows, w_side, through,
                own_part, normed,
            ],
            [
                f((own, self.width), F32), f((HALO, self.width), F32), f((8, state2), F32), f((8, heads), F32),
                f((self.dps, wide, self.rows), BF16),
            ],
            [
                pltpu.VMEM((self.ext, wide), BF16), pltpu.VMEM((own + 2 * HALO, state2), F32),
                pltpu.VMEM((own, state2), F32),
            ],
            12,
        )


def from_earlier(values, distance, size):
    return lax.ppermute(values, SEQ, [(i, i + distance) for i in range(size - distance)])


def from_later(values, distance, size):
    return lax.ppermute(values, SEQ, [(i + distance, i) for i in range(size - distance)])


def body(
    residual,
    segment_ids,
    norm_in_gain,
    w_zx,
    w_bc,
    w_dt,
    conv_x_weight,
    conv_x_bias,
    conv_bc_weight,
    conv_bc_bias,
    dt_bias,
    a_log,
    d_skip,
    norm_gain,
    w_out,
    cotangent,
):
    own, width = residual.shape
    dp_size = lax.axis_size("dp")
    size = lax.axis_size(SEQ)
    place = lax.axis_index(SEQ)
    dp_rows, _, cols = w_zx.shape
    heads_own = w_dt.shape[1]
    inner = cols * size
    heads = heads_own * size
    state2 = w_bc.shape[1]
    bc_cols = state2 // size
    head_width = inner // heads

    sizes = (dp_size // 2, lax.axis_size("head"), lax.axis_size("tensor"))
    taps = conv_x_weight.shape[0]
    bc_own = lax.dynamic_slice_in_dim(w_bc, place * bc_cols, bc_cols, 1)
    side_part = jnp.concatenate([bc_own, w_dt], 1).T
    side_part = jnp.pad(side_part, ((0, bc_cols + 16 - side_part.shape[0]), (0, 0)))
    small_rows = [conv_x_weight, conv_x_bias[None], norm_gain[None]]
    head_rows = jnp.stack([dt_bias, a_log, d_skip])
    small = jnp.concatenate(small_rows + [jnp.pad(head_rows, ((0, 0), (0, cols - heads_own)))], 0)
    small = jnp.pad(small, ((0, 16 - small.shape[0]), (0, 0)))

    def gathered(part):
        full = lax.all_gather(part, ALL, axis=0, tiled=False)
        return full.reshape(dp_size, size, dp_rows, cols)

    rows_ext = jnp.concatenate([from_earlier(residual[-HALO:], 1, size), residual], 0).astype(F32)
    inv_ext = lax.rsqrt(jnp.mean(rows_ext * rows_ext, axis=1, keepdims=True) + EPSILON)
    normed = (rows_ext * inv_ext * norm_in_gain).astype(BF16)
    normed_own = normed[HALO:]
    rows_in, inv_rms = rows_ext[HALO:], inv_ext[HALO:]

    seg_all = jnp.pad(segment_ids[0], (HALO, 0), constant_values=-1).astype(F32)
    seg_ext = lax.dynamic_slice_in_dim(seg_all, place * own, own + HALO)
    seg_row = jnp.broadcast_to(seg_ext[None, HALO:], (8, own))
    bc_rows = jnp.concatenate([conv_bc_weight, conv_bc_bias[None]], 0)
    bc_rows = jnp.pad(bc_rows, ((0, 8 - bc_rows.shape[0]), (0, 0)))

    w_z = gathered(w_zx[:, 0])
    side_full, w_x, small_full = gather_weights([side_part, w_zx[:, 1]], small, sizes)
    w_out_later, small_full = lax.optimization_barrier((w_out, small_full))
    w_o = gathered(w_out_later)
    w_x = w_x.reshape(dp_size, size, dp_rows, cols)
    side_full = side_full.reshape(dp_size, size, bc_cols + 16, dp_rows)
    small_full = jnp.moveaxis(small_full.reshape(size, 16, cols), 0, 1)
    per_channel = small_full.reshape(16, inner)
    per_head = small_full[taps + 2 : taps + 5, :, :heads_own].reshape(3, heads)
    conv_rows = per_channel[:8]
    gain_row = per_channel[taps + 1 : taps + 2]
    head_rows = jnp.pad(per_head[:2], ((0, 6), (0, 0)))
    skip_rows = jnp.repeat(per_head[2], head_width)[None]

    scan = Scan(own, sizes, dp_rows, cols, heads_own, taps)
    (
        ext_left, own_left, cot_left, w_side, bc_ext, bc, same, dt, sig, cum_g, cumt_g, dt3, tail3, entry3, keep, keep3, keep_send, coupling, bias,
    ) = scan.prepare(normed, cotangent, side_full, seg_ext[:, None], seg_row, bc_rows, head_rows, bc_cols, heads_own)
    x_ext, x, within, added, local = scan.s1(
        normed, w_x, conv_rows, same, dt3, tail3, cum_g, cumt_g, coupling, bias, bc, keep3
    )
    (entering,) = exchange_states(local, keep_send, sizes, True)
    z, y, states, squares = scan.s2(
        normed_own, w_z, within, x, skip_rows, entry3, bc, entering, added, keep3
    )
    grad_gate, cross, gain_rows, block_out, out_pieces = scan.s3(
        y, z, squares, gain_row, w_o, cotangent, residual, cot_left
    )
    dy, back_added, back_local, own_part, z_pieces = scan.s4(
        y, z, squares, cross, gain_row, grad_gate, w_z, entry3, bc, keep3, own_left
    )

    grid = (dp_size,) + sizes[1:]
    leaving, grad_wo = exchange_states(
        back_local, keep_send, sizes, False, (out_pieces.reshape(grid + (dp_rows, cols)),)
    )
    conv_sums, head_sums, dots, dbc, dmix, through, x_pieces, grad_wz = scan.s5(
        dy, x_ext, within, conv_rows, skip_rows, same, dt3, tail3, entry3, cum_g, cumt_g, coupling, bias, bc,
        states, leaving, back_added, keep3, w_x, ext_left,
        (z_pieces,), sizes
    )
    part, halo, bc_sums, scan_sums, side_pieces = scan.finish(
        dbc, dmix, bc, bc_ext, bc_rows, same, head_sums, dots, keep, dt, sig, head_rows, w_side, through, own_part,
        normed
    )

    grad_normed = part.at[own - HALO :].add(from_later(halo, 1, size))
    scaled_in = grad_normed * norm_in_gain
    input_grad = (
        cotangent.astype(F32)
        + inv_rms * scaled_in
        - rows_in * (inv_rms * inv_rms * inv_rms) * jnp.mean(scaled_in * rows_in, axis=1, keepdims=True)
    )
    grad_in_gain = jnp.sum(grad_normed * rows_in * inv_rms, axis=0)

    grad_skip = jnp.sum(conv_sums[taps + 1].reshape(heads, head_width), axis=1)
    head_sum = jnp.concatenate([scan_sums[0], scan_sums[1], grad_skip])
    row = jnp.concatenate([grad_in_gain, bc_sums[: taps + 1].reshape(-1)])
    small_sum = jnp.concatenate(
        [
            conv_sums[: taps + 1],
            gain_rows[:1],
            jnp.pad(row, (0, inner - row.shape[0]))[None],
            jnp.pad(head_sum, (0, inner - head_sum.shape[0]))[None],
        ],
        0,
    )
    grad_side, grad_wx, small_sum = scatter_gradients(
        [side_pieces.reshape(grid + (-1, dp_rows)), x_pieces.reshape(grid + (dp_rows, cols))], small_sum, sizes
    )
    grad_wzx = jnp.stack([grad_wz, grad_wx], 1)
    grad_side = grad_side.reshape(-1, dp_rows).astype(F32)
    grad_wbc = grad_side[:state2].T
    grad_wdt = lax.dynamic_slice_in_dim(grad_side, state2 + place * heads_own, heads_own, 0).T
    channel_own = lax.dynamic_slice_in_dim(small_sum[: taps + 2], place * cols, cols, 1)
    row = small_sum[taps + 2]
    gain_sum = row[:width]
    taps_sum = row[width : width + taps * state2].reshape(taps, state2)
    bias_sum = row[width + taps * state2 : width + (taps + 1) * state2]
    head_sum = small_sum[taps + 3, : 3 * heads].reshape(3, heads)
    head_own = lax.dynamic_slice_in_dim(head_sum, place * heads_own, heads_own, 1)
    return (
        block_out,
        input_grad,
        gain_sum,
        grad_wzx,
        grad_wbc,
        grad_wdt,
        channel_own[:taps],
        channel_own[taps],
        taps_sum,
        bias_sum,
        head_own[0],
        head_own[1],
        head_own[2],
        channel_own[taps + 1],
        grad_wo,
    )


def solution(mesh):
    rows = P(ALL, None)
    in_specs = (
        rows,
        P("dp", None),
        P(),
        P("dp", None, SEQ),
        P("dp", None),
        P("dp", SEQ),
        P(None, SEQ),
        P(SEQ),
        P(),
        P(),
        P(SEQ),
        P(SEQ),
        P(SEQ),
        P(SEQ),
        P("dp", SEQ),
        rows,
    )
    out_specs = (
        rows,
        rows,
        P(),
        P("dp", None, SEQ),
        P("dp", None),
        P("dp", SEQ),
        P(None, SEQ),
        P(SEQ),
        P(),
        P(),
        P(SEQ),
        P(SEQ),
        P(SEQ),
        P(SEQ),
        P("dp", SEQ),
    )
    return jax.shard_map(
        body, mesh=mesh, in_specs=in_specs, out_specs=out_specs, check_vma=False
    )
```

```python
import functools

import jax
import jax.numpy as jnp
from jax import lax
from jax.experimental import pallas as pl
from jax.experimental.pallas import tpu as pltpu
from jax.sharding import PartitionSpec as P

EPSILON = 1e-05
CHUNK = 128
HALO = 16
AHEAD = 4
LAGS = (0, 2, 4, 6)
HOSTED_LAGS = (0, 4, 6, 8)
SLOTS = 2
CHUNK_ROWS = 48
MASKED = -1e30
HIGHEST = lax.Precision.HIGHEST
SEQ = ("head", "tensor")
ALL = ("dp", "head", "tensor")
BF16 = jnp.bfloat16
F32 = jnp.float32
MESH = pl.DeviceIdType.MESH
VMEM_BYTES = 56 << 20


def coordinates():
    dp = lax.axis_index("dp")
    return lax.div(dp, 2), lax.rem(dp, 2), lax.axis_index("head"), lax.axis_index("tensor")


def enter_kernel(x, core, head, tensor, xs, hs, ts, sibling):
    barrier = pltpu.get_barrier_semaphore()
    count = 0
    for step in range(1, hs):
        pl.semaphore_signal(barrier, 1, device_id={"head": lax.rem(head + step, hs)}, device_id_type=MESH)
        count += 1
    for step in range(1, ts):
        pl.semaphore_signal(barrier, 1, device_id={"tensor": lax.rem(tensor + step, ts)}, device_id_type=MESH)
        count += 1
    for step in range(1, xs):
        other = 2 * lax.rem(x + step, xs) + core
        pl.semaphore_signal(barrier, 1, device_id={"dp": other}, device_id_type=MESH)
        count += 1
    if sibling:
        pl.semaphore_signal(barrier, 1, device_id={"dp": 2 * x + 1 - core}, device_id_type=MESH)
        count += 1
    pl.semaphore_wait(barrier, count)


def gatherer(sizes, chunks, parts, fulls, sems):
    xs, hs, ts = sizes
    send, recv, own_sem = sems
    x, core, head, tensor = coordinates()
    dp = 2 * x + core
    total = len(chunks)
    ahead = 4

    def own():
        return [
            pltpu.make_async_copy(part, full.at[dp, head, tensor], own_sem.at[kind])
            for kind, (part, full) in enumerate(zip(parts, fulls))
        ]

    def copy(src, dst, index, slot, device):
        return pltpu.make_async_remote_copy(
            src_ref=src,
            dst_ref=dst,
            send_sem=send.at[index, slot],
            recv_sem=recv.at[index, slot],
            device_id=device,
            device_id_type=MESH,
        )

    def along_head(index):
        kind, start, length, _ = chunks[index]
        rows = pl.ds(start, length)
        return [
            copy(
                parts[kind].at[rows],
                fulls[kind].at[dp, head, tensor, rows],
                index,
                step - 1,
                {"head": lax.rem(head + step, hs)},
            )
            for step in range(1, hs)
        ]

    def over(index, axis, second):
        kind, start, length, _ = chunks[index]
        rows = pl.ds(start, length)
        base = hs - 1 if second else hs - 1 + max(xs, ts)
        copies = []
        if axis == "tensor":
            homes = [dp] if second else [2 * home + core for home in range(xs)]
            for step in range(1, ts):
                for home in homes:
                    view = fulls[kind].at[home, :, tensor, rows]
                    device = {"tensor": lax.rem(tensor + step, ts)}
                    copies.append(copy(view, view, index, base + len(copies), device))
        else:
            for step in range(1, xs):
                view = fulls[kind].at[dp, :, tensor, rows] if second else fulls[kind].at[dp, :, :, rows]
                device = {"dp": 2 * lax.rem(x + step, xs) + core}
                copies.append(copy(view, view, index, base + len(copies), device))
        return copies

    def to_sibling(index):
        kind, start, length, _ = chunks[index]
        rows = pl.ds(start, length)
        base = hs - 1 + max(xs, ts) + max(xs, xs * ts)
        return [
            copy(
                fulls[kind].at[2 * home + core, :, :, rows],
                fulls[kind].at[2 * home + core, :, :, rows],
                index,
                base + home,
                {"dp": 2 * x + 1 - core},
            )
            for home in range(xs)
        ]

    def stage(index, number):
        tensor_first = chunks[index][3]
        if number == 0:
            return along_head(index)
        if number == 1:
            return over(index, "tensor" if tensor_first else "x", True)
        if number == 2:
            return over(index, "x" if tensor_first else "tensor", False)
        return to_sibling(index)

    def start(first):
        if first:
            for one in own():
                one.start()
        else:
            for index in range(min(ahead, total)):
                for one in stage(index, 0):
                    one.start()
            for one in own():
                one.wait()

    def tick(at):
        for number in range(4):
            index = at - 2 * number
            if 0 <= index < total:
                for one in stage(index, number):
                    one.wait_recv()
                if number < 3:
                    for one in stage(index, number + 1):
                        one.start()
                if number == 0 and index + ahead < total:
                    for one in stage(index + ahead, 0):
                        one.start()

    def end():
        for index in range(total):
            for number in range(4):
                for one in stage(index, number):
                    one.wait_send()

    return start, tick, end, total + 6


def gatherer_scratch(sizes, chunks, kinds):
    xs, hs, ts = sizes
    slots = hs - 1 + max(xs, ts) + max(xs, xs * ts) + xs
    return [
        pltpu.SemaphoreType.DMA((len(chunks), slots)),
        pltpu.SemaphoreType.DMA((len(chunks), slots)),
        pltpu.SemaphoreType.DMA((kinds,)),
    ]


def gather_kernel(sizes, chunks, kinds, *refs):
    xs, hs, ts = sizes
    parts, small = refs[:kinds], refs[kinds]
    fulls, small_full = refs[kinds + 1 : 2 * kinds + 1], refs[2 * kinds + 1]
    sems, rest = refs[2 * kinds + 2 : 2 * kinds + 5], refs[2 * kinds + 5 :]
    small_send, small_recv, small_own = rest
    x, core, head, tensor = coordinates()
    begin, step_on, end, ticks = gatherer(sizes, chunks, parts, fulls, sems)
    begin(True)
    own_small = pltpu.make_async_copy(small, small_full.at[head, tensor], small_own.at[0])
    own_small.start()
    enter_kernel(x, core, head, tensor, xs, hs, ts, True)
    small_tensor = [
        pltpu.make_async_remote_copy(
            src_ref=small,
            dst_ref=small_full.at[head, tensor],
            send_sem=small_send.at[step - 1],
            recv_sem=small_recv.at[step - 1],
            device_id={"tensor": lax.rem(tensor + step, ts)},
            device_id_type=MESH,
        )
        for step in range(1, ts)
    ]
    small_head = [
        pltpu.make_async_remote_copy(
            src_ref=small_full.at[head],
            dst_ref=small_full.at[head],
            send_sem=small_send.at[ts + step - 2],
            recv_sem=small_recv.at[ts + step - 2],
            device_id={"head": lax.rem(head + step, hs)},
            device_id_type=MESH,
        )
        for step in range(1, hs)
    ]
    for one in small_tensor:
        one.start()
    begin(False)
    own_small.wait()
    for one in small_tensor:
        one.wait_recv()
    for one in small_head:
        one.start()
    for tick in range(ticks):
        step_on(tick)
    for one in small_head:
        one.wait_recv()
    for one in small_tensor + small_head:
        one.wait_send()
    end()


def row_chunks(rows, first, kinds, pieces):
    step = rows // pieces
    return [
        (kind, piece * step, step, piece % 2 == 1)
        for kind in range(first, kinds)
        for piece in range(pieces)
    ]


def gather_weights(parts, small, sizes):
    xs, hs, ts = sizes
    kinds = len(parts)
    count = parts[1].shape[0]
    chunks = [(0, 0, parts[0].shape[0], True)] + row_chunks(count, 1, kinds, count // CHUNK_ROWS)
    full = [jax.ShapeDtypeStruct((2 * xs, hs, ts) + part.shape, part.dtype) for part in parts]
    full.append(jax.ShapeDtypeStruct((hs, ts) + small.shape, small.dtype))
    anywhere = pl.BlockSpec(memory_space=pl.ANY)
    return pl.pallas_call(
        functools.partial(gather_kernel, sizes, chunks, kinds),
        out_shape=full,
        in_specs=[anywhere] * (kinds + 1),
        out_specs=[anywhere] * (kinds + 1),
        scratch_shapes=gatherer_scratch(sizes, chunks, kinds)
        + [
            pltpu.SemaphoreType.DMA((hs + ts,)),
            pltpu.SemaphoreType.DMA((hs + ts,)),
            pltpu.SemaphoreType.DMA((1,)),
        ],
        compiler_params=pltpu.CompilerParams(
            collective_id=0, has_side_effects=True, vmem_limit_bytes=VMEM_BYTES
        ),
        cost_estimate=busy(60),
    )(*parts, small)


def reducer(sizes, chunks, parts, bufs, sems, put, lags=LAGS):
    xs, hs, ts = sizes
    send, recv, own_sem = sems
    x, core, head, tensor = coordinates()
    total = len(chunks)

    def loads(index):
        kind, start, length, _ = chunks[index]
        rows = pl.ds(start, length)
        return [
            pltpu.make_async_copy(
                parts[kind].at[2 * home + core, :, :, rows],
                bufs[5 * index].at[home],
                own_sem.at[index, home],
            )
            for home in range(xs)
        ]

    def stage(index, number):
        kind, start, length, x_first = chunks[index]
        rows = pl.ds(start, length)
        held = bufs[5 * index]
        into = bufs[5 * index + 1 + number]
        slots = (0, xs, xs + max(xs, ts) - 1, xs + 2 * (max(xs, ts) - 1))
        by_x = [
            (lax.rem(x + step, xs), {"dp": 2 * lax.rem(x + step, xs) + core}) for step in range(1, xs)
        ]
        by_tensor = [
            (lax.rem(tensor + step, ts), {"tensor": lax.rem(tensor + step, ts)}) for step in range(1, ts)
        ]
        if number == 0:
            moves = [
                (parts[kind].at[2 * home + 1 - core, :, :, rows], into.at[home], {"dp": 2 * x + 1 - core})
                for home in range(xs)
            ]
        elif number == 1 and x_first:
            moves = [(held.at[to], into.at[at], device) for at, (to, device) in enumerate(by_x)]
        elif number == 1:
            moves = [(held.at[:, :, to], into.at[at], device) for at, (to, device) in enumerate(by_tensor)]
        elif number == 2 and x_first:
            moves = [(held.at[x, :, to], into.at[at], device) for at, (to, device) in enumerate(by_tensor)]
        elif number == 2:
            moves = [(held.at[to, :, tensor], into.at[at], device) for at, (to, device) in enumerate(by_x)]
        else:
            moves = []
            for step in range(1, hs):
                to = lax.rem(head + step, hs)
                moves.append((held.at[x, to, tensor], into.at[step - 1], {"head": to}))
        return [
            pltpu.make_async_remote_copy(
                src_ref=src,
                dst_ref=dst,
                send_sem=send.at[index, slots[number] + at],
                recv_sem=recv.at[index, slots[number] + at],
                device_id=device,
                device_id_type=MESH,
            )
            for at, (src, dst, device) in enumerate(moves)
        ]

    def add(index, number):
        kind, start, length, x_first = chunks[index]
        held = bufs[5 * index]
        into = bufs[5 * index + 1 + number]
        def plus(own, others):
            if len(others) == 1:
                return own + others[0]
            value = own.astype(F32)
            for one in others:
                value = value + one.astype(F32)
            return value.astype(BF16)

        if number == 0:

            @pl.loop(0, xs * hs)
            def _(both):
                one, two = lax.div(both, hs), lax.rem(both, hs)
                held[one, two] = plus(held[one, two], [into[one, two]])

        elif number == 1 and x_first:

            @pl.loop(0, hs)
            def _(one):
                held[x, one] = plus(held[x, one], [into[step, one] for step in range(xs - 1)])

        elif number == 1:

            @pl.loop(0, xs * hs)
            def _(both):
                one, two = lax.div(both, hs), lax.rem(both, hs)
                held[one, two, tensor] = plus(
                    held[one, two, tensor], [into[step, one, two] for step in range(ts - 1)]
                )

        elif number == 2:

            @pl.loop(0, hs)
            def _(one):
                held[x, one, tensor] = plus(
                    held[x, one, tensor], [into[step, one] for step in range(into.shape[0])]
                )

        else:
            value = held[x, head, tensor].astype(F32)
            for step in range(hs - 1):
                value = value + into[step].astype(F32)
            put(kind, start, length, value)

    def start(first):
        for index in range(total):
            if first:
                for one in loads(index):
                    one.start()
            elif index < AHEAD:
                for one in stage(index, 0):
                    one.start()

    def tick(at):
        for number, lag in enumerate(lags):
            index = at - lag
            if 0 <= index < total:
                for one in stage(index, number):
                    one.wait_recv()
                if number == 0:
                    if index + AHEAD < total:
                        for one in stage(index + AHEAD, 0):
                            one.start()
                    for one in loads(index):
                        one.wait()
                add(index, number)
                if number < 3:
                    for one in stage(index, number + 1):
                        one.start()

    def end():
        for index in range(total):
            for number in range(4):
                for one in stage(index, number):
                    one.wait_send()

    return start, tick, end, total + lags[3]


def reducer_scratch(sizes, chunks, parts):
    xs, hs, ts = sizes
    scratch = []
    for kind, _, length, x_first in chunks:
        block = (length, parts[kind].shape[4])
        kept = (hs, ts) if x_first else (xs, hs)
        near, far = (xs, ts) if x_first else (ts, xs)
        scratch += [
            pltpu.VMEM((xs, hs, ts) + block, BF16),
            pltpu.VMEM((xs, hs, ts) + block, BF16),
            pltpu.VMEM((near - 1,) + kept + block, BF16),
            pltpu.VMEM((far - 1, hs) + block, BF16),
            pltpu.VMEM((hs - 1,) + block, BF16),
        ]
    slots = xs + 2 * (max(xs, ts) - 1) + hs - 1
    return scratch + [
        pltpu.SemaphoreType.DMA((len(chunks), slots)),
        pltpu.SemaphoreType.DMA((len(chunks), slots)),
        pltpu.SemaphoreType.DMA((len(chunks), xs)),
    ]


def scatter_kernel(sizes, chunks, kinds, *refs):
    xs, hs, ts = sizes
    parts, small = refs[:kinds], refs[kinds]
    outs, small_out = refs[kinds + 1 : 2 * kinds + 1], refs[2 * kinds + 1]
    rest = refs[2 * kinds + 2 :]
    count = 5 * len(chunks)
    bufs, sems, rest = rest[:count], rest[count : count + 3], rest[count + 3 :]
    small_acc, small_in, small_send, small_recv, side_send, side_recv = rest
    x, core, head, tensor = coordinates()

    def put(kind, start, length, value):
        if kind == 0:
            outs[kind][head, tensor] = value.astype(BF16)
        else:
            outs[kind][start : start + length, :] = value

    begin, step_on, end, ticks = reducer(sizes, chunks, parts, bufs, sems, put)

    def side_copy(view, slot, device):
        return pltpu.make_async_remote_copy(
            src_ref=view,
            dst_ref=view,
            send_sem=side_send.at[slot],
            recv_sem=side_recv.at[slot],
            device_id=device,
            device_id_type=MESH,
        )

    side_tensor = [
        side_copy(outs[0].at[head, tensor], step - 1, {"tensor": lax.rem(tensor + step, ts)})
        for step in range(1, ts)
    ]
    side_head = [
        side_copy(outs[0].at[head], ts + step - 2, {"head": lax.rem(head + step, hs)})
        for step in range(1, hs)
    ]
    small_slots = [1, xs - 1, ts - 1, hs - 1]
    small_base = [0, 1, xs, xs + ts - 1]

    def small_stage(number):
        copies = []
        for step in range(1, small_slots[number] + 1):
            slot = small_base[number] + step - 1
            device = (
                {"dp": 2 * x + 1 - core},
                {"dp": 2 * lax.rem(x + step, xs) + core},
                {"tensor": lax.rem(tensor + step, ts)},
                {"head": lax.rem(head + step, hs)},
            )[number]
            copies.append(
                pltpu.make_async_remote_copy(
                    src_ref=small if number == 0 else small_acc.at[number - 1],
                    dst_ref=small_in.at[slot],
                    send_sem=small_send.at[slot],
                    recv_sem=small_recv.at[slot],
                    device_id=device,
                    device_id_type=MESH,
                )
            )
        return copies

    def small_add(number):
        mine = small[...] if number == 0 else small_acc[number - 1]
        size = small_slots[number] + 1
        place = (core, x, tensor, head)[number]
        value = None
        for at in range(size):
            step = lax.rem(place - at + size, size)
            slot = small_base[number] + jnp.maximum(step - 1, 0)
            here = jnp.where(step == 0, mine, small_in[slot])
            value = here if value is None else value + here
        if number < 3:
            small_acc[number] = value
        else:
            small_out[...] = value

    begin(True)
    enter_kernel(x, core, head, tensor, xs, hs, ts, True)
    for one in small_stage(0):
        one.start()
    begin(False)
    for tick in range(max(ticks, LAGS[3] + 3)):
        step_on(tick)
        if tick == LAGS[3]:
            for one in side_tensor:
                one.start()
        if tick == LAGS[3] + 2:
            for one in side_tensor:
                one.wait_recv()
            for one in side_head:
                one.start()
        if tick in (0, 2, 4, 6):
            number = tick // 2
            for one in small_stage(number):
                one.wait_recv()
            small_add(number)
            if number < 3:
                for one in small_stage(number + 1):
                    one.start()
    for one in side_head:
        one.wait_recv()
    for one in side_tensor + side_head:
        one.wait_send()
    for number in range(4):
        for one in small_stage(number):
            one.wait_send()
    end()


def scatter_gradients(parts, small, sizes):
    xs, hs, ts = sizes
    kinds = len(parts)
    count = parts[1].shape[3]
    chunks = [(0, 0, parts[0].shape[3], True)] + row_chunks(count, 1, kinds, count // CHUNK_ROWS)
    small_slots = xs + ts + hs - 2
    anywhere = pl.BlockSpec(memory_space=pl.ANY)
    whole = pl.BlockSpec(memory_space=pltpu.VMEM)
    return pl.pallas_call(
        functools.partial(scatter_kernel, sizes, chunks, kinds),
        out_shape=[jax.ShapeDtypeStruct((hs, ts) + parts[0].shape[3:], BF16)]
        + [jax.ShapeDtypeStruct(part.shape[3:], F32) for part in parts[1:]]
        + [jax.ShapeDtypeStruct(small.shape, F32)],
        in_specs=[anywhere] * kinds + [whole],
        out_specs=[whole] * (kinds + 1),
        scratch_shapes=reducer_scratch(sizes, chunks, parts)
        + [
            pltpu.VMEM((3,) + small.shape, F32),
            pltpu.VMEM((small_slots,) + small.shape, F32),
            pltpu.SemaphoreType.DMA((small_slots,)),
            pltpu.SemaphoreType.DMA((small_slots,)),
            pltpu.SemaphoreType.DMA((hs + ts,)),
            pltpu.SemaphoreType.DMA((hs + ts,)),
        ],
        compiler_params=pltpu.CompilerParams(
            collective_id=1, has_side_effects=True, vmem_limit_bytes=VMEM_BYTES
        ),
        cost_estimate=busy(60),
    )(*parts, small)


def exchange_kernel(sizes, forward, chunks, *refs):
    xs, hs, ts = sizes
    size = hs * ts
    hosts = bool(chunks)
    local, keep = refs[:2]
    parts, out = refs[2 : 2 + hosts], refs[2 + hosts]
    outs, rest = refs[3 + hosts : 3 + 2 * hosts], refs[3 + 2 * hosts :]
    got, keeps, sums, sems, keep_sems, back_sems = rest[:6]
    x, core, head, tensor = coordinates()
    me = head * ts + tensor

    def put(kind, start, length, value):
        outs[kind][start : start + length, :] = value

    ticks = 0
    if hosts:
        begin, step_on, end, ticks = reducer(sizes, chunks, parts, rest[6:-3], rest[-3:], put)
        begin(True)
    barrier = pltpu.get_barrier_semaphore()
    peers = []
    for step in range(1, size):
        to = lax.rem(me + step, size)
        peers.append((to, {"head": lax.div(to, ts), "tensor": lax.rem(to, ts)}))
    others = [device for _, device in peers]
    if hosts:
        others += [{"dp": 2 * lax.rem(x + step, xs) + core} for step in range(1, xs)]
        others.append({"dp": 2 * x + 1 - core})
    for device in others:
        pl.semaphore_signal(barrier, 1, device_id=device, device_id_type=MESH)
    pl.semaphore_wait(barrier, len(others))

    def copies(src, dst, pair):
        return [
            pltpu.make_async_remote_copy(
                src_ref=src.at[to],
                dst_ref=dst.at[me],
                send_sem=pair.at[0, at],
                recv_sem=pair.at[1, at],
                device_id=device,
                device_id_type=MESH,
            )
            for at, (to, device) in enumerate(peers)
        ]

    factors = copies(keep, keeps, keep_sems)
    states = copies(local, got, sems)
    for one in factors + states:
        one.start()
    if hosts:
        begin(False)
    got[me] = local[me]
    keeps[me] = keep[me]
    for tick in range(min(3, ticks)):
        step_on(tick)
    for one in factors + states:
        one.wait_recv()
    third = lax.broadcasted_iota(jnp.int32, (keep.shape[1], local.shape[2]), 0) < 3
    third = third.astype(BF16)
    held = jnp.zeros(local.shape[1:], F32)
    order = range(size) if forward else range(size - 1, -1, -1)
    for at in order:
        sums[at] = held.astype(BF16)
        held = got[at].astype(F32) + dot_tn(keeps[at], third) * held
    back = copies(sums, out, back_sems)
    for one in back:
        one.start()
    out[me] = sums[me]
    for tick in range(3, ticks):
        step_on(tick)
    for one in back:
        one.wait_recv()
    for one in factors + states + back:
        one.wait_send()
    if hosts:
        end()


def exchange_states(local, keep, sizes, forward, parts=()):
    _, hs, ts = sizes
    size = hs * ts
    inner, state = local.shape
    blocks = (size, inner // size, state)
    whole = pl.BlockSpec(memory_space=pltpu.VMEM)
    anywhere = pl.BlockSpec(memory_space=pl.ANY)
    pair = pltpu.SemaphoreType.DMA((2, size))
    chunks, scratch = [], []
    if parts:
        count = parts[0].shape[3]
        chunks = row_chunks(count, 0, 1, count // CHUNK_ROWS)
        scratch = reducer_scratch(sizes, chunks, parts)
    out = pl.pallas_call(
        functools.partial(exchange_kernel, sizes, forward, chunks),
        out_shape=[jax.ShapeDtypeStruct(blocks, BF16)]
        + [jax.ShapeDtypeStruct(part.shape[3:], F32) for part in parts],
        in_specs=[whole, whole] + [anywhere] * len(parts),
        out_specs=[whole] * (1 + len(parts)),
        scratch_shapes=[
            pltpu.VMEM(blocks, BF16),
            pltpu.VMEM(keep.shape, BF16),
            pltpu.VMEM(blocks, BF16),
            pair,
            pair,
            pair,
        ]
        + scratch,
        compiler_params=pltpu.CompilerParams(
            collective_id=2 if forward else 3, has_side_effects=True, vmem_limit_bytes=VMEM_BYTES
        ),
        cost_estimate=busy(60),
    )(local.reshape(blocks), keep, *parts)
    return (out[0].reshape(inner, state),) + tuple(out[1:])


def group_of(cols):
    return 1 if cols % 128 == 0 else 128 // cols if 128 % cols == 0 else 2


def busy(microseconds):
    return pl.CostEstimate(flops=microseconds * 900_000_000, bytes_accessed=0, transcendentals=0)


def remote_params(collective):
    return pltpu.CompilerParams(
        collective_id=collective, has_side_effects=True, vmem_limit_bytes=VMEM_BYTES
    )


def local_params():
    return pltpu.CompilerParams(vmem_limit_bytes=VMEM_BYTES)


def silu_of(v):
    return v * jax.nn.sigmoid(v)


def dot_nt(left, right):
    return lax.dot_general(left, right, (((1,), (1,)), ((), ())), preferred_element_type=F32)


def dot_tn(left, right):
    return lax.dot_general(left, right, (((0,), (0,)), ((), ())), preferred_element_type=F32)


def dot_nn(left, right):
    return jnp.dot(left, right, preferred_element_type=F32)


def dot_exact(left, right):
    return jnp.dot(left, right, preferred_element_type=F32, precision=HIGHEST)


def thirds(v):
    high = v.astype(BF16)
    rest = v - high.astype(F32)
    middle = rest.astype(BF16)
    return high, middle, (rest - middle.astype(F32)).astype(BF16)


def places(shape):
    return lax.broadcasted_iota(jnp.int32, shape, 0), lax.broadcasted_iota(jnp.int32, shape, 1)


def one_hot(hit):
    return hit.astype(F32).astype(BF16)


def tiles(count, step=32):
    return [slice(at, min(at + step, count)) for at in range(0, count, step)]


def moved(rows, by):
    return slice(rows.start + by, rows.stop + by)


def conv_pre(ext_ref, taps_ref, same_ref, rows, width):
    total = taps_ref[width : width + 1] + taps_ref[width - 1 : width] * ext_ref[moved(rows, HALO)]
    for back in range(1, width):
        total = total + (
            taps_ref[width - 1 - back : width - back]
            * ext_ref[moved(rows, HALO - back)]
            * same_ref[moved(rows, HALO), back - 1 : back]
        )
    return total


def lane_masks():
    lane = lax.broadcasted_iota(jnp.int32, (1, 128), 1)
    first = (lane < 64).astype(F32)
    return first, 1.0 - first


def two_apart(pair, masks):
    return jnp.concatenate([pair * masks[0].astype(BF16), pair * masks[1].astype(BF16)], 0)


def decay_pair(cum_ref, cumt_ref, bias, rows, pair):
    parts = []
    for head in (2 * pair, 2 * pair + 1):
        spread = cum_ref[0, rows, head : head + 1] - cumt_ref[0, head : head + 1, rows] + bias
        parts.append(jnp.exp(spread))
    return parts


class Scan:
    def __init__(self, own, sizes, rows, cols, heads_own, taps):
        self.own, self.ext, self.taps = own, own + HALO, taps
        self.dps, self.hts = 2 * sizes[0], sizes[1] * sizes[2]
        self.rows, self.cols = rows, cols
        self.group = group_of(cols)
        self.wide = self.group * cols
        self.heads = self.group * heads_own
        self.groups = self.hts // self.group
        self.chunks = own // CHUNK
        self.width = self.dps * rows
        self.inner = self.hts * cols
        self.pairs = self.wide // 128

    def call(self, kernel, ins, outs, scratch=(), collective=None):
        arrays = [array for array, _ in ins]
        return pl.pallas_call(
            kernel,
            grid=(self.groups,),
            out_shape=[shape for shape, _ in outs],
            in_specs=[spec for _, spec in ins],
            out_specs=[spec for _, spec in outs],
            scratch_shapes=list(scratch),
            compiler_params=local_params() if collective is None else remote_params(collective),
            cost_estimate=busy(22),
        )(*arrays)

    def full(self, array):
        mode = None if isinstance(array, jax.ShapeDtypeStruct) else pl.Buffered(1)
        return (array, pl.BlockSpec(array.shape, lambda j: (0,) * array.ndim, pipeline_mode=mode))

    def pieces(self, array):
        block = (self.dps, self.group, self.rows, self.cols)
        return (array, pl.BlockSpec(block, lambda j: (0, j, 0, 0)))

    def lanes(self, array):
        lead = array.shape[:-1]
        return (array, pl.BlockSpec(lead + (self.wide,), lambda j: (0,) * len(lead) + (j,)))

    def states(self, array):
        lead = array.shape[:-2]
        block = lead + (self.wide, array.shape[-1])
        return (array, pl.BlockSpec(block, lambda j: (0,) * len(lead) + (j, 0)))

    def grouped(self, array):
        block = (1,) + array.shape[1:]
        return (array, pl.BlockSpec(block, lambda j: (j,) + (0,) * (array.ndim - 1)))

    def project(self, rows_ref, piece_ref, out_ref):
        for one in range(self.group):
            weights = piece_ref[:, one].reshape(self.width, self.cols)
            out_ref[:, one * self.cols : (one + 1) * self.cols] = dot_nn(rows_ref, weights)

    def project_back(self, value_ref, piece_ref, out_ref):
        @pl.when(pl.program_id(0) == 0)
        def _():
            out_ref[...] = jnp.zeros_like(out_ref)

        for one in range(self.group):
            weights = piece_ref[:, one].reshape(self.width, self.cols)
            out_ref[...] += dot_nt(value_ref[:, one * self.cols : (one + 1) * self.cols], weights)

    def chunk_rows(self, c):
        return slice(c * CHUNK, (c + 1) * CHUNK)

    def lane_sums(self, v):
        total = v[:, :128]
        for pair in range(1, self.pairs):
            total = total + v[:, pair * 128 : (pair + 1) * 128]
        return total

    def widen(self):
        count = self.heads * self.groups
        row, lane = places((3 * count, self.wide))
        row = row - jnp.where(row >= 2 * count, 2 * count, jnp.where(row >= count, count, 0))
        return one_hot(row == pl.program_id(0) * self.heads + lax.div(lane, 64))

    def heads_of(self):
        row, lane = places((self.wide, 128))
        return one_hot(lane == pl.program_id(0) * self.heads + lax.div(row, 64))

    def keep_columns(self, keep_ref, widen):
        return dot_tn(widen, keep_ref[...])

    def halves(self, v):
        high = v.astype(BF16)
        return high, (v - high.astype(F32)).astype(BF16)

    def head_sums(self, v, heads_of):
        high, low = self.halves(v)
        return dot_nn(high, heads_of) + dot_nn(low, heads_of)

    def gradient(self, left_ref, value_ref, out_ref):
        for at in range(self.dps):
            for one in range(self.group):
                value = value_ref[:, one * self.cols : (one + 1) * self.cols]
                out_ref[at, one] = dot_nn(left_ref[at], value).astype(BF16)

    def piece_shape(self):
        return jax.ShapeDtypeStruct((self.dps, self.hts, self.rows, self.cols), BF16)

    def s1(self, normed, w_x, conv_rows, same, dt3, tail3, cum_g, cumt_g, coupling, bias, bc, keep3):
        own, state = self.own, bc.shape[1] // 2

        def kernel(
            normed_ref, w_ref, conv_ref, same_ref, dt_ref, tail_ref, cum_ref, cumt_ref,
            coupling_ref, bias_ref, bc_ref, keep_ref, ext_ref, x_ref, within_ref, added_ref, local_ref, xd_ref, xt_ref,
            dtw_ref, tailw_ref,
        ):
            self.project(normed_ref[...], w_ref, ext_ref)
            widen = self.widen()
            keep = self.keep_columns(keep_ref, widen)
            dtw_ref[...] = dot_nn(dt_ref[...], widen)
            tailw_ref[...] = dot_nn(tail_ref[...], widen)
            for rows in tiles(own):
                x = silu_of(conv_pre(ext_ref, conv_ref, same_ref, rows, self.taps))
                x_ref[rows] = x
                xd = x * dtw_ref[rows]
                xd_ref[rows] = xd.astype(BF16)
                xt_ref[rows] = (xd * tailw_ref[rows]).astype(BF16)
            masks = lane_masks()
            held = None
            for c in range(self.chunks):
                rows = self.chunk_rows(c)
                for pair in range(self.pairs):
                    lanes = slice(pair * 128, (pair + 1) * 128)
                    first, second = decay_pair(cum_ref, cumt_ref, bias_ref[c], rows, pair)
                    mix = coupling_ref[c]
                    kernel16 = jnp.concatenate([(first * mix).astype(BF16), (second * mix).astype(BF16)], 1)
                    within_ref[rows, lanes] = dot_nn(kernel16, two_apart(xd_ref[rows, lanes], masks))
                added = dot_tn(xt_ref[rows], bc_ref[rows, :state])
                added_ref[c] = added
                held = added if held is None else added + keep[:, c : c + 1] * held
            local_ref[...] = held.astype(BF16)

        f = jax.ShapeDtypeStruct
        return self.call(
            kernel,
            [
                self.full(normed), self.pieces(w_x), self.lanes(conv_rows), self.full(same), self.full(dt3),
                self.full(tail3), self.grouped(cum_g), self.grouped(cumt_g),
                self.full(coupling), self.full(bias), self.full(bc), self.full(keep3),
            ],
            [
                self.lanes(f((self.ext, self.inner), F32)), self.lanes(f((own, self.inner), F32)),
                self.lanes(f((own, self.inner), F32)), self.states(f((self.chunks, self.inner, state), F32)),
                self.states(f((self.inner, state), BF16)),
            ],
            [pltpu.VMEM((own, self.wide), BF16)] * 2 + [pltpu.VMEM((own, self.wide), F32)] * 2,
        )

    def s2(self, normed_own, w_z, within, x, skip_rows, entry3, bc, entering, added, keep3):
        own, state = self.own, bc.shape[1] // 2

        def kernel(
            normed_ref, w_ref, within_ref, x_ref, skip_ref, entry_ref, bc_ref, entering_ref,
            added_ref, keep_ref, z_ref, y_ref, states_ref, squares_ref, entry_wide_ref, carried_ref,
        ):
            self.project(normed_ref[...], w_ref, z_ref)
            widen = self.widen()
            keep = self.keep_columns(keep_ref, widen)
            entry_wide_ref[...] = dot_nn(entry_ref[...], widen)
            held = entering_ref[...].astype(F32)
            for c in range(self.chunks):
                rows = self.chunk_rows(c)
                held16 = held.astype(BF16)
                states_ref[c] = held16
                carried_ref[rows] = dot_nt(bc_ref[rows, state:], held16)
                if c + 1 < self.chunks:
                    held = added_ref[c] + keep[:, c : c + 1] * held

            @pl.when(pl.program_id(0) == 0)
            def _():
                squares_ref[...] = jnp.zeros_like(squares_ref)

            for rows in tiles(own):
                y = within_ref[rows] + carried_ref[rows] * entry_wide_ref[rows] + skip_ref[...] * x_ref[rows]
                y_ref[rows] = y
                gated = y * silu_of(z_ref[rows])
                squares_ref[rows] += self.lane_sums(gated * gated)

        f = jax.ShapeDtypeStruct
        return self.call(
            kernel,
            [
                self.full(normed_own), self.pieces(w_z), self.lanes(within), self.lanes(x), self.lanes(skip_rows),
                self.full(entry3), self.full(bc), self.states(entering), self.states(added),
                self.full(keep3),
            ],
            [
                self.lanes(f((own, self.inner), F32)), self.lanes(f((own, self.inner), F32)),
                self.states(f((self.chunks, self.inner, state), BF16)), self.full(f((own, 128), F32)),
            ],
            [pltpu.VMEM((own, self.wide), F32)] * 2,
        )

    def inv_gate(self, squares_ref, rows):
        return lax.rsqrt(jnp.sum(squares_ref[rows], axis=1, keepdims=True) / self.inner + EPSILON)

    def s3(self, y, z, squares, gain_row, w_o, cotangent, residual, cot_left):
        own = self.own

        def kernel(
            y_ref, z_ref, squares_ref, gain_ref, w_ref, cot_ref, residual_ref, left_ref,
            grad_ref, cross_ref, gain_grad_ref, out_ref, pieces_ref, gated_ref, sum_ref, normal_ref,
        ):
            for rows in tiles(own):
                normal = y_ref[rows] * silu_of(z_ref[rows]) * self.inv_gate(squares_ref, rows)
                normal_ref[rows] = normal
                gated_ref[rows] = (normal * gain_ref[...]).astype(BF16)
            self.project_back(gated_ref, w_ref, sum_ref)
            self.gradient(left_ref, gated_ref, pieces_ref)
            self.project(cot_ref[...], w_ref, grad_ref)

            @pl.when(pl.program_id(0) == 0)
            def _():
                cross_ref[...] = jnp.zeros_like(cross_ref)

            gain_grad = None
            for rows in tiles(own):
                product = grad_ref[rows] * normal_ref[rows]
                summed = jnp.sum(product, axis=0, keepdims=True)
                gain_grad = summed if gain_grad is None else gain_grad + summed
                cross_ref[rows] += self.lane_sums(product * gain_ref[...])
            gain_grad_ref[...] = jnp.broadcast_to(gain_grad, gain_grad_ref.shape)

            @pl.when(pl.program_id(0) == self.groups - 1)
            def _():
                out_ref[...] = (residual_ref[...].astype(F32) + sum_ref[...]).astype(BF16)

        f = jax.ShapeDtypeStruct
        return self.call(
            kernel,
            [
                self.lanes(y), self.lanes(z), self.full(squares), self.lanes(gain_row), self.pieces(w_o),
                self.full(cotangent), self.full(residual), self.full(cot_left),
            ],
            [
                self.lanes(f((own, self.inner), F32)), self.full(f((own, 128), F32)),
                self.lanes(f((8, self.inner), F32)), self.full(f((own, self.width), BF16)),
                self.pieces(self.piece_shape()),
            ],
            [
                pltpu.VMEM((own, self.wide), BF16), pltpu.VMEM((own, self.width), F32),
                pltpu.VMEM((own, self.wide), F32),
            ],
        )

    def s4(self, y, z, squares, cross, gain_row, grad_gate, w_z, entry3, bc, keep3, left):
        own, state = self.own, bc.shape[1] // 2

        def kernel(
            y_ref, z_ref, squares_ref, cross_ref, gain_ref, grad_ref, w_ref, entry_ref, bc_ref,
            keep_ref, left_ref, dy_ref, back_ref, local_ref, through_ref, pieces_ref, low_ref, dye_ref,
            entry_wide_ref,
        ):
            widen = self.widen()
            keep = self.keep_columns(keep_ref, widen)
            entry_wide_ref[...] = dot_nn(entry_ref[...], widen)
            for rows in tiles(own):
                inv = self.inv_gate(squares_ref, rows)
                cross_mean = jnp.sum(cross_ref[rows], axis=1, keepdims=True) / self.inner
                z = z_ref[rows]
                gate = jax.nn.sigmoid(z)
                z_gate = z * gate
                y = y_ref[rows]
                grad_gated = inv * (grad_ref[rows] * gain_ref[...]) - (y * z_gate) * (inv * inv * cross_mean)
                dy = grad_gated * z_gate
                dy_ref[rows] = dy
                low_ref[rows] = (grad_gated * y * (gate * (1.0 + z * (1.0 - gate)))).astype(BF16)
                dye_ref[rows] = (dy * entry_wide_ref[rows]).astype(BF16)
            self.project_back(low_ref, w_ref, through_ref)
            self.gradient(left_ref, low_ref, pieces_ref)
            held = None
            for c in range(self.chunks - 1, -1, -1):
                rows = self.chunk_rows(c)
                added = dot_tn(dye_ref[rows], bc_ref[rows, state:])
                back_ref[c] = added
                held = added if held is None else added + keep[:, c : c + 1] * held
            local_ref[...] = held.astype(BF16)

        f = jax.ShapeDtypeStruct
        return self.call(
            kernel,
            [
                self.lanes(y), self.lanes(z), self.full(squares), self.full(cross), self.lanes(gain_row),
                self.lanes(grad_gate), self.pieces(w_z), self.full(entry3), self.full(bc),
                self.full(keep3), self.full(left),
            ],
            [
                self.lanes(f((own, self.inner), F32)),
                self.states(f((self.chunks, self.inner, state), F32)), self.states(f((self.inner, state), BF16)),
                self.full(f((own, self.width), F32)), self.pieces(self.piece_shape()),
            ],
            [pltpu.VMEM((own, self.wide), BF16)] * 2 + [pltpu.VMEM((own, self.wide), F32)],
        )

    def s5(
        self, dy, x_ext, within, conv_rows, skip_rows, same, dt3, tail3, entry3, cum_g, cumt_g, coupling,
        bias, bc, states, leaving, back_added, keep3, w_x, left, others, sizes,
    ):
        own, state = self.own, bc.shape[1] // 2
        taps = self.taps
        xs, hs, ts = sizes
        others = [other.reshape((self.dps, hs, ts) + other.shape[2:]) for other in others]
        kinds = len(others)
        moving = row_chunks(self.rows, 0, kinds, self.rows // CHUNK_ROWS)
        buffers = reducer_scratch(sizes, moving, others)
        anywhere = pl.BlockSpec(memory_space=pl.ANY)

        def kernel(
            dy_ref, ext_ref, within_ref, conv_ref, skip_ref, same_ref, dt_ref, tail_ref, entry_ref,
            cum_ref, cumt_ref, coupling_ref, bias_ref, bc_ref, states_ref, leaving_ref, back_ref, keep_ref,
            w_ref, left_ref, *rest,
        ):
            other_refs, rest = rest[:kinds], rest[kinds:]
            rows_ref, head_ref, dots_ref, dbc_ref, dmix_ref, through_ref, pieces_ref = rest[:7]
            sum_refs, rest = rest[7 : 7 + kinds], rest[7 + kinds :]
            low_ref, xd_ref, xt_ref, dy16_ref, dye_ref, halves_ref, shift_ref, dxd_ref = rest[:8]
            dtw_ref, tailw_ref, pre_ref, spread_ref, carried_ref = rest[8:13]
            bufs = rest[13:]
            x_at, core, head, tensor = coordinates()

            def put(kind, start, length, value):
                sum_refs[kind][start : start + length, :] = value

            begin, step_on, end, ticks = reducer(
                sizes, moving, other_refs, bufs[:-3], bufs[-3:], put, HOSTED_LAGS
            )

            def scatter_on(slot):
                for step in range(self.groups):
                    if slot < SLOTS and SLOTS * step + slot < ticks:

                        @pl.when(pl.program_id(0) == step)
                        def _(at=SLOTS * step + slot):
                            step_on(at)

            @pl.when(pl.program_id(0) == 0)
            def _():
                begin(True)
                enter_kernel(x_at, core, head, tensor, xs, hs, ts, True)
                begin(False)

            first_step = pl.program_id(0) == 0

            @pl.when(first_step)
            def _():
                dbc_ref[...] = jnp.zeros_like(dbc_ref)
                dmix_ref[...] = jnp.zeros_like(dmix_ref)
                head_ref[...] = jnp.zeros_like(head_ref)
                dots_ref[...] = jnp.zeros_like(dots_ref)

            widen, heads_of = self.widen(), self.heads_of()
            keep = self.keep_columns(keep_ref, widen)
            dtw_ref[...] = dot_nn(dt_ref[...], widen)
            tailw_ref[...] = dot_nn(tail_ref[...], widen)
            spread_ref[...] = dot_nn(entry_ref[...], widen)
            for rows in tiles(own):
                pre = conv_pre(ext_ref, conv_ref, same_ref, rows, taps)
                pre_ref[rows] = pre
                xd = silu_of(pre) * dtw_ref[rows]
                xd_ref[rows] = xd.astype(BF16)
                xt_ref[rows] = (xd * tailw_ref[rows]).astype(BF16)
                dy = dy_ref[rows]
                dy16_ref[rows] = dy.astype(BF16)
                dye_ref[rows] = (dy * spread_ref[rows]).astype(BF16)
            scatter_on(0)
            masks = lane_masks()
            held = leaving_ref[...].astype(F32)
            for c in range(self.chunks - 1, -1, -1):
                rows = self.chunk_rows(c)
                held16 = held.astype(BF16)
                into16 = states_ref[c]
                product = held * into16.astype(F32)
                high, low = self.halves(product)
                dots_ref[c] += dot_tn(high, heads_of) + dot_tn(low, heads_of)
                spread_ref[rows] = dot_nt(bc_ref[rows, :state], held16)
                carried_ref[rows] = dot_nt(bc_ref[rows, state:], into16)
                dmix = dmix_ref[c]
                for pair in range(self.pairs):
                    lanes = slice(pair * 128, (pair + 1) * 128)
                    first, second = decay_pair(cum_ref, cumt_ref, bias_ref[c], rows, pair)
                    mix = coupling_ref[c]
                    kernel16 = jnp.concatenate([(first * mix).astype(BF16), (second * mix).astype(BF16)], 1)
                    dy_pair = dy16_ref[rows, lanes]
                    both = dot_tn(kernel16, dy_pair)
                    dxd_ref[rows, lanes] = both[:CHUNK] * masks[0] + both[CHUNK:] * masks[1]
                    dkernel = dot_nt(dy_pair, two_apart(xd_ref[rows, lanes], masks))
                    dmix = dmix + dkernel[:, :CHUNK] * first + dkernel[:, CHUNK:] * second
                dmix_ref[c] = dmix
                dbc_ref[rows, :state] += dot_nn(xt_ref[rows], held16)
                dbc_ref[rows, state:] += dot_nn(dye_ref[rows], into16)
                if c > 0:
                    held = back_ref[c] + keep[:, c : c + 1] * held
            scatter_on(1)
            halves = (
                (dy16_ref, dye_ref), (xd_ref, xt_ref), (low_ref.at[:own], halves_ref),
            )
            shift_ref[:HALO] = jnp.zeros((HALO, self.wide), F32)
            shift_ref[HALO + own :] = jnp.zeros((HALO, self.wide), F32)
            sums = [None] * (taps + 2)

            def add_to(at, v):
                v = jnp.sum(v, axis=0, keepdims=True)
                sums[at] = v if sums[at] is None else sums[at] + v

            for rows in tiles(own):
                dxd_within = dxd_ref[rows]
                falls = (
                    dy16_ref[rows].astype(F32) * within_ref[rows]
                    + dye_ref[rows].astype(F32) * carried_ref[rows]
                    - xd_ref[rows].astype(F32) * dxd_within
                )
                dxd = dxd_within + tailw_ref[rows] * spread_ref[rows]
                pre, dy = pre_ref[rows], dy_ref[rows]
                gate = jax.nn.sigmoid(pre)
                x = pre * gate
                rises = xt_ref[rows].astype(F32) * spread_ref[rows]
                for part, (high_ref, low_part_ref) in zip((falls, rises, x * dxd), halves):
                    high_ref[rows], low_part_ref[rows] = self.halves(part)
                slope = gate * (1.0 + pre * (1.0 - gate))
                grad = (dxd * dtw_ref[rows] + skip_ref[...] * dy) * slope
                shift_ref[moved(rows, HALO)] = grad
                add_to(taps, grad)
                add_to(taps + 1, dy * x)
                add_to(taps - 1, grad * ext_ref[moved(rows, HALO)])
                for back in range(1, taps):
                    masked = grad * same_ref[moved(rows, HALO), back - 1 : back]
                    add_to(taps - 1 - back, masked * ext_ref[moved(rows, HALO - back)])
            for at in range(taps + 2):
                rows_ref[at : at + 1] = sums[at]
            for at, (high_ref, low_part_ref) in enumerate(halves):
                head_ref[at] += dot_nn(high_ref[...], heads_of) + dot_nn(low_part_ref[...], heads_of)
            for rows in tiles(own + HALO):
                total = conv_ref[taps - 1 : taps] * shift_ref[rows]
                for back in range(1, taps):
                    total = total + (
                        conv_ref[taps - 1 - back : taps - back]
                        * shift_ref[moved(rows, back)]
                        * same_ref[moved(rows, back), back - 1 : back]
                    )
                low_ref[rows] = total.astype(BF16)
            scatter_on(2)
            self.project_back(low_ref, w_ref, through_ref)
            self.gradient(left_ref, low_ref, pieces_ref)

            @pl.when(pl.program_id(0) == self.groups - 1)
            def _():
                for at in range(SLOTS * self.groups, ticks):
                    step_on(at)
                end()

        f = jax.ShapeDtypeStruct
        scratch16 = pltpu.VMEM((own, self.wide), BF16)
        return self.call(
            kernel,
            [
                self.lanes(dy), self.lanes(x_ext), self.lanes(within), self.lanes(conv_rows), self.lanes(skip_rows),
                self.full(same), self.full(dt3), self.full(tail3), self.full(entry3),
                self.grouped(cum_g), self.grouped(cumt_g), self.full(coupling), self.full(bias),
                self.full(bc), self.states(states), self.states(leaving), self.states(back_added),
                self.full(keep3), self.pieces(w_x), self.full(left),
            ]
            + [(other, anywhere) for other in others],
            [
                self.lanes(f((8, self.inner), F32)), self.full(f((3, own, 128), F32)),
                self.full(f((self.chunks, state, 128), F32)),
                self.full(f((own, 2 * state), F32)), self.full(f((self.chunks, CHUNK, CHUNK), F32)),
                self.full(f((self.ext, self.width), F32)), self.pieces(self.piece_shape()),
            ]
            + [self.full(f((self.rows, self.cols), F32))] * kinds,
            [
                pltpu.VMEM((self.ext, self.wide), BF16), scratch16, scratch16, scratch16, scratch16,
                pltpu.VMEM((own, self.wide), BF16), pltpu.VMEM((own + 2 * HALO, self.wide), F32),
            ]
            + [pltpu.VMEM((own, self.wide), F32)] * 6
            + buffers,
            4,
        )

    def alone(self, kernel, ins, outs, scratch, microseconds):
        whole = pl.BlockSpec(memory_space=pltpu.VMEM)
        return pl.pallas_call(
            kernel,
            out_shape=outs,
            in_specs=[whole] * len(ins),
            out_specs=[whole] * len(outs),
            scratch_shapes=scratch,
            compiler_params=local_params(),
            cost_estimate=busy(microseconds),
        )(*ins)

    def prepare(self, normed, cotangent, side, seg_col, seg_row, bc_rows, head_rows, bc_cols, heads_own):
        own, taps, chunks = self.own, self.taps, self.chunks
        heads = heads_own * self.hts
        state2 = bc_cols * self.hts
        state = state2 // 2
        wide = self.hts * side.shape[2]

        def kernel(
            normed_ref, cot_ref, side_ref, seg_ref, segr_ref, bcw_ref, headw_ref,
            ext_left_ref, own_left_ref, cot_left_ref, w_ref, bce_ref, bc_ref, same_ref, dt_ref, sig_ref, cum_ref, cumt_ref, dt3_ref, tail3_ref, entry3_ref,
            keep_ref, keep3_ref, send_ref, mix_ref, bias_ref, raw_ref,
        ):
            row, lane = places((heads, self.hts * 16))
            pick = one_hot(lane == lax.div(row, heads_own) * 16 + lax.rem(row, heads_own))
            w_ref[...] = jnp.zeros_like(w_ref)
            for at in range(self.dps):
                cols = slice(at * self.rows, (at + 1) * self.rows)
                ext_left_ref[at] = normed_ref[:, cols].T
                own_left_ref[at] = normed_ref[HALO:, cols].T
                cot_left_ref[at] = cot_ref[:, cols].T
            for at in range(self.dps):
                cols = slice(at * self.rows, (at + 1) * self.rows)
                for one in range(self.hts):
                    w_ref[one * bc_cols : (one + 1) * bc_cols, cols] = side_ref[at, one, :bc_cols]
                padded = jnp.concatenate(
                    [side_ref[at, one, bc_cols : bc_cols + 16] for one in range(self.hts)], 0
                )
                w_ref[state2 : state2 + heads, cols] = dot_nn(pick, padded).astype(BF16)
            bce_ref[...] = dot_nt(normed_ref[...], w_ref[:state2])
            raw_ref[...] = dot_nt(normed_ref[HALO:], w_ref[state2 : state2 + 128])
            mine = seg_ref[HALO:]
            same_ref[...] = jnp.zeros_like(same_ref)
            for back in range(1, taps):
                hit = seg_ref[HALO - back : HALO - back + own] == mine
                same_ref[HALO : HALO + own, back - 1 : back] = hit.astype(F32)
            bc_ref[...] = silu_of(conv_pre(bce_ref, bcw_ref, same_ref, slice(0, own), taps)).astype(BF16)
            shifted = raw_ref[:, :heads] + headw_ref[0:1]
            dt = jnp.maximum(shifted, 0.0) + jnp.log1p(jnp.exp(-jnp.abs(shifted)))
            dt_ref[...] = dt
            sig_ref[...] = jax.nn.sigmoid(shifted)
            rate = -jnp.exp(headw_ref[1:2])
            row, lane = places((CHUNK, CHUNK))
            lower = row >= lane
            triangle = lower.astype(F32)

            def put_thirds(ref, rows, v):
                for at, part in enumerate(thirds(v)):
                    ref[rows, at * heads : (at + 1) * heads] = part

            put_thirds(dt3_ref, slice(0, own), dt)
            keep_all = None
            for c in range(chunks):
                rows = self.chunk_rows(c)
                seg = mine[rows]
                before = seg_ref[HALO + c * CHUNK - 1 : HALO + c * CHUNK]
                end = seg_ref[HALO + (c + 1) * CHUNK - 1 : HALO + (c + 1) * CHUNK]
                cum = dot_exact(triangle, dt_ref[rows] * rate)
                last = cum[CHUNK - 1 : CHUNK]
                put_thirds(tail3_ref, rows, jnp.exp(last - cum) * (seg == end).astype(F32))
                put_thirds(entry3_ref, rows, jnp.exp(cum) * (seg == before).astype(F32))
                keep = jnp.exp(last) * (before == end).astype(F32)
                keep_ref[c : c + 1] = keep
                keep_all = keep if keep_all is None else keep_all * keep
                flipped = cum.T
                for j in range(self.groups):
                    cum_ref[j, rows] = cum[:, j * self.heads : (j + 1) * self.heads]
                    cumt_ref[j, :, rows] = flipped[j * self.heads : (j + 1) * self.heads]
                mix_ref[c] = dot_nt(bc_ref[rows, state:], bc_ref[rows, :state])
                bias_ref[c] = jnp.where((seg == segr_ref[0:1, rows]) & lower, 0.0, MASKED)
            keep_ref[chunks:] = jnp.zeros((8 - chunks, heads), F32)
            for at, part in enumerate(thirds(keep_ref[...].T)):
                keep3_ref[at * heads : (at + 1) * heads] = part
            first, second, third = thirds(keep_all)
            row, _ = places((16, heads))
            stacked = jnp.where(
                row == 0,
                first.astype(F32),
                jnp.where(row == 1, second.astype(F32), jnp.where(row == 2, third.astype(F32), 0.0)),
            ).astype(BF16)
            row, lane = places((heads, self.cols))
            for one in range(self.hts):
                spread = one_hot(row == one * heads_own + lax.div(lane, 64))
                send_ref[one] = dot_nn(stacked, spread).astype(BF16)

        f = jax.ShapeDtypeStruct
        return self.alone(
            kernel,
            [normed, cotangent, side, seg_col, seg_row, bc_rows, head_rows],
            [
                f((self.dps, self.rows, self.ext), BF16), f((self.dps, self.rows, own), BF16),
                f((self.dps, self.rows, own), BF16),
                f((wide, self.width), BF16), f((self.ext, state2), F32), f((own, state2), BF16), f((own + 2 * HALO, 8), F32),
                f((own, heads), F32), f((own, heads), F32), f((self.groups, own, self.heads), F32),
                f((self.groups, self.heads, own), F32), f((own, 3 * heads), BF16), f((own, 3 * heads), BF16),
                f((own, 3 * heads), BF16), f((8, heads), F32), f((3 * heads, 8), BF16),
                f((self.hts, 16, self.cols), BF16), f((chunks, CHUNK, CHUNK), F32), f((chunks, CHUNK, CHUNK), F32),
            ],
            [pltpu.VMEM((own, 128), F32)],
            10,
        )

    def finish(
        self, dbc, dmix, bc, bc_ext, bc_rows, same, head_sums, dots, keep, dt, sig, head_rows, w_side, through,
        own_part, normed,
    ):
        own, taps, chunks = self.own, self.taps, self.chunks
        heads = dt.shape[1]
        state2 = bc.shape[1]
        state = state2 // 2
        wide = w_side.shape[0]

        def kernel(
            dbc_ref, dmix_ref, bc_ref, bce_ref, bcw_ref, same_ref, sums_ref, dots_ref, keep_ref, dt_ref, sig_ref,
            headw_ref, w_ref, through_ref, own_ref, normed_ref,
            part_ref, halo_ref, taps_ref, heads_ref, pieces_ref, low_ref, shift_ref, full_ref,
        ):
            rate = -jnp.exp(headw_ref[1:2])
            row, lane = places((CHUNK, CHUNK))
            upper = (row <= lane).astype(F32)
            strict = (row > lane).astype(F32)
            low_ref[...] = jnp.zeros_like(low_ref)
            grad_shift = jnp.zeros((1, heads), F32)
            grad_log = jnp.zeros((1, heads), F32)
            for c in range(chunks):
                rows = self.chunk_rows(c)
                dmix16 = dmix_ref[c].astype(BF16)
                full_ref[rows, :state] = dbc_ref[rows, :state] + dot_tn(dmix16, bc_ref[rows, state:])
                full_ref[rows, state:] = dbc_ref[rows, state:] + dot_nn(dmix16, bc_ref[rows, :state])
                crossing = jnp.sum(dots_ref[c], axis=0, keepdims=True)[:, :heads]
                da = (
                    dot_exact(upper, sums_ref[0, rows, :heads])
                    + dot_exact(strict, sums_ref[1, rows, :heads])
                    + keep_ref[c : c + 1] * crossing
                )
                grad_log = grad_log + jnp.sum(dt_ref[rows] * da, axis=0, keepdims=True)
                ddt_raw = (sums_ref[2, rows, :heads] + rate * da) * sig_ref[rows]
                grad_shift = grad_shift + jnp.sum(ddt_raw, axis=0, keepdims=True)
                low_ref[HALO + c * CHUNK : HALO + (c + 1) * CHUNK, state2 : state2 + heads] = ddt_raw.astype(BF16)
            heads_ref[...] = jnp.zeros_like(heads_ref)
            heads_ref[0:1] = grad_shift
            heads_ref[1:2] = rate * grad_log
            pre = conv_pre(bce_ref, bcw_ref, same_ref, slice(0, own), taps)
            gate = jax.nn.sigmoid(pre)
            grad = full_ref[...] * (gate * (1.0 + pre * (1.0 - gate)))
            shift_ref[:HALO] = jnp.zeros((HALO, state2), F32)
            shift_ref[HALO + own :] = jnp.zeros((HALO, state2), F32)
            taps_ref[...] = jnp.zeros_like(taps_ref)
            taps_ref[taps : taps + 1] = jnp.sum(grad, axis=0, keepdims=True)
            total = None
            for back in range(taps):
                masked = grad if back == 0 else grad * same_ref[HALO : HALO + own, back - 1 : back]
                shift_ref[HALO : HALO + own] = masked
                piece = bcw_ref[taps - 1 - back : taps - back] * shift_ref[back : back + own + HALO]
                total = piece if total is None else total + piece
                taps_ref[taps - 1 - back : taps - back] = jnp.sum(
                    masked * bce_ref[HALO - back : HALO - back + own], axis=0, keepdims=True
                )
            low_ref[:, :state2] = total.astype(BF16)
            part = through_ref[...] + dot_nn(low_ref[...], w_ref[...])
            part_ref[...] = part[HALO:] + own_ref[...]
            halo_ref[...] = part[:HALO]
            for at in range(self.dps):
                cols = slice(at * self.rows, (at + 1) * self.rows)
                pieces_ref[at] = dot_tn(low_ref[...], normed_ref[:, cols]).astype(BF16)

        f = jax.ShapeDtypeStruct
        return self.alone(
            kernel,
            [
                dbc, dmix, bc, bc_ext, bc_rows, same, head_sums, dots, keep, dt, sig, head_rows, w_side, through,
                own_part, normed,
            ],
            [
                f((own, self.width), F32), f((HALO, self.width), F32), f((8, state2), F32), f((8, heads), F32),
                f((self.dps, wide, self.rows), BF16),
            ],
            [
                pltpu.VMEM((self.ext, wide), BF16), pltpu.VMEM((own + 2 * HALO, state2), F32),
                pltpu.VMEM((own, state2), F32),
            ],
            12,
        )


def from_earlier(values, distance, size):
    return lax.ppermute(values, SEQ, [(i, i + distance) for i in range(size - distance)])


def from_later(values, distance, size):
    return lax.ppermute(values, SEQ, [(i + distance, i) for i in range(size - distance)])


def body(
    residual,
    segment_ids,
    norm_in_gain,
    w_zx,
    w_bc,
    w_dt,
    conv_x_weight,
    conv_x_bias,
    conv_bc_weight,
    conv_bc_bias,
    dt_bias,
    a_log,
    d_skip,
    norm_gain,
    w_out,
    cotangent,
):
    own, width = residual.shape
    dp_size = lax.axis_size("dp")
    size = lax.axis_size(SEQ)
    place = lax.axis_index(SEQ)
    dp_rows, _, cols = w_zx.shape
    heads_own = w_dt.shape[1]
    inner = cols * size
    heads = heads_own * size
    state2 = w_bc.shape[1]
    bc_cols = state2 // size
    head_width = inner // heads

    sizes = (dp_size // 2, lax.axis_size("head"), lax.axis_size("tensor"))
    taps = conv_x_weight.shape[0]
    bc_own = lax.dynamic_slice_in_dim(w_bc, place * bc_cols, bc_cols, 1)
    side_part = jnp.concatenate([bc_own, w_dt], 1).T
    side_part = jnp.pad(side_part, ((0, bc_cols + 16 - side_part.shape[0]), (0, 0)))
    small_rows = [conv_x_weight, conv_x_bias[None], norm_gain[None]]
    head_rows = jnp.stack([dt_bias, a_log, d_skip])
    small = jnp.concatenate(small_rows + [jnp.pad(head_rows, ((0, 0), (0, cols - heads_own)))], 0)
    small = jnp.pad(small, ((0, 16 - small.shape[0]), (0, 0)))

    def gathered(part):
        full = lax.all_gather(part, ALL, axis=0, tiled=False)
        return full.reshape(dp_size, size, dp_rows, cols)

    rows_ext = jnp.concatenate([from_earlier(residual[-HALO:], 1, size), residual], 0).astype(F32)
    inv_ext = lax.rsqrt(jnp.mean(rows_ext * rows_ext, axis=1, keepdims=True) + EPSILON)
    normed = (rows_ext * inv_ext * norm_in_gain).astype(BF16)
    normed_own = normed[HALO:]
    rows_in, inv_rms = rows_ext[HALO:], inv_ext[HALO:]

    seg_all = jnp.pad(segment_ids[0], (HALO, 0), constant_values=-1).astype(F32)
    seg_ext = lax.dynamic_slice_in_dim(seg_all, place * own, own + HALO)
    seg_row = jnp.broadcast_to(seg_ext[None, HALO:], (8, own))
    bc_rows = jnp.concatenate([conv_bc_weight, conv_bc_bias[None]], 0)
    bc_rows = jnp.pad(bc_rows, ((0, 8 - bc_rows.shape[0]), (0, 0)))

    w_z = gathered(w_zx[:, 0])
    side_full, w_x, small_full = gather_weights([side_part, w_zx[:, 1]], small, sizes)
    w_out_later, small_full = lax.optimization_barrier((w_out, small_full))
    w_o = gathered(w_out_later)
    w_x = w_x.reshape(dp_size, size, dp_rows, cols)
    side_full = side_full.reshape(dp_size, size, bc_cols + 16, dp_rows)
    small_full = jnp.moveaxis(small_full.reshape(size, 16, cols), 0, 1)
    per_channel = small_full.reshape(16, inner)
    per_head = small_full[taps + 2 : taps + 5, :, :heads_own].reshape(3, heads)
    conv_rows = per_channel[:8]
    gain_row = per_channel[taps + 1 : taps + 2]
    head_rows = jnp.pad(per_head[:2], ((0, 6), (0, 0)))
    skip_rows = jnp.repeat(per_head[2], head_width)[None]

    scan = Scan(own, sizes, dp_rows, cols, heads_own, taps)
    (
        ext_left, own_left, cot_left, w_side, bc_ext, bc, same, dt, sig, cum_g, cumt_g, dt3, tail3, entry3, keep, keep3, keep_send, coupling, bias,
    ) = scan.prepare(normed, cotangent, side_full, seg_ext[:, None], seg_row, bc_rows, head_rows, bc_cols, heads_own)
    x_ext, x, within, added, local = scan.s1(
        normed, w_x, conv_rows, same, dt3, tail3, cum_g, cumt_g, coupling, bias, bc, keep3
    )
    (entering,) = exchange_states(local, keep_send, sizes, True)
    z, y, states, squares = scan.s2(
        normed_own, w_z, within, x, skip_rows, entry3, bc, entering, added, keep3
    )
    grad_gate, cross, gain_rows, block_out, out_pieces = scan.s3(
        y, z, squares, gain_row, w_o, cotangent, residual, cot_left
    )
    dy, back_added, back_local, own_part, z_pieces = scan.s4(
        y, z, squares, cross, gain_row, grad_gate, w_z, entry3, bc, keep3, own_left
    )

    grid = (dp_size,) + sizes[1:]
    leaving, grad_wo = exchange_states(
        back_local, keep_send, sizes, False, (out_pieces.reshape(grid + (dp_rows, cols)),)
    )
    conv_sums, head_sums, dots, dbc, dmix, through, x_pieces, grad_wz = scan.s5(
        dy, x_ext, within, conv_rows, skip_rows, same, dt3, tail3, entry3, cum_g, cumt_g, coupling, bias, bc,
        states, leaving, back_added, keep3, w_x, ext_left,
        (z_pieces,), sizes
    )
    part, halo, bc_sums, scan_sums, side_pieces = scan.finish(
        dbc, dmix, bc, bc_ext, bc_rows, same, head_sums, dots, keep, dt, sig, head_rows, w_side, through, own_part,
        normed
    )

    grad_normed = part.at[own - HALO :].add(from_later(halo, 1, size))
    scaled_in = grad_normed * norm_in_gain
    input_grad = (
        cotangent.astype(F32)
        + inv_rms * scaled_in
        - rows_in * (inv_rms * inv_rms * inv_rms) * jnp.mean(scaled_in * rows_in, axis=1, keepdims=True)
    )
    grad_in_gain = jnp.sum(grad_normed * rows_in * inv_rms, axis=0)

    grad_skip = jnp.sum(conv_sums[taps + 1].reshape(heads, head_width), axis=1)
    head_sum = jnp.concatenate([scan_sums[0], scan_sums[1], grad_skip])
    row = jnp.concatenate([grad_in_gain, bc_sums[: taps + 1].reshape(-1)])
    small_sum = jnp.concatenate(
        [
            conv_sums[: taps + 1],
            gain_rows[:1],
            jnp.pad(row, (0, inner - row.shape[0]))[None],
            jnp.pad(head_sum, (0, inner - head_sum.shape[0]))[None],
        ],
        0,
    )
    grad_side, grad_wx, small_sum = scatter_gradients(
        [side_pieces.reshape(grid + (-1, dp_rows)), x_pieces.reshape(grid + (dp_rows, cols))], small_sum, sizes
    )
    grad_wzx = jnp.stack([grad_wz, grad_wx], 1)
    grad_side = grad_side.reshape(-1, dp_rows).astype(F32)
    grad_wbc = grad_side[:state2].T
    grad_wdt = lax.dynamic_slice_in_dim(grad_side, state2 + place * heads_own, heads_own, 0).T
    channel_own = lax.dynamic_slice_in_dim(small_sum[: taps + 2], place * cols, cols, 1)
    row = small_sum[taps + 2]
    gain_sum = row[:width]
    taps_sum = row[width : width + taps * state2].reshape(taps, state2)
    bias_sum = row[width + taps * state2 : width + (taps + 1) * state2]
    head_sum = small_sum[taps + 3, : 3 * heads].reshape(3, heads)
    head_own = lax.dynamic_slice_in_dim(head_sum, place * heads_own, heads_own, 1)
    return (
        block_out,
        input_grad,
        gain_sum,
        grad_wzx,
        grad_wbc,
        grad_wdt,
        channel_own[:taps],
        channel_own[taps],
        taps_sum,
        bias_sum,
        head_own[0],
        head_own[1],
        head_own[2],
        channel_own[taps + 1],
        grad_wo,
    )


def solution(mesh):
    rows = P(ALL, None)
    in_specs = (
        rows,
        P("dp", None),
        P(),
        P("dp", None, SEQ),
        P("dp", None),
        P("dp", SEQ),
        P(None, SEQ),
        P(SEQ),
        P(),
        P(),
        P(SEQ),
        P(SEQ),
        P(SEQ),
        P(SEQ),
        P("dp", SEQ),
        rows,
    )
    out_specs = (
        rows,
        rows,
        P(),
        P("dp", None, SEQ),
        P("dp", None),
        P("dp", SEQ),
        P(None, SEQ),
        P(SEQ),
        P(),
        P(),
        P(SEQ),
        P(SEQ),
        P(SEQ),
        P(SEQ),
        P("dp", SEQ),
    )
    return jax.shard_map(
        body, mesh=mesh, in_specs=in_specs, out_specs=out_specs, check_vma=False
    )
```
